128 devices in a mesh: dp: 32 (over z, x, core), seq: 4 (over y).
Axes of the slice: x: 4, y: 4, z: 4, core: 2. Of those that a mesh axis runs over, the one named last changes fastest.
Arguments:
- tokens: bfloat16 [32, 576, 768], P('dp', 'seq'), may hold values from -6 to 6
- cotangent: bfloat16 [32, 576, 768], P('dp', 'seq'), may hold values from -6 to 6
- ln_gain: float32 [4, 768], replicated, may hold values from 0.5 to 1.5
- ln_shift: float32 [4, 768], replicated, may hold values from -1.2 to 1.2
- qkv_weight: bfloat16 [2, 768, 2304], P(None, 'dp'), may hold values from -0.21875 to 0.21875
- qv_bias: float32 [2, 1536], replicated, may hold values from -1.2 to 1.2
- out_weight: bfloat16 [2, 768, 768], P(None, 'dp'), may hold values from -0.875 to 0.875
- out_bias: float32 [2, 768], replicated, may hold values from -1.2 to 1.2
- up_weight: bfloat16 [768, 3072], P('dp'), may hold values from -0.21875 to 0.21875
- up_bias: float32 [3072], replicated, may hold values from -1.2 to 1.2
- down_weight: bfloat16 [3072, 768], P('dp'), may hold values from -0.21875 to 0.21875
- down_bias: float32 [768], replicated, may hold values from -1.2 to 1.2
- router: bfloat16 [768, 32], replicated, may hold values from -0.15625 to 0.15625
- expert_up: bfloat16 [32, 768, 3072], P('dp', None, 'seq'), may hold values from -0.21875 to 0.21875
- expert_up_bias: bfloat16 [32, 3072], P('dp', 'seq'), may hold values from -1.1953125 to 1.1953125
- expert_down: bfloat16 [32, 3072, 768], P('dp', 'seq'), may hold values from -0.21875 to 0.21875
- expert_down_bias: float32 [32, 768], P('dp'), may hold values from -1.2 to 1.2
- expert_ids: int32 [32, 576, 2], P('dp', 'seq'), may hold values from 0 to 31, all different within a row
- priority: int32 [32, 576, 2], P('dp', 'seq'), may hold values from 0 to 65535
Outputs:
- result: float32 [32, 576, 768], P('dp', 'seq')
- d_tokens: float32 [32, 576, 768], P('dp', 'seq')
- g_ln_gain: float32 [4, 768], replicated
- g_ln_shift: float32 [4, 768], replicated
- g_qkv_weight: float32 [2, 768, 2304], replicated
- g_qv_bias: float32 [2, 1536], replicated
- g_out_weight: float32 [2, 768, 768], replicated
- g_out_bias: float32 [2, 768], replicated
- g_up_weight: float32 [768, 3072], replicated
- g_up_bias: float32 [3072], replicated
- g_down_weight: float32 [3072, 768], replicated
- g_down_bias: float32 [768], replicated
- g_router: float32 [768, 32], replicated
- g_expert_up: float32 [32, 768, 3072], P('dp', None, 'seq')
- g_expert_up_bias: float32 [32, 3072], P('dp', 'seq')
- g_expert_down: float32 [32, 3072, 768], P('dp', 'seq')
- g_expert_down_bias: float32 [32, 768], P('dp', 'seq')
The draws below stay inside these ranges and needn't reach their ends.
Inputs may be any that keep to these rules, and one draw needn't show every extreme that they name: `expert_ids`: each patch names two different experts, and every expert is named by some patch.
All inputs are finite; a program needn't handle non-finite values.
Results may differ from the reference program's by a relative error of at most 0.018.
Values may be sent and summed in bfloat16 or wider, within the bound.
A program may use at most 256 MiB of HBM per device.

```python
from functools import partial
import jax
import jax.numpy as jnp
from jax import lax

D = 768
HEADS = 12
HEAD_DIM = 64
FF = 3072
PATCHES = 576
IMG_DEV = 1
EXPERTS = 32
IMAGES = 32
CAP = 4
N_DP = 32
N_SEQ = 4


def touch_ends(values, key, smallest, largest):
    longest = values.shape.index(max(values.shape))
    spots = []
    for shift in (0, 1):
        where = [jax.random.randint(jax.random.fold_in(key, axis), (), 0, length) for axis, length in enumerate(values.shape)]
        where[longest] = (where[longest] + shift) % values.shape[longest]
        spots.append(tuple(where))
    return values.at[spots[0]].set(smallest).at[spots[1]].set(largest)


def shard_levels(rng, extent, cuts, smallest, largest):
    def one(position, blocks):
        heights = jax.random.uniform(jax.random.fold_in(jax.random.fold_in(rng, 6), position), (blocks,), jnp.float32, smallest / len(cuts), largest / len(cuts))
        return jnp.repeat(jnp.exp(heights), extent[position] // blocks).reshape((-1,) + (1,) * (len(extent) - position - 1))

    factor_of = one(*cuts[0])
    for cut in cuts[1:]:
        factor_of = factor_of * one(*cut)
    return factor_of


def choose_distinct(stream_key, rows, amount, top, lift):
    ranking = jax.random.permutation(jax.random.fold_in(stream_key, 1), amount)
    favour = ranking
    for power in range(3):
        favour = favour * favour // amount
    favour = favour * lift // amount
    lots = jax.random.randint(jax.random.fold_in(stream_key, 2), (rows, amount), 0, 4096) + favour
    sure = jax.random.permutation(jax.random.fold_in(stream_key, 3), rows)[jnp.arange(amount) % rows]
    lots = jnp.where(jnp.arange(rows)[:, None] == sure[None, :], 1 << 14, lots)
    merit = lots * amount + jnp.arange(amount)
    return lax.top_k(merit.astype(jnp.int32), top)[1].astype(jnp.int32)


def bell_draw(stream_key, shape, width, bound, shards=(), kind=jnp.bfloat16):
    values = width * jax.random.normal(stream_key, shape, jnp.float32)
    if shards:
        values = values * shard_levels(stream_key, shape, shards, -0.22, 0.18)
    return jnp.clip(values, -bound, bound).astype(kind)


def setup_inputs(seed: int = 0) -> dict:
    streams_of = jax.random.split(jax.random.key(seed), 20)
    tokens = bell_draw(streams_of[0], (IMAGES, PATCHES, D), 1.0, 6.0, ((0, 32), (1, 4)))
    cotangent = bell_draw(streams_of[1], (IMAGES, PATCHES, D), 1.0, 6.0, ((0, 32), (1, 4)))
    ln_gain = jnp.clip(1.0 + 0.1 * jax.random.normal(streams_of[2], (4, D), jnp.float32), 0.5, 1.5)
    ln_shift = bell_draw(streams_of[3], (4, D), 0.2, 1.2, (), jnp.float32)
    qkv_weight = bell_draw(streams_of[4], (2, D, 3 * D), D ** -0.5, 0.21875, ((1, 32),))
    qv_bias = bell_draw(streams_of[5], (2, 2 * D), 0.2, 1.2, (), jnp.float32)
    out_weight = bell_draw(streams_of[6], (2, D, D), (D // 16) ** -0.5, 0.875, ((1, 32),))
    out_bias = bell_draw(streams_of[7], (2, D), 0.2, 1.2, (), jnp.float32)
    up_weight = bell_draw(streams_of[8], (D, FF), D ** -0.5, 0.21875, ((0, 32),))
    up_bias = bell_draw(streams_of[9], (FF,), 0.2, 1.2, (), jnp.float32)
    down_weight = bell_draw(streams_of[10], (FF, D), (FF // 4) ** -0.5, 0.21875, ((0, 32),))
    down_bias = bell_draw(streams_of[11], (D,), 0.2, 1.2, (), jnp.float32)
    router = bell_draw(streams_of[12], (D, EXPERTS), (2 * D) ** -0.5, 0.15625)
    expert_up = bell_draw(streams_of[13], (EXPERTS, D, FF), D ** -0.5, 0.21875, ((0, 32), (2, 4)))
    expert_up_bias = bell_draw(streams_of[14], (EXPERTS, FF), 0.2, 1.1953125, ((0, 32), (1, 4)))
    expert_down = bell_draw(streams_of[15], (EXPERTS, FF, D), (FF // 4) ** -0.5, 0.21875, ((0, 32), (1, 4)))
    expert_down_bias = bell_draw(streams_of[16], (EXPERTS, D), 0.2, 1.2, ((0, 32),), jnp.float32)
    expert_ids = choose_distinct(streams_of[17], IMAGES * PATCHES, EXPERTS, 2, 512).reshape((IMAGES, PATCHES, 2))
    priority = touch_ends(jax.random.randint(streams_of[18], (IMAGES, PATCHES, 2), 0, 65536), jax.random.fold_in(streams_of[18], 1), 0, 65535).astype(jnp.int32)
    return {"tokens": tokens, "cotangent": cotangent, "ln_gain": ln_gain, "ln_shift": ln_shift, "qkv_weight": qkv_weight, "qv_bias": qv_bias, "out_weight": out_weight, "out_bias": out_bias, "up_weight": up_weight, "up_bias": up_bias, "down_weight": down_weight, "down_bias": down_bias, "router": router, "expert_up": expert_up, "expert_up_bias": expert_up_bias, "expert_down": expert_down, "expert_down_bias": expert_down_bias, "expert_ids": expert_ids, "priority": priority}


HIGH_PRECISION = lax.Precision.HIGHEST
EPS = 1e-06

@jax.custom_vjp
def low(v):
    return lax.optimization_barrier(v.astype(jnp.bfloat16)).astype(jnp.float32)

@jax.custom_vjp
def reduced_backward(v):
    return v

def low_keep(v):
    return (low(v), None)

def low_pass(kept, grad):
    return (grad,)

def back_keep(v):
    return (v, None)

def back_low(kept, grad):
    return (low(grad),)
low.defvjp(low_keep, low_pass)
reduced_backward.defvjp(back_keep, back_low)

def layer_norm(values_in, gain_row, shift_row):
    row_mean = lax.optimization_barrier(jnp.mean(values_in, axis=-1, keepdims=True))
    centred = values_in - row_mean
    spread = lax.optimization_barrier(jnp.mean(centred * centred, axis=-1, keepdims=True))
    return centred * lax.rsqrt(spread + EPS) * gain_row + shift_row

def soft_weights(attention_scores):
    row_top = lax.optimization_barrier(jnp.max(attention_scores, axis=-1, keepdims=True))
    exp_scores = jnp.exp(attention_scores - row_top)
    return exp_scores / lax.optimization_barrier(jnp.sum(exp_scores, axis=-1, keepdims=True))

def gelu_tanh(values_in):
    return jax.nn.gelu(values_in, approximate=True)

def route(choices, priority, experts, capacity):
    pair_ids = choices.reshape(-1)
    pair_count = pair_ids.shape[0]
    pair_order = jnp.arange(pair_count, dtype=jnp.int32)
    pair_keys = priority.reshape(-1) * pair_count + pair_order
    same_expert = pair_ids[:, None] == pair_ids[None, :]
    earlier = pair_keys[None, :] < pair_keys[:, None]
    pair_rank = lax.optimization_barrier(jnp.sum((same_expert & earlier).astype(jnp.int32), axis=1))
    kept_mask = pair_rank < capacity
    slot_of = jnp.where(kept_mask, pair_ids * capacity + pair_rank, experts * capacity)
    slot_table = slot_of[None, :] == jnp.arange(experts * capacity, dtype=jnp.int32)[:, None]
    filled = lax.optimization_barrier(jnp.sum(slot_table.astype(jnp.int32), axis=1))
    source = lax.optimization_barrier(jnp.sum(jnp.where(slot_table, pair_order[None, :], 0), axis=1)) // 2
    return (kept_mask, slot_of, filled, source)

def attention(normed, qkv_w, qkv_b, out_w, out_b):
    model_width = normed.shape[-1]
    scores_scale_factor = HEAD_DIM ** (-0.5)

    def one_image(patch_rows):
        total_row_count = patch_rows.shape[0]
        low_in = low(patch_rows)
        projected = low(reduced_backward(jnp.dot(low_in, qkv_w, precision=HIGH_PRECISION) + qkv_b))
        query_rows = projected[:, :model_width].reshape(total_row_count, HEADS, HEAD_DIM)
        gathered_keys = projected[:, model_width:2 * model_width].reshape(total_row_count, HEADS, HEAD_DIM)
        gathered_values = projected[:, 2 * model_width:].reshape(total_row_count, HEADS, HEAD_DIM)
        attention_scores = reduced_backward(jnp.einsum('fuz,puz->ufp', query_rows, gathered_keys, precision=HIGH_PRECISION) * scores_scale_factor)
        softmax_reduced = low(soft_weights(attention_scores))
        attention_output = jnp.einsum('xsp,pxf->sxf', softmax_reduced, gathered_values, precision=HIGH_PRECISION).reshape(total_row_count, model_width)
        attention_output = low(reduced_backward(attention_output))
        return reduced_backward(jnp.dot(attention_output, out_w, precision=HIGH_PRECISION) + out_b)
    return lax.map(jax.checkpoint(one_image), normed)

def feed_forward(normed, up_w, up_b, down_w, down_b):

    def one_image(patch_rows):
        low_in = low(patch_rows)
        hidden_pre = reduced_backward(jnp.dot(low_in, up_w, precision=HIGH_PRECISION) + up_b)
        hidden_act = low(gelu_tanh(hidden_pre))
        return reduced_backward(jnp.dot(hidden_act, down_w, precision=HIGH_PRECISION) + down_b)
    return lax.map(jax.checkpoint(one_image), normed)

def mixture(normed, router_w, e_up, e_up_b, e_down, e_down_b, pick_table, kept_f, slot_of, filled_f, source):
    groups = N_DP * N_SEQ
    low_in = low(normed)
    grouped = low_in.reshape(N_DP, IMG_DEV, N_SEQ, PATCHES // N_SEQ, D).transpose(0, 2, 1, 3, 4).reshape(groups, -1, D)
    logits = jnp.einsum('gtd,de->gte', grouped, router_w, precision=HIGH_PRECISION)
    chosen = lax.optimization_barrier(jnp.sum(logits[:, :, None, :] * pick_table, axis=-1))
    weights = soft_weights(chosen) * kept_f
    dispatched = jnp.take_along_axis(grouped, source[:, :, None], axis=1) * filled_f[:, :, None]
    dispatched = reduced_backward(dispatched)
    per_expert = dispatched.reshape(groups, EXPERTS, CAP, D).transpose(1, 0, 2, 3)

    def one_expert(packed):
        slot_rows, w_up, b_up, w_down, b_down = packed
        hidden_pre = reduced_backward(jnp.einsum('gcd,df->gcf', slot_rows, w_up, precision=HIGH_PRECISION) + b_up)
        hidden_act = low(gelu_tanh(hidden_pre))
        return low(reduced_backward(jnp.einsum('gcf,fd->gcd', hidden_act, w_down, precision=HIGH_PRECISION) + b_down))
    outputs = lax.map(jax.checkpoint(one_expert), (per_expert, e_up, e_up_b, e_down, e_down_b))
    flat_out = outputs.transpose(1, 0, 2, 3).reshape(groups, EXPERTS * CAP, D)
    slot_index = jnp.minimum(slot_of, EXPERTS * CAP - 1)
    taken_rows = jnp.take_along_axis(flat_out, slot_index[:, :, None], axis=1).reshape(groups, -1, 2, D)
    combined = lax.optimization_barrier(jnp.sum(weights[..., None] * taken_rows, axis=2))
    combined = combined.reshape(N_DP, N_SEQ, IMG_DEV, PATCHES // N_SEQ, D).transpose(0, 2, 1, 3, 4)
    return combined.reshape(IMAGES, PATCHES, D)

def full_bias(bias_row):
    return jnp.concatenate([bias_row[:D], jnp.zeros((D,), bias_row.dtype), bias_row[D:]])

def reference(tokens, cotangent, ln_gain, ln_shift, qkv_weight, qv_bias, out_weight, out_bias, up_weight, up_bias, down_weight, down_bias, router, expert_up, expert_up_bias, expert_down, expert_down_bias, expert_ids, priority):
    groups = N_DP * N_SEQ
    group_ids = expert_ids.reshape(N_DP, IMG_DEV, N_SEQ, PATCHES // N_SEQ, 2).transpose(0, 2, 1, 3, 4).reshape(groups, -1)
    group_prio = priority.reshape(N_DP, IMG_DEV, N_SEQ, PATCHES // N_SEQ, 2).transpose(0, 2, 1, 3, 4).reshape(groups, -1)
    kept_mask, slot_of, filled, source = jax.vmap(partial(route, experts=EXPERTS, capacity=CAP))(group_ids, group_prio)
    kept_f = kept_mask.astype(jnp.float32).reshape(groups, -1, 2)
    filled_f = filled.astype(jnp.float32)
    pick_table = (group_ids.reshape(groups, -1, 2)[..., None] == jnp.arange(EXPERTS, dtype=jnp.int32)).astype(jnp.float32)
    floats = tuple((array.astype(jnp.float32) for array in (tokens, ln_gain, ln_shift, qkv_weight, qv_bias, out_weight, out_bias, up_weight, up_bias, down_weight, down_bias, router, expert_up, expert_up_bias, expert_down, expert_down_bias)))

    def forward(stream, gains, shifts, qkv_w, qv_b, out_w, out_b, up_w, up_b, down_w, down_b, router_w, e_up, e_up_b, e_down, e_down_b):
        normed = layer_norm(stream, gains[0], shifts[0])
        stream = stream + attention(normed, qkv_w[0], full_bias(qv_b[0]), out_w[0], out_b[0])
        normed = layer_norm(stream, gains[1], shifts[1])
        stream = stream + feed_forward(normed, up_w, up_b, down_w, down_b)
        normed = layer_norm(stream, gains[2], shifts[2])
        stream = stream + attention(normed, qkv_w[1], full_bias(qv_b[1]), out_w[1], out_b[1])
        normed = layer_norm(stream, gains[3], shifts[3])
        return stream + mixture(normed, router_w, e_up, e_up_b, e_down, e_down_b, pick_table, kept_f, slot_of, filled_f, source)
    result, pull_back = jax.vjp(forward, *floats)
    grads_all = pull_back(cotangent.astype(jnp.float32))
    return (result, grads_all[0], grads_all[1], grads_all[2], grads_all[3], grads_all[4], grads_all[5], grads_all[6], grads_all[7], grads_all[8], grads_all[9], grads_all[10], grads_all[11], grads_all[12], grads_all[13], grads_all[14], grads_all[15])
```

```python
import functools
import types

import jax
import jax.numpy as jnp
from jax import lax
from jax.experimental import pallas as pl
from jax.experimental.pallas import tpu as pltpu
from jax.sharding import PartitionSpec as P

MESH = pl.DeviceIdType.MESH
F32, BF16 = jnp.float32, jnp.bfloat16

D = 768
HEADS_DEV = 3
HW = 192
ROWS = 144
NY = 4
NDP = 32
EXPERTS = 32
CAP = 4
EPS = 1e-06
LO, HI = 80, 64
HALF = D // 2

NN = (((1,), (0,)), ((), ()))
RING4 = (1, 2, 3)
NT = (((1,), (1,)), ((), ()))
TN = (((0,), (0,)), ((), ()))


def mm(a, b, dims=NN):
    return lax.dot_general(a, b, dims, preferred_element_type=F32)


def ln_stats(x):
    mean = jnp.mean(x, axis=-1, keepdims=True)
    cen = x - mean
    rstd = lax.rsqrt(jnp.mean(cen * cen, axis=-1, keepdims=True) + EPS)
    return cen * rstd, rstd


def ln_forward(x, gain, shift):
    nhat, _ = ln_stats(x)
    return nhat * gain + shift


def ln_backward(x, gain, grad):
    nhat, rstd = ln_stats(x)
    d_gain = jnp.sum(grad * nhat, axis=0, keepdims=True)
    d_shift = jnp.sum(grad, axis=0, keepdims=True)
    gg = grad * gain
    dx = rstd * (
        gg
        - jnp.mean(gg, axis=-1, keepdims=True)
        - nhat * jnp.mean(gg * nhat, axis=-1, keepdims=True)
    )
    return dx, d_gain, d_shift


GC = 0.7978845608028654
GA = 0.044715


def gelu_both(u):
    sq = u * u
    t = jnp.tanh(GC * u * (1.0 + GA * sq))
    half = 0.5 * (1.0 + t)
    slope = half + 0.5 * u * (1.0 - t * t) * (GC * (1.0 + 3.0 * GA * sq))
    return u * half, slope


class Ring:
    def __init__(self):
        self.y = lax.axis_index("seq")
        self.right = lax.rem(self.y + 1, NY)
        self.left = lax.rem(self.y + 3, NY)
        self.opp = lax.rem(self.y + 2, NY)


def send(src, dst, ss, rs, i, to):
    c = pltpu.make_async_remote_copy(
        src_ref=src,
        dst_ref=dst,
        send_sem=ss.at[i],
        recv_sem=rs.at[i],
        device_id={"seq": to},
        device_id_type=MESH,
    )
    c.start()
    return c


def gather_start(ring, buf, lo, hi, ss, rs):
    y, low, high = ring.y, pl.ds(0, lo), pl.ds(lo, hi)
    a0 = send(buf.at[y, low], buf.at[y, low], ss, rs, 0, ring.right)
    b0 = send(buf.at[y, high], buf.at[y, high], ss, rs, 1, ring.left)
    a1 = send(buf.at[y, high], buf.at[y, high], ss, rs, 2, ring.right)
    b1 = send(buf.at[y, low], buf.at[y, low], ss, rs, 3, ring.left)
    return a0, b0, a1, b1


def gather_forward(ring, buf, lo, hi, ss, rs, copies):
    a0, b0, a1, b1 = copies
    low, high = pl.ds(0, lo), pl.ds(lo, hi)
    a0.wait_recv()
    a2 = send(buf.at[ring.left, low], buf.at[ring.left, low], ss, rs, 4, ring.right)
    b0.wait_recv()
    b2 = send(buf.at[ring.right, high], buf.at[ring.right, high], ss, rs, 5, ring.left)
    a1.wait_recv()
    b1.wait_recv()
    return a2, b2


def nothing():
    pass


def gather_blocks(ring, buf, lo, hi, ss, rs, use, early=nothing, late=nothing):
    first = gather_start(ring, buf, lo, hi, ss, rs)
    early()
    use(ring.y)
    last = gather_forward(ring, buf, lo, hi, ss, rs, first)

    def near(i, carry):
        use(lax.rem(ring.y + 1 + 2 * i, NY))
        return carry

    lax.fori_loop(0, 2, near, 0)
    late()
    for c in last:
        c.wait_recv()
    use(ring.opp)
    for c in first + last:
        c.wait_send()


def scatter_sum(ring, part, lo, hi, sbuf, rbuf, ss, rs, beside=nothing):
    low, high = pl.ds(0, lo), pl.ds(lo, hi)
    sbuf[0] = part[ring.opp].astype(BF16)
    a0 = send(sbuf.at[0, low], rbuf.at[0, low], ss, rs, 0, ring.right)
    b0 = send(sbuf.at[0, high], rbuf.at[0, high], ss, rs, 1, ring.left)
    sbuf[1, high] = part[ring.right, high].astype(BF16)
    a1 = send(sbuf.at[1, high], rbuf.at[1, high], ss, rs, 2, ring.right)
    sbuf[2, low] = part[ring.left, low].astype(BF16)
    b1 = send(sbuf.at[2, low], rbuf.at[2, low], ss, rs, 3, ring.left)
    a0.wait_recv()
    sbuf[1, low] = (part[ring.right, low] + rbuf[0, low].astype(F32)).astype(BF16)
    a2 = send(sbuf.at[1, low], rbuf.at[1, low], ss, rs, 4, ring.right)
    b0.wait_recv()
    sbuf[2, high] = (part[ring.left, high] + rbuf[0, high].astype(F32)).astype(BF16)
    b2 = send(sbuf.at[2, high], rbuf.at[2, high], ss, rs, 5, ring.left)
    beside()
    for c in (a1, b1, a2, b2):
        c.wait_recv()
    total = part[ring.y] + rbuf[1].astype(F32) + rbuf[2].astype(F32)
    for c in (a0, b0, a1, b1, a2, b2):
        c.wait_send()
    return total


def swap_all(d, sbuf, rbuf, ss, rs):
    def copy(k):
        to = lax.rem(d + k, NDP)
        return pltpu.make_async_remote_copy(
            src_ref=sbuf.at[to],
            dst_ref=rbuf.at[d],
            send_sem=ss.at[k],
            recv_sem=rs.at[k],
            device_id={"dp": to},
            device_id_type=MESH,
        )

    def start(k, carry):
        copy(k).start()
        return carry

    lax.fori_loop(1, NDP, start, 0)
    rbuf[d] = sbuf[d]

    def finish(k, carry):
        copy(k).wait()
        return carry

    lax.fori_loop(1, NDP, finish, 0)


class Place:
    def __init__(self):
        d = lax.axis_index("dp")
        self.d = d
        self.z, self.x, self.c = lax.div(d, 8), lax.rem(lax.div(d, 2), 4), lax.rem(d, 2)

    def at(self, z=None, x=None, c=None):
        z, x, c = (m if v is None else v for v, m in ((z, self.z), (x, self.x), (c, self.c)))
        return {"dp": (z * 4 + x) * 2 + c}


def push(src, dst, ssem, rsem, to):
    c = pltpu.make_async_remote_copy(
        src_ref=src, dst_ref=dst, send_sem=ssem, recv_sem=rsem, device_id=to, device_id_type=MESH
    )
    c.start()
    return c


class Weights:
    def __init__(self, R, place, ring):
        self.R, self.p, self.ring = R, place, ring
        self.own, self.got = (R.wa0, R.wa1), (R.wa0g, R.wa1g)
        self.done, self.now = [], {}

    def sems(self, i):
        return self.R.wss.at[i], self.R.wrs.at[i]

    def start(self):
        p = self.p
        for n in range(2):
            buf = self.got[n]
            self.now[n] = [
                push(self.own[n], buf.at[p.z, p.x, p.c], *self.sems(3 * n + k - 1), p.at(x=lax.rem(p.x + k, 4)))
                for k in RING4
            ]
            buf[p.z, p.x, p.c] = self.own[n][...]

    def b_along_z(self):
        R, p = self.R, self.p
        own = R.wbg.at[p.x, p.c]

        def copy(k):
            return pltpu.make_async_remote_copy(
                src_ref=R.wb,
                dst_ref=own,
                send_sem=R.wss.at[5 + k],
                recv_sem=R.wrs.at[6],
                device_id=p.at(z=lax.rem(p.z + k, 4)),
                device_id_type=MESH,
            )

        self.zb = copy

        @pl.when(p.z == self.ring.y)
        def _():
            for k in RING4:
                copy(k).start()
            R.wbg[p.x, p.c] = R.wb[...]

    def along_z(self, n):
        p, buf = self.p, self.got[n]
        for c in self.now[n]:
            c.wait_recv()
        i = 9 + 3 * n
        self.done += self.now[n]
        self.now[n] = [
            push(buf.at[p.z, :, p.c], buf.at[p.z, :, p.c], *self.sems(i + k - 1), p.at(z=lax.rem(p.z + k, 4)))
            for k in RING4
        ]

    def along_core(self, n):
        p, buf = self.p, self.got[n]
        for c in self.now[n]:
            c.wait_recv()
        i = 15 + n
        self.done += self.now[n]
        self.now[n] = [push(buf.at[:, :, p.c], buf.at[:, :, p.c], *self.sems(i), p.at(c=1 - p.c))]

    def finish(self, n):
        for c in self.now[n]:
            c.wait_recv()
        self.done += self.now[n]

    def b_along_x(self):
        p, buf = self.p, self.R.wbg

        @pl.when(p.z != self.ring.y)
        def _():
            self.zb(1).wait_recv()

        self.now[2] = [
            push(buf.at[p.x, p.c], buf.at[p.x, p.c], *self.sems(17 + k - 1), p.at(x=lax.rem(p.x + k, 4)))
            for k in RING4
        ]

    def b_along_core(self):
        p, buf = self.p, self.R.wbg
        for c in self.now[2]:
            c.wait_recv()
        self.done += self.now[2]
        self.now[2] = [push(buf.at[:, p.c], buf.at[:, p.c], *self.sems(20), p.at(c=1 - p.c))]

    def sent(self):
        for c in self.done:
            c.wait_send()

        @pl.when(self.p.z == self.ring.y)
        def _():
            for k in RING4:
                self.zb(k).wait_send()

    def lay_a0(self):
        R = self.R
        self.finish(0)

        def one(z, carry):
            v = R.wa0g[z].astype(F32).reshape(192, 3 * HW).astype(BF16)
            for t in range(3):
                R.wqkv[0, t, pl.ds(pl.multiple_of(192 * z, 192), 192)] = v[:, t * HW : (t + 1) * HW]
            return carry

        lax.fori_loop(0, 4, one, 0)

    def lay_a1(self):
        R = self.R
        self.finish(1)

        def one(z, carry):
            rows = pl.ds(pl.multiple_of(192 * z, 192), 192)
            v = R.wa1g[z].astype(F32).reshape(192, D + 3 * HW).astype(BF16)
            R.up[rows] = v[:, 0:D]
            for t in range(3):
                R.wqkv[1, t, rows] = v[:, D + t * HW : D + (t + 1) * HW]
            return carry

        lax.fori_loop(0, 4, one, 0)

    def lay_b(self):
        R = self.R
        self.finish(2)

        def one(x, carry):
            v = R.wbg[x].astype(F32)
            for i in range(2):
                R.wout[i, pl.ds(pl.multiple_of(48 * x, 48), 48)] = (
                    v[:, 24 * i : 24 * (i + 1)].reshape(48, D).astype(BF16)
                )
            R.down[pl.ds(pl.multiple_of(192 * x, 192), 192)] = v[:, 48:144].reshape(192, D).astype(BF16)
            return carry

        lax.fori_loop(0, 4, one, 0)


def head_mask(h, dtype):
    lane = lax.broadcasted_iota(jnp.int32, (1, HW), 1)
    return ((lane >= 64 * h) & (lane < 64 * (h + 1))).astype(dtype)


def keep_grad(ref, first, grad):
    depth = ref.shape[3]
    count = grad.shape[0] // (4 * depth)
    low = grad.astype(BF16)
    for c in range(2):
        half = low[:, c * HALF : (c + 1) * HALF].reshape(count, 4, depth, HALF)
        ref[c, first : first + count] = half


def flat(ref):
    v = ref[...]
    return v.reshape(v.shape[0] * v.shape[1], v.shape[2])


def attn_forward(R, ring, i, x, gain, shift, w=None):
    nbuf, q, k, v, o, st = R.n[2 * i], R.q[i], R.k[i], R.v[i], R.o[i], R.st[i]
    wqkv, wout, qvb, part, vm = R.wqkv, R.wout, R.qvb, R.part, R.vm
    nbuf[ring.y] = ln_forward(x, gain, shift).astype(BF16)

    def project(j):
        nj = nbuf[j]
        q[j] = ((mm(nj, wqkv[i, 0]) + qvb[pl.ds(2 * i, 1)]).astype(BF16).astype(F32) * 0.125).astype(BF16)
        k[j] = mm(nj, wqkv[i, 1]).astype(BF16)
        v[j] = (mm(nj, wqkv[i, 2]) + qvb[pl.ds(2 * i + 1, 1)]).astype(BF16)

    def early():
        w.along_z(0)
        w.along_core(0)
        w.b_along_z()
        w.lay_a0()

    gather_blocks(
        ring, nbuf, LO, HI, R.ssem.at[2 * i], R.rsem.at[2 * i], project, nothing if w is None else early
    )
    if w is not None:
        w.along_z(1)
        w.b_along_x()
    v_all = flat(v)
    for h in range(HEADS_DEV):
        vm[h] = v_all * head_mask(h, BF16)
    k_all = flat(k)

    def rows(b, carry):
        qb = q[b]
        acc = jnp.zeros((ROWS, HW), F32)
        stats = jnp.zeros((ROWS, 128), F32)
        lane = lax.broadcasted_iota(jnp.int32, (ROWS, 128), 1)
        for h in range(HEADS_DEV):
            s = mm(qb * head_mask(h, BF16), k_all, NT)
            top = jnp.max(s, axis=-1, keepdims=True)
            e = jnp.exp(s - top)
            tot = jnp.sum(e, axis=-1, keepdims=True)
            acc = acc + mm(e.astype(BF16), vm[h]) * (1.0 / tot)
            stats = jnp.where(lane == h, top + jnp.log(tot), stats)
        o[b] = acc
        st[b] = stats
        return carry

    lax.fori_loop(0, 2, rows, 0)
    if w is not None:
        w.b_along_core()
    lax.fori_loop(2, NY, rows, 0)
    if w is not None:
        w.lay_b()
        w.along_core(1)

    def out(b, carry):
        part[b] = mm(o[b].astype(BF16), wout[i])
        return carry

    lax.fori_loop(0, NY, out, 0)
    total = scatter_sum(
        ring,
        part,
        LO,
        HI,
        R.sb,
        R.rb,
        R.ssem.at[2 * i + 1],
        R.rsem.at[2 * i + 1],
        nothing if w is None else w.lay_a1,
    )
    return x + total + R.out_bias[pl.ds(i, 1)]


def attn_backward(R, ring, i, x, gain, grad, slot, hooks):
    nbuf, q, k, v, o, st = R.n[2 * i], R.q[i], R.k[i], R.v[i], R.o[i], R.st[i]
    wqkv, wout, part = R.wqkv, R.wout, R.part
    gb, go, gm, qm, gq, gk, gv, dq = R.gb[slot // 2 % 2], R.go, R.vm, R.qm, R.gq, R.gk, R.gv, R.dq
    low = grad.astype(BF16)
    gb[ring.y] = low
    R.small[pl.ds(8 + i, 1)] = jnp.sum(low.astype(F32), axis=0, keepdims=True)

    def project(j):
        g = mm(gb[j], wout[i], NT).astype(BF16)
        go[j] = g
        prod = g.astype(F32) * o[j]
        stats = st[j]
        lane = lax.broadcasted_iota(jnp.int32, (ROWS, 128), 1)
        for h in range(HEADS_DEV):
            inner = jnp.sum(prod * head_mask(h, F32), axis=-1, keepdims=True)
            stats = jnp.where(lane == 4 + h, inner, stats)
        st[j] = stats

    gather_blocks(ring, gb, LO, HI, R.ssem.at[slot], R.rsem.at[slot], project, hooks[0], hooks[1])
    go_all, q_all = flat(go), flat(q)
    for h in range(HEADS_DEV):
        gm[h] = go_all * head_mask(h, BF16)
        qm[h] = q_all * head_mask(h, BF16)
    stats_t = jnp.transpose(flat(st))
    R.stt[...] = stats_t[0:8]
    dq[...] = jnp.zeros((NY * ROWS, HW), F32)

    def keys(b, carry):
        kb, vb = k[b], v[b]
        dk = jnp.zeros((ROWS, HW), F32)
        dv = jnp.zeros((ROWS, HW), F32)
        for h in range(HEADS_DEV):
            kh = kb * head_mask(h, BF16)
            p = jnp.exp(mm(kh, qm[h], NT) - R.stt[h : h + 1])
            dp = mm(vb, gm[h], NT)
            ds = (p * (dp - R.stt[4 + h : 5 + h])).astype(BF16)
            dv = dv + mm(p.astype(BF16), gm[h])
            dk = dk + mm(ds, qm[h])
            dq[...] += mm(ds, kh, TN)
        gk[b] = dk.astype(BF16)
        gv[b] = dv.astype(BF16)
        return carry

    lax.fori_loop(0, 2, keys, 0)
    hooks[2]()
    lax.fori_loop(2, NY, keys, 0)
    hooks[3]()
    gq[...] = (dq[...] * 0.125).astype(BF16).reshape(NY, ROWS, HW)

    def back(b, carry):
        part[b] = mm(gq[b], wqkv[i, 0], NT) + mm(gk[b], wqkv[i, 1], NT) + mm(gv[b], wqkv[i, 2], NT)
        return carry

    def weights():
        n_all, grads = flat(nbuf), R.g13[i]
        for t, g in enumerate((gq, gk, gv)):
            g_all = flat(g)
            keep_grad(grads, t, mm(g_all, n_all, TN))
            if t != 1:
                at = 12 + 2 * i + t // 2
                R.small[at : at + 1, 0:HW] = jnp.sum(g_all.astype(F32), axis=0, keepdims=True)
        keep_grad(grads, 3, mm(flat(o).astype(BF16), flat(gb), TN))

    first, then = hooks[4]
    if first:
        weights()
        first()
    lax.fori_loop(0, NY, back, 0)

    def beside():
        if not first:
            weights()
        then()

    total = scatter_sum(ring, part, LO, HI, R.sb, R.rb, R.ssem.at[slot + 1], R.rsem.at[slot + 1], beside)
    hooks[5]()
    dx, d_gain, d_shift = ln_backward(x, gain, total)
    R.small[pl.ds(2 * i, 1)] = d_gain
    R.small[pl.ds(4 + 2 * i, 1)] = d_shift
    return grad + dx


def feed_forward(R, ring, x, gain, shift):
    nbuf, u, a, part = R.n[1], R.u, R.a, R.part
    nbuf[ring.y] = ln_forward(x, gain, shift).astype(BF16)

    def use(j):
        uj = mm(nbuf[j], R.up[...]) + R.up_bias[...]
        act, slope = gelu_both(uj)
        u[j] = slope
        aj = act.astype(BF16)
        a[j] = aj
        part[j] = mm(aj, R.down[...])

    gather_blocks(ring, nbuf, LO, HI, R.ssem.at[4], R.rsem.at[4], use)
    total = scatter_sum(ring, part, LO, HI, R.sb, R.rb, R.ssem.at[5], R.rsem.at[5])
    return x + total + R.down_bias[...]


def feed_backward(R, ring, x, gain, grad, slot, hooks):
    nbuf, u, a, part, gb, gu = R.n[1], R.u, R.a, R.part, R.gb[slot // 2 % 2], R.gu
    low = grad.astype(BF16)
    gb[ring.y] = low
    R.small[10:11] = jnp.sum(low.astype(F32), axis=0, keepdims=True)

    def use(j):
        g = (mm(gb[j], R.down[...], NT) * u[j]).astype(BF16)
        gu[j] = g
        part[j] = mm(g, R.up[...], NT)

    gather_blocks(ring, gb, LO, HI, R.ssem.at[slot], R.rsem.at[slot], use, hooks[0], hooks[1])

    def beside():
        n_all, g_all, a_all, gb_all = flat(nbuf), flat(gu), flat(a), flat(gb)
        keep_grad(R.g2, 0, mm(n_all, g_all, TN))
        keep_grad(R.g2, 2, mm(a_all, gb_all, TN))
        R.small[11:12] = jnp.sum(g_all.astype(F32), axis=0, keepdims=True)
        hooks[2]()

    total = scatter_sum(
        ring, part, LO, HI, R.sb, R.rb, R.ssem.at[slot + 1], R.rsem.at[slot + 1], beside
    )
    dx, d_gain, d_shift = ln_backward(x, gain, total)
    R.small[1:2] = d_gain
    R.small[5:6] = d_shift
    return grad + dx


def iota(shape, dim):
    return lax.broadcasted_iota(jnp.int32, shape, dim)


def slot_ids(shape, dim):
    r = iota(shape, dim)
    e, t = r >> 3, r & 7
    z = jnp.where(t < 4, e * 4 + t, -1)
    g = jnp.where(t >= 4, e * 4 + t - 4, -1)
    return z.astype(F32), g.astype(F32)


def one_hot(cond):
    return jnp.where(cond, 1.0, 0.0).astype(BF16)


def mixture(R, ring, d, x, gain, shift):
    low = ln_forward(x, gain, shift).astype(BF16)
    cot = R.cot[...].astype(F32)
    logits = mm(low, R.router[...])

    idc, idr = R.idc, R.idr
    key_c, key_r = [], []
    for k in range(2):
        key_c.append(R.prc[:, k : k + 1] * (2 * ROWS) + 2 * iota((ROWS, 1), 0) + k)
        key_r.append(R.prr[k : k + 1, :] * (2 * ROWS) + 2 * iota((1, ROWS), 1) + k)
    rank_c = [jnp.zeros((ROWS, 1), F32) for _ in range(2)]
    rank_r = [jnp.zeros((1, ROWS), F32) for _ in range(2)]
    for k in range(2):
        for j in range(2):
            same = idc[:, k : k + 1] == idr[j : j + 1, :]
            before = key_r[j] < key_c[k]
            after = key_c[k] < key_r[j]
            rank_c[k] = rank_c[k] + jnp.sum(jnp.where(same & before, 1.0, 0.0), axis=1, keepdims=True)
            rank_r[j] = rank_r[j] + jnp.sum(jnp.where(same & after, 1.0, 0.0), axis=0, keepdims=True)
    kept = [jnp.where(r < CAP, 1.0, 0.0) for r in rank_c]
    slot_c = [jnp.where(rank_c[k] < CAP, idc[:, k : k + 1].astype(F32) * CAP + rank_c[k], 1000.0) for k in range(2)]
    slot_r = [jnp.where(rank_r[k] < CAP, idr[k : k + 1, :].astype(F32) * CAP + rank_r[k], 1000.0) for k in range(2)]

    picks = [jnp.where(iota((ROWS, EXPERTS), 1) == idc[:, k : k + 1], 1.0, 0.0) for k in range(2)]
    chosen = [jnp.sum(logits * p, axis=-1, keepdims=True) for p in picks]
    top = jnp.maximum(chosen[0], chosen[1])
    ex = [jnp.exp(c - top) for c in chosen]
    gates = [e / (ex[0] + ex[1]) for e in ex]

    zid, gid = slot_ids((8 * EXPERTS, ROWS), 0)
    rows = mm(one_hot((zid == slot_r[0]) | (zid == slot_r[1])), low)
    for k in range(2):
        rows = rows + mm(one_hot(gid == slot_r[k]), (gates[k] * cot).astype(BF16))
    R.ds[...] = rows.reshape(EXPERTS, 8, D).astype(BF16)
    swap_all(d, R.ds, R.dr.at[0], R.dssem.at[0], R.drsem.at[0])

    n_slots = CAP * NDP
    back = iota((2 * n_slots, 2 * n_slots), 0)
    col = iota((2 * n_slots, 2 * n_slots), 1)
    s = back & (n_slots - 1)
    src = (s >> 2) * 8 + (s & 3) + jnp.where(back >= n_slots, 4, 0)
    sort = one_hot(src == col)
    arrived = R.dr[0].astype(F32).reshape(2 * n_slots, D).astype(BF16)
    moe = R.moe
    moe[ring.y] = mm(sort, arrived).astype(BF16)
    part = R.mpart

    def use(j):
        z, gy = moe[j, 0:n_slots], moe[j, n_slots : 2 * n_slots]
        c = mm(z, R.e_up[...]) + R.e_up_bias[...].astype(F32)
        act, slope = gelu_both(c)
        b = act.astype(BF16)
        R.eb[j] = b
        gc = (slope * mm(gy, R.e_down[...], NT)).astype(BF16)
        R.egc[j] = gc
        part[j, 0:n_slots] = mm(b, R.e_down[...])
        part[j, n_slots : 2 * n_slots] = mm(gc, R.e_up[...], NT)

    gather_blocks(ring, moe, n_slots, n_slots, R.ssem.at[12], R.rsem.at[12], use)

    def beside():
        z_all = moe[:, 0:n_slots].reshape(NY * n_slots, D)
        gy_all = moe[:, n_slots : 2 * n_slots].reshape(NY * n_slots, D)
        b_all, gc_all = flat(R.eb), flat(R.egc)
        R.g_eup[...] = mm(z_all, gc_all, TN)
        R.g_edown[...] = mm(b_all, gy_all, TN)
        R.g_eub[...] = jnp.sum(gc_all.astype(F32), axis=0, keepdims=True)
        R.g_edb[...] = jnp.sum(gy_all.astype(F32), axis=0, keepdims=True)

    total = scatter_sum(
        ring, part, n_slots, n_slots, R.msb, R.mrb, R.ssem.at[13], R.rsem.at[13], beside
    )
    is_y = jnp.where(iota((2 * n_slots, 1), 0) < n_slots, 1.0, 0.0)
    total = (total + is_y * R.e_down_bias[...]).astype(BF16)
    unsort = one_hot((col & (n_slots - 1)) * 2 - (col & 3) + jnp.where(col >= n_slots, 4, 0) == back)
    R.ds[...] = mm(unsort, total).reshape(NDP, 8, D).astype(BF16)
    swap_all(d, R.ds, R.dr.at[1], R.dssem.at[1], R.drsem.at[1])
    came = R.dr[1].astype(F32).reshape(8 * EXPERTS, D).astype(BF16)

    zid, gid = slot_ids((ROWS, 8 * EXPERTS), 1)
    result = x
    grad_gate = []
    for k in range(2):
        taken = mm(one_hot(zid == slot_c[k]), came)
        result = result + (gates[k] * kept[k]) * taken
        grad_gate.append(kept[k] * jnp.sum(taken * cot, axis=-1, keepdims=True))
    R.result[...] = result
    inner = gates[0] * grad_gate[0] + gates[1] * grad_gate[1]
    gl = sum(gates[k] * (grad_gate[k] - inner) * picks[k] for k in range(2))
    gl_hi = gl.astype(BF16)
    rest = gl - gl_hi.astype(F32)
    gl_mid = rest.astype(BF16)
    gl_lo = (rest - gl_mid.astype(F32)).astype(BF16)
    grad_low = mm(one_hot((gid == slot_c[0]) | (gid == slot_c[1])), came)
    g_router = jnp.zeros((EXPERTS, D), F32)
    for piece in (gl_hi, gl_mid, gl_lo):
        grad_low = grad_low + mm(piece, R.router[...], NT)
        g_router = g_router + mm(piece, low, TN)
    R.small[16 : 16 + EXPERTS] = g_router
    dx, d_gain, d_shift = ln_backward(x, gain, grad_low)
    R.small[3:4] = d_gain
    R.small[7:8] = d_shift
    return cot + dx


ORDERS = ("zxy", "xyz", "yzx")


def sum_scratch(r):
    low, sems = (lambda *sh: pltpu.VMEM(sh, BF16)), pltpu.SemaphoreType.DMA
    a, b = r * 2 // 3, r // 3
    return dict(
        r=low(4, 4, r, HALF),
        xa=low(3, 4, a, HALF),
        zb=low(3, 4, b, HALF),
        ba=low(4, a, HALF),
        bb=low(4, b, HALF),
        za=low(3, a, HALF),
        xb=low(3, b, HALF),
        o=low(r, HALF),
        ss=sems((70,)),
        rs=sems((70,)),
        local=sems,
    )


def wait_all(copies):
    for c in copies:
        c.wait_recv()


def add_up(first, *rest):
    total = first.astype(F32)
    for r in rest:
        total = total + r.astype(F32)
    return total.astype(BF16)


class Pushes:
    def __init__(self, place, ring, ss, rs):
        self.p, self.ring = place, ring
        self.ss, self.rs = ss, rs
        self.all = []
        self.other = place.at(c=1 - place.c)
        self.me = dict(x=place.x, y=ring.y, z=place.z)

    def push(self, src, dst, to):
        i = len(self.all)
        c = push(src, dst, self.ss.at[i], self.rs.at[i], to)
        self.all.append(c)
        return c

    def pos(self, axis, k=0):
        return lax.rem(self.me[axis] + k, 4)

    def peer(self, axis, k):
        at = self.pos(axis, k)
        return {"seq": at} if axis == "y" else self.p.at(**{axis: at})

    def end(self):
        for c in self.all:
            c.wait_send()


class Sum(Pushes):
    def __init__(self, R, place, ring, grad, full, scr):
        s = types.SimpleNamespace(**scr)
        super().__init__(place, ring, s.ss, s.rs)
        self.s, self.grad, self.full = s, grad, full
        self.rows = grad.shape[3]
        self.a = self.rows * 2 // 3
        self.third = self.rows // 3

    def halves(self):
        self.core = [self.push(self.grad.at[1 - self.p.c], self.s.r, self.other)]

    def first_axis(self):
        s, p, a = self.s, self.p, self.a
        wait_all(self.core)

        def add(z, carry):
            s.r[z] = add_up(self.grad[p.c, z], s.r[z])
            return carry

        lax.fori_loop(0, 4, add, 0)
        top, rest = pl.ds(0, a), pl.ds(a, self.rows - a)
        self.na = [self.push(s.r.at[:, self.pos("x", k), top], s.xa.at[k - 1], self.peer("x", k)) for k in RING4]
        self.nb = [self.push(s.r.at[self.pos("z", k), :, rest], s.zb.at[k - 1], self.peer("z", k)) for k in RING4]

    def second_axis(self):
        s, p, a = self.s, self.p, self.a
        wait_all(self.na)
        s.ba[...] = add_up(s.r[:, p.x, 0:a], *(s.xa[k] for k in range(3)))
        self.na = [self.push(s.ba.at[self.pos("z", k)], s.za.at[k - 1], self.peer("z", k)) for k in RING4]
        wait_all(self.nb)
        s.bb[...] = add_up(s.r[p.z, :, a : self.rows], *(s.zb[k] for k in range(3)))
        self.nb = [self.push(s.bb.at[self.pos("x", k)], s.xb.at[k - 1], self.peer("x", k)) for k in RING4]

    def view(self, t, index):
        every = pl.ds(0, 4)
        y, z, x = (index.get(n, every) for n in "yzx")
        return self.full.at[self.p.c, y, z, x, pl.ds(self.third * t, self.third)]

    def own(self):
        s, p, a, me = self.s, self.p, self.a, self.me
        wait_all(self.na)
        s.o[0:a] = add_up(s.ba[p.z], *(s.za[k] for k in range(3)))
        wait_all(self.nb)
        s.o[a : self.rows] = add_up(s.bb[p.x], *(s.xb[k] for k in range(3)))
        self.mine = pltpu.make_async_copy(s.o, self.full.at[p.c, me["y"], p.z, p.x], s.local)
        self.mine.start()
        self.one = [
            [
                self.push(s.o.at[pl.ds(self.third * t, self.third)], self.view(t, me), self.peer(order[0], k))
                for k in RING4
            ]
            for t, order in enumerate(ORDERS)
        ]

    def without(self, *axes):
        return {n: v for n, v in self.me.items() if n not in axes}

    def start(self, t, index, a, axis):
        low, high = (self.view(t, {**index, a: pl.ds(2 * h, 2)}) for h in range(2))
        right, left = self.peer(axis, 1), self.peer(axis, 3)
        a0 = self.push(low, low, right)
        b0 = self.push(high, high, left)
        return a0, b0, self.push(high, high, right), self.push(low, low, left)

    def forward(self, t, index, a, axis, copies):
        a0, b0, a1, b1 = copies
        a0.wait_recv()
        low = self.view(t, {**index, axis: self.pos(axis, 3), a: pl.ds(0, 2)})
        a2 = self.push(low, low, self.peer(axis, 1))
        b0.wait_recv()
        high = self.view(t, {**index, axis: self.pos(axis, 1), a: pl.ds(2, 2)})
        b2 = self.push(high, high, self.peer(axis, 3))
        wait_all((a1, b1))
        return a2, b2

    def to_core(self, t, index):
        v = self.view(t, index)
        self.core.append(self.push(v, v, self.other))

    def two(self):
        self.mine.wait()
        self.hop = []
        for t, (a, b, _) in enumerate(ORDERS):
            wait_all(self.one[t])
            self.hop.append(self.start(t, self.without(a), a, b))

    def two_forward(self):
        self.last = [self.forward(t, self.without(a), a, b, self.hop[t]) for t, (a, b, _) in enumerate(ORDERS)]

    def three(self):
        self.hop, self.core = [], []
        for t, (a, b, c) in enumerate(ORDERS):
            wait_all(self.last[t])
            self.hop.append(self.start(t, self.without(a, b), a, c))
        for t, (a, b, c) in enumerate(ORDERS):
            self.to_core(t, self.without(a, b))

    def three_forward(self):
        self.last = []
        for t, (a, b, c) in enumerate(ORDERS):
            self.last.append(self.forward(t, self.without(a, b), a, c, self.hop[t]))
        for t, (a, b, c) in enumerate(ORDERS):
            self.to_core(t, {c: self.pos(c, 1)})
            self.to_core(t, {c: self.pos(c, 3)})

    def three_end(self):
        for t, (a, b, c) in enumerate(ORDERS):
            wait_all(self.last[t])
            self.to_core(t, {c: self.pos(c, 2)})

    def end(self):
        wait_all(self.core)
        super().end()


class Small(Pushes):
    def __init__(self, R, place, ring):
        super().__init__(place, ring, R.tss, R.trs)
        self.R = R

    def halves(self):
        R = self.R
        for c in range(2):
            R.s0[c] = R.small[:, c * HALF : (c + 1) * HALF].astype(BF16)
        self.now = [self.push(R.s0.at[1 - self.p.c], R.sr, self.other)]

    def along_x(self):
        R = self.R
        wait_all(self.now)
        R.s1[...] = add_up(R.s0[self.p.c], R.sr[...])
        self.now = [self.push(R.s1, R.sx.at[k - 1], self.peer("x", k)) for k in RING4]

    def along_z(self):
        R = self.R
        wait_all(self.now)
        R.s2[...] = add_up(R.s1[...], *(R.sx[k] for k in range(3)))
        self.now = [self.push(R.s2, R.sz.at[k - 1], self.peer("z", k)) for k in RING4]

    def along_y(self):
        R = self.R
        wait_all(self.now)
        own = R.fs.at[self.p.c, self.ring.y]
        own[...] = add_up(R.s2[...], *(R.sz[k] for k in range(3)))
        self.now = [self.push(own, own, self.peer("y", k)) for k in RING4]

    def to_core(self):
        half = self.R.fs.at[self.p.c]
        wait_all(self.now)
        self.now = [self.push(half, half, self.other)]

    def end(self):
        wait_all(self.now)
        super().end()


IN = ("tok", "cot", "gain", "shift", "wa0", "wa1", "wb", "qvb", "out_bias", "up_bias", "down_bias", "router")
IN = IN + ("e_up", "e_up_bias", "e_down", "e_down_bias", "idc", "idr", "prc", "prr")


def outputs():
    return dict(
        result=((ROWS, D), F32),
        d_tok=((ROWS, D), F32),
        g_eup=((D, D), F32),
        g_edown=((D, D), F32),
        g_eub=((1, D), F32),
        g_edb=((1, D), F32),
        fs=((2, 4, 48, HALF), BF16),
        f13=((2, 2, 4, 4, 4, 48, HALF), BF16),
        f2=((2, 4, 4, 4, 96, HALF), BF16),
    )


def scratch():
    blk, att = (NY, ROWS, D), (NY, ROWS, HW)
    low, wide, sems = (lambda *sh: pltpu.VMEM(sh, BF16)), (lambda *sh: pltpu.VMEM(sh, F32)), pltpu.SemaphoreType.DMA
    n_slots = CAP * NDP
    return dict(
        n=[low(*blk) for _ in range(3)],
        q=[low(*att) for _ in range(2)],
        k=[low(*att) for _ in range(2)],
        v=[low(*att) for _ in range(2)],
        o=[wide(*att) for _ in range(2)],
        st=[wide(NY, ROWS, 128) for _ in range(2)],
        gb=[low(*blk) for _ in range(2)],
        go=low(*att),
        gq=low(*att),
        gk=low(*att),
        gv=low(*att),
        vm=low(HEADS_DEV, NY * ROWS, HW),
        qm=low(HEADS_DEV, NY * ROWS, HW),
        dq=wide(NY * ROWS, HW),
        stt=wide(8, NY * ROWS),
        u=wide(*blk),
        a=low(*blk),
        gu=low(*blk),
        moe=low(NY, 2 * n_slots, D),
        mpart=wide(NY, 2 * n_slots, D),
        msb=low(3, 2 * n_slots, D),
        mrb=low(3, 2 * n_slots, D),
        eb=low(NY, n_slots, D),
        egc=low(NY, n_slots, D),
        ds=low(EXPERTS, 8, D),
        dr=low(2, EXPERTS, 8, D),
        wa0g=low(4, 4, 2, 24, 3 * HW),
        wa1g=low(4, 4, 2, 24, D + 3 * HW),
        wbg=low(4, 2, 144, D),
        wqkv=low(2, 3, D, HW),
        wout=low(2, HW, D),
        up=low(D, D),
        down=low(D, D),
        xs=wide(4, ROWS, D),
        gs=wide(ROWS, D),
        small=wide(48, D),
        g13=[low(2, 4, 4, 48, HALF) for _ in range(2)],
        g2=low(2, 4, 4, 96, HALF),
        sums=[sum_scratch(r) for r in (48, 96, 48)],
        s0=low(2, 48, HALF),
        sr=low(48, HALF),
        s1=low(48, HALF),
        sx=low(3, 48, HALF),
        s2=low(48, HALF),
        sz=low(3, 48, HALF),
        ssem=sems((14, 6)),
        rsem=sems((14, 6)),
        dssem=sems((2, NDP)),
        drsem=sems((2, NDP)),
        wss=sems((21,)),
        wrs=sems((21,)),
        tss=sems((11,)),
        trs=sems((11,)),
    )


def kernel(*refs):
    n_in, n_out = len(IN), len(outputs())
    R = types.SimpleNamespace(**dict(zip(IN + tuple(outputs()), refs)), **refs[n_in + n_out])
    R.sb = R.msb.at[:, pl.ds(0, ROWS)]
    R.rb = R.mrb.at[:, pl.ds(0, ROWS)]
    R.part = R.mpart.at[:, pl.ds(0, ROWS)]
    ring, place = Ring(), Place()
    d = place.d
    barrier = pltpu.get_barrier_semaphore()
    for k in RING4:
        pl.semaphore_signal(barrier, inc=1, device_id={"seq": lax.rem(ring.y + k, NY)}, device_id_type=MESH)

    def greet(k, carry):
        pl.semaphore_signal(barrier, inc=1, device_id={"dp": lax.rem(d + k, NDP)}, device_id_type=MESH)
        return carry

    lax.fori_loop(1, NDP, greet, 0)
    R.small[...] = jnp.zeros((48, D), F32)
    pl.semaphore_wait(barrier, NDP + 2)

    gain = lambda j: R.gain[j : j + 1]
    shift = lambda j: R.shift[j : j + 1]
    xs, gs = R.xs, R.gs
    xs[0] = R.tok[...].astype(F32)
    w = Weights(R, place, ring)
    w.start()
    xs[1] = attn_forward(R, ring, 0, xs[0], gain(0), shift(0), w)
    w.sent()
    xs[2] = feed_forward(R, ring, xs[1], gain(1), shift(1))
    xs[3] = attn_forward(R, ring, 1, xs[2], gain(2), shift(2))
    gs[...] = mixture(R, ring, d, xs[3], gain(3), shift(3))

    a1 = Sum(R, place, ring, R.g13[1], R.f13.at[1], R.sums[0])
    ff = Sum(R, place, ring, R.g2, R.f2, R.sums[1])
    a0 = Sum(R, place, ring, R.g13[0], R.f13.at[0], R.sums[2])
    small = Small(R, place, ring)

    def steps(*fs):
        def run():
            for f in fs:
                f()

        return run

    no = nothing
    gs[...] = attn_backward(R, ring, 1, xs[2], gain(2), gs[...], 6, (no, no, no, no, (None, a1.halves), no))
    gs[...] = feed_backward(
        R, ring, xs[1], gain(1), gs[...], 8, (a1.first_axis, a1.second_axis, steps(ff.halves, a1.own))
    )
    R.d_tok[...] = attn_backward(
        R,
        ring,
        0,
        xs[0],
        gain(0),
        gs[...],
        10,
        (
            steps(ff.first_axis, a1.two),
            a1.two_forward,
            steps(ff.second_axis, a1.three),
            steps(ff.own, a1.three_forward),
            (a0.halves, steps(a0.first_axis, ff.two, a1.three_end)),
            steps(a0.second_axis, ff.two_forward),
        ),
    )
    small.halves()
    a0.own()
    ff.three()
    small.along_x()
    a0.two()
    small.along_z()
    a0.two_forward()
    ff.three_forward()
    small.along_y()
    a0.three()
    small.to_core()
    a0.three_forward()
    ff.three_end()
    a0.three_end()
    for s in (a1, ff, a0, small):
        s.end()


def layers(ins):
    vmem, hbm = pl.BlockSpec(memory_space=pltpu.VMEM), pl.BlockSpec(memory_space=pl.ANY)
    out = outputs()
    return dict(
        zip(
            out,
            pl.pallas_call(
                kernel,
                out_shape=[jax.ShapeDtypeStruct(*sh) for sh in out.values()],
                in_specs=[vmem] * len(IN),
                out_specs=[vmem] * (len(out) - 2) + [hbm, hbm],
                scratch_shapes=[scratch()],
                compiler_params=pltpu.CompilerParams(
                    collective_id=0, has_side_effects=True, vmem_limit_bytes=62 * 2**20
                ),
                name="layers",
            )(*ins),
        )
    )


def spread_attention(f13):
    def body(f_ref, qkv_ref, out_ref):
        t = pl.program_id(1)
        v = f_ref[0, 0, :, 0].reshape(D, HALF).astype(F32)

        @pl.when(t < 3)
        def _():
            qkv_ref[0] = jnp.transpose(v)

        @pl.when(t == 3)
        def _():
            out_ref[0] = v

    return pl.pallas_call(
        body,
        grid=(2, 4, 2),
        in_specs=[pl.BlockSpec((1, 1, 4, 1, 4, 48, HALF), lambda i, t, c: (i, c, 0, t, 0, 0, 0))],
        out_specs=[
            pl.BlockSpec((1, HALF, D), lambda i, t, c: (i, jnp.where(t == 3, 1, c), jnp.minimum(t, 2))),
            pl.BlockSpec((1, D, HALF), lambda i, t, c: (i, 0, jnp.where(t == 3, c, 0))),
        ],
        out_shape=[jax.ShapeDtypeStruct((2, D, 3 * D), F32), jax.ShapeDtypeStruct((2, D, D), F32)],
        compiler_params=pltpu.CompilerParams(vmem_limit_bytes=40 * 2**20),
        name="spread_attention",
    )(f13)


def spread_feed(f2):
    def body(f_ref, up_ref, down_ref):
        z = pl.program_id(1)
        v = f_ref[:, 0, 0].reshape(2, HALF, HALF).astype(F32)

        @pl.when(z < 2)
        def _():
            up_ref[:, 0:HALF] = v[0]
            up_ref[:, HALF:D] = v[1]

        @pl.when(z >= 2)
        def _():
            down_ref[:, 0:HALF] = v[0]
            down_ref[:, HALF:D] = v[1]

    return pl.pallas_call(
        body,
        grid=(4, 4),
        in_specs=[pl.BlockSpec((2, 1, 1, 4, 96, HALF), lambda y, z: (0, y, z, 0, 0, 0))],
        out_specs=[
            pl.BlockSpec((HALF, D), lambda y, z: (jnp.minimum(z, 1), y)),
            pl.BlockSpec((HALF, D), lambda y, z: (2 * y + jnp.maximum(z - 2, 0), 0)),
        ],
        out_shape=[jax.ShapeDtypeStruct((D, NY * D), F32), jax.ShapeDtypeStruct((NY * D, D), F32)],
        compiler_params=pltpu.CompilerParams(vmem_limit_bytes=40 * 2**20),
        name="spread_feed",
    )(f2)


def local(
    tokens,
    cotangent,
    ln_gain,
    ln_shift,
    qkv_weight,
    qv_bias,
    out_weight,
    out_bias,
    up_weight,
    up_bias,
    down_weight,
    down_bias,
    router,
    expert_up,
    expert_up_bias,
    expert_down,
    expert_down_bias,
    expert_ids,
    priority,
):
    y = lax.axis_index("seq")
    part = lax.dynamic_slice_in_dim(qkv_weight.reshape(2, 24, 3, D), y * HW, HW, 3).reshape(2, 24, 3 * HW)
    wa1 = jnp.concatenate([lax.dynamic_slice_in_dim(up_weight, y * D, D, 1), part[1]], axis=1)
    wb = jnp.concatenate([out_weight[0], out_weight[1], down_weight], axis=0)
    qvb = lax.dynamic_slice_in_dim(qv_bias.reshape(4, D), y * HW, HW, 1)
    upb = lax.dynamic_slice_in_dim(up_bias, y * D, D, 0)[None]
    ids, pri = expert_ids[0], priority[0]
    outs = layers(
        (
            tokens[0],
            cotangent[0],
            ln_gain,
            ln_shift,
            part[0],
            wa1,
            wb,
            qvb,
            out_bias,
            upb,
            down_bias[None],
            router,
            expert_up[0],
            expert_up_bias,
            expert_down[0],
            expert_down_bias,
            ids,
            ids.T,
            pri,
            pri.T,
        )
    )
    o = types.SimpleNamespace(**outs)
    f13, f2, fs = o.f13, o.f2, o.fs
    g_qkv, g_out = spread_attention(f13)
    g_up, g_down = spread_feed(f2)
    fs = fs.astype(F32).transpose(1, 2, 0, 3).reshape(NY, 48, D)
    small = jnp.sum(fs, axis=0)
    g_qvb = fs[:, 12:16, 0:HW].transpose(1, 0, 2).reshape(2, 2 * D)
    return (
        o.result[None],
        o.d_tok[None],
        small[0:4],
        small[4:8],
        g_qkv,
        g_qvb,
        g_out,
        small[8:10],
        g_up,
        fs[:, 11].reshape(NY * D),
        g_down,
        small[10],
        small[16:48].T,
        o.g_eup[None],
        o.g_eub,
        o.g_edown[None],
        lax.dynamic_slice_in_dim(o.g_edb, y * HW, HW, 1),
    )


def solution(mesh):
    in_specs = (
        P("dp", "seq", None),
        P("dp", "seq", None),
        P(),
        P(),
        P(None, "dp", None),
        P(),
        P(None, "dp", None),
        P(),
        P("dp", None),
        P(),
        P("dp", None),
        P(),
        P(),
        P("dp", None, "seq"),
        P("dp", "seq"),
        P("dp", "seq", None),
        P("dp", None),
        P("dp", "seq", None),
        P("dp", "seq", None),
    )
    out_specs = (
        P("dp", "seq", None),
        P("dp", "seq", None),
        P(),
        P(),
        P(),
        P(),
        P(),
        P(),
        P(),
        P(),
        P(),
        P(),
        P(),
        P("dp", None, "seq"),
        P("dp", "seq"),
        P("dp", "seq", None),
        P("dp", "seq"),
    )
    return jax.shard_map(local, mesh=mesh, in_specs=in_specs, out_specs=out_specs, check_vma=False)
```

```python
import functools
import types

import jax
import jax.numpy as jnp
from jax import lax
from jax.experimental import pallas as pl
from jax.experimental.pallas import tpu as pltpu
from jax.sharding import PartitionSpec as P

MESH = pl.DeviceIdType.MESH
F32, BF16 = jnp.float32, jnp.bfloat16

D = 768
HEADS_DEV = 3
HW = 192
ROWS = 144
NY = 4
NDP = 32
EXPERTS = 32
CAP = 4
EPS = 1e-06
LO, HI = 80, 64
HALF = D // 2

NN = (((1,), (0,)), ((), ()))
RING4 = (1, 2, 3)
NT = (((1,), (1,)), ((), ()))
TN = (((0,), (0,)), ((), ()))


def mm(a, b, dims=NN):
    return lax.dot_general(a, b, dims, preferred_element_type=F32)


def ln_stats(x):
    mean = jnp.mean(x, axis=-1, keepdims=True)
    cen = x - mean
    rstd = lax.rsqrt(jnp.mean(cen * cen, axis=-1, keepdims=True) + EPS)
    return cen * rstd, rstd


def ln_forward(x, gain, shift):
    nhat, _ = ln_stats(x)
    return nhat * gain + shift


def ln_backward(x, gain, grad):
    nhat, rstd = ln_stats(x)
    d_gain = jnp.sum(grad * nhat, axis=0, keepdims=True)
    d_shift = jnp.sum(grad, axis=0, keepdims=True)
    gg = grad * gain
    dx = rstd * (
        gg
        - jnp.mean(gg, axis=-1, keepdims=True)
        - nhat * jnp.mean(gg * nhat, axis=-1, keepdims=True)
    )
    return dx, d_gain, d_shift


GC = 0.7978845608028654
GA = 0.044715


def gelu_both(u):
    sq = u * u
    t = jnp.tanh(GC * u * (1.0 + GA * sq))
    half = 0.5 * (1.0 + t)
    slope = half + 0.5 * u * (1.0 - t * t) * (GC * (1.0 + 3.0 * GA * sq))
    return u * half, slope


class Ring:
    def __init__(self):
        self.y = lax.axis_index("seq")
        self.right = lax.rem(self.y + 1, NY)
        self.left = lax.rem(self.y + 3, NY)
        self.opp = lax.rem(self.y + 2, NY)


def send(src, dst, ss, rs, i, to):
    c = pltpu.make_async_remote_copy(
        src_ref=src,
        dst_ref=dst,
        send_sem=ss.at[i],
        recv_sem=rs.at[i],
        device_id={"seq": to},
        device_id_type=MESH,
    )
    c.start()
    return c


def gather_start(ring, buf, lo, hi, ss, rs):
    y, low, high = ring.y, pl.ds(0, lo), pl.ds(lo, hi)
    a0 = send(buf.at[y, low], buf.at[y, low], ss, rs, 0, ring.right)
    b0 = send(buf.at[y, high], buf.at[y, high], ss, rs, 1, ring.left)
    a1 = send(buf.at[y, high], buf.at[y, high], ss, rs, 2, ring.right)
    b1 = send(buf.at[y, low], buf.at[y, low], ss, rs, 3, ring.left)
    return a0, b0, a1, b1


def gather_forward(ring, buf, lo, hi, ss, rs, copies):
    a0, b0, a1, b1 = copies
    low, high = pl.ds(0, lo), pl.ds(lo, hi)
    a0.wait_recv()
    a2 = send(buf.at[ring.left, low], buf.at[ring.left, low], ss, rs, 4, ring.right)
    b0.wait_recv()
    b2 = send(buf.at[ring.right, high], buf.at[ring.right, high], ss, rs, 5, ring.left)
    a1.wait_recv()
    b1.wait_recv()
    return a2, b2


def nothing():
    pass


def gather_blocks(ring, buf, lo, hi, ss, rs, use, early=nothing, late=nothing):
    first = gather_start(ring, buf, lo, hi, ss, rs)
    early()
    use(ring.y)
    last = gather_forward(ring, buf, lo, hi, ss, rs, first)

    def near(i, carry):
        use(lax.rem(ring.y + 1 + 2 * i, NY))
        return carry

    lax.fori_loop(0, 2, near, 0)
    late()
    for c in last:
        c.wait_recv()
    use(ring.opp)
    for c in first + last:
        c.wait_send()


class Scatter:
    def __init__(self, ring, part, lo, hi, sbuf, rbuf, ss, rs):
        self.ring, self.part, self.sbuf, self.rbuf, self.ss, self.rs = ring, part, sbuf, rbuf, ss, rs
        self.low, self.high = pl.ds(0, lo), pl.ds(lo, hi)
        self.all = []

    def send(self, slot, rows, right):
        i = len(self.all)
        to = self.ring.right if right else self.ring.left
        c = send(self.sbuf.at[slot, rows], self.rbuf.at[slot, rows], self.ss, self.rs, i, to)
        self.all.append(c)
        return c

    def near(self, right):
        slot, rows, j = (1, self.high, self.ring.right) if right else (2, self.low, self.ring.left)
        self.sbuf[slot, rows] = self.part[j, rows].astype(BF16)
        self.send(slot, rows, right)

    def opposite(self):
        self.sbuf[0] = self.part[self.ring.opp].astype(BF16)
        self.over = self.send(0, self.low, True), self.send(0, self.high, False)

    def onward(self):
        for c, slot, rows, j, right in (
            (self.over[0], 1, self.low, self.ring.right, True),
            (self.over[1], 2, self.high, self.ring.left, False),
        ):
            c.wait_recv()
            self.sbuf[slot, rows] = (self.part[j, rows] + self.rbuf[0, rows].astype(F32)).astype(BF16)
            self.send(slot, rows, right)

    def end(self):
        for c in self.all:
            if all(c is not o for o in self.over):
                c.wait_recv()
        total = self.part[self.ring.y] + self.rbuf[1].astype(F32) + self.rbuf[2].astype(F32)
        for c in self.all:
            c.wait_send()
        return total


def pass_through(ring, buf, sc, lo, hi, ss, rs, use, early=nothing, late=nothing, beside=nothing):
    first = gather_start(ring, buf, lo, hi, ss, rs)
    early()
    use(ring.y)
    last = gather_forward(ring, buf, lo, hi, ss, rs, first)

    def near(i, carry):
        use(lax.rem(ring.y + 1 + 2 * i, NY))
        return carry

    lax.fori_loop(0, 2, near, 0)
    sc.near(True)
    sc.near(False)
    late()
    for c in last:
        c.wait_recv()
    use(ring.opp)
    sc.opposite()
    for c in first + last:
        c.wait_send()
    sc.onward()
    beside()
    return sc.end()


def swap_all(d, sbuf, rbuf, ss, rs):
    def copy(k):
        to = lax.rem(d + k, NDP)
        return pltpu.make_async_remote_copy(
            src_ref=sbuf.at[to],
            dst_ref=rbuf.at[d],
            send_sem=ss.at[k],
            recv_sem=rs.at[k],
            device_id={"dp": to},
            device_id_type=MESH,
        )

    def start(k, carry):
        copy(k).start()
        return carry

    lax.fori_loop(1, NDP, start, 0)
    rbuf[d] = sbuf[d]

    def finish(k, carry):
        copy(k).wait()
        return carry

    lax.fori_loop(1, NDP, finish, 0)


class Place:
    def __init__(self):
        d = lax.axis_index("dp")
        self.d = d
        self.z, self.x, self.c = lax.div(d, 8), lax.rem(lax.div(d, 2), 4), lax.rem(d, 2)

    def at(self, z=None, x=None, c=None):
        z, x, c = (m if v is None else v for v, m in ((z, self.z), (x, self.x), (c, self.c)))
        return {"dp": (z * 4 + x) * 2 + c}


def push(src, dst, ssem, rsem, to):
    c = pltpu.make_async_remote_copy(
        src_ref=src, dst_ref=dst, send_sem=ssem, recv_sem=rsem, device_id=to, device_id_type=MESH
    )
    c.start()
    return c


def across(v, sel):
    hi = v.astype(BF16)
    rest = v.astype(F32) - hi.astype(F32)
    mid = rest.astype(BF16)
    return mm(hi, sel) + mm(mid, sel) + mm((rest - mid.astype(F32)).astype(BF16), sel)


class Weights:
    def __init__(self, R, place, ring):
        self.R, self.p, self.ring = R, place, ring
        self.own = (R.wa0, R.wa1, R.w_out, R.w_down)
        self.got = (R.wa0g, R.wa1g, R.woutg, R.wdowng)
        self.done, self.now = [], {}
        self.next = 0

    def push(self, src, dst, to):
        i = self.next
        self.next += 1
        return push(src, dst, self.R.wss.at[i], self.R.wrs.at[i], to)

    def cut(self):
        R, y = self.R, self.ring.y
        sel = one_hot(iota((D, HW), 0) == iota((D, HW), 1) + HW * y)
        for t in range(3):
            at = pl.ds(t * HW, HW)
            R.wa0[:, at] = mm(R.w_qkv[0, :, t * D : (t + 1) * D], sel).astype(BF16)
            R.wa1[:, pl.ds(D + t * HW, HW)] = mm(R.w_qkv[1, :, t * D : (t + 1) * D], sel).astype(BF16)
        R.wa1[:, 0:D] = R.w_up[:, pl.ds(pl.multiple_of(D * y, D), D)]
        for t in range(2):
            R.qvb[2 * t : 2 * t + 2] = across(R.qv_bias[:, t * D : (t + 1) * D], sel)

    def a_along_x(self, n):
        p, buf = self.p, self.got[n]
        self.now[n] = [
            self.push(self.own[n], buf.at[p.z, p.x, p.c], p.at(x=lax.rem(p.x + k, 4))) for k in RING4
        ]
        buf[p.z, p.x, p.c] = self.own[n][...]

    def wait(self, n):
        for c in self.now[n]:
            c.wait_recv()
        self.done += self.now[n]

    def a_along_z(self, n):
        p, buf = self.p, self.got[n]
        self.wait(n)
        row = buf.at[p.z, :, p.c]
        self.now[n] = [self.push(row, row, p.at(z=lax.rem(p.z + k, 4))) for k in RING4]

    def a_along_core(self, n):
        p = self.p
        self.wait(n)
        half = self.got[n].at[:, :, p.c]
        self.now[n] = [self.push(half, half, p.at(c=1 - p.c))]

    def b_copy(self, n, k):
        p, R = self.p, self.R
        return pltpu.make_async_remote_copy(
            src_ref=self.own[n],
            dst_ref=self.got[n].at[p.x, p.c],
            send_sem=R.bss.at[n - 2, k],
            recv_sem=R.bss.at[n - 2, 0],
            device_id=p.at(z=lax.rem(p.z + k, 4)),
            device_id_type=MESH,
        )

    def b_along_z(self, n):
        @pl.when(self.p.z == self.ring.y)
        def _():
            for k in RING4:
                self.b_copy(n, k).start()
            self.got[n][self.p.x, self.p.c] = self.own[n][...]

    def b_along_x(self, n):
        p = self.p

        @pl.when(p.z != self.ring.y)
        def _():
            self.b_copy(n, 1).wait_recv()

        own = self.got[n].at[p.x, p.c]
        self.now[n] = [self.push(own, own, p.at(x=lax.rem(p.x + k, 4))) for k in RING4]

    def b_along_core(self, n):
        p = self.p
        self.wait(n)
        half = self.got[n].at[:, p.c]
        self.now[n] = [self.push(half, half, p.at(c=1 - p.c))]

    def sent(self):
        for c in self.done:
            c.wait_send()

        @pl.when(self.p.z == self.ring.y)
        def _():
            for n in (2, 3):
                for k in RING4:
                    self.b_copy(n, k).wait_send()

    def lay(self, n):
        R = self.R
        self.wait(n)

        def one(j, carry):
            rows = pl.ds(pl.multiple_of(192 * j, 192), 192)
            v = self.got[n][j].astype(F32)
            if n == 0:
                v = v.reshape(192, 3 * HW).astype(BF16)
                for t in range(3):
                    R.wqkv[0, t, rows] = v[:, t * HW : (t + 1) * HW]
            elif n == 1:
                v = v.reshape(192, D + 3 * HW).astype(BF16)
                R.up[rows] = v[:, 0:D]
                for t in range(3):
                    R.wqkv[1, t, rows] = v[:, D + t * HW : D + (t + 1) * HW]
            elif n == 2:
                for i in range(2):
                    R.wout[i, pl.ds(pl.multiple_of(48 * j, 48), 48)] = v[:, i].reshape(48, D).astype(BF16)
            else:
                R.down[rows] = v.reshape(192, D).astype(BF16)
            return carry

        lax.fori_loop(0, 4, one, 0)


def head_mask(h, dtype):
    lane = lax.broadcasted_iota(jnp.int32, (1, HW), 1)
    return ((lane >= 64 * h) & (lane < 64 * (h + 1))).astype(dtype)


def keep_grad(ref, first, grad):
    depth = ref.shape[3]
    count = grad.shape[0] // (4 * depth)
    low = grad.astype(BF16)
    for c in range(2):
        half = low[:, c * HALF : (c + 1) * HALF].reshape(count, 4, depth, HALF)
        ref[c, first : first + count] = half


def flat(ref):
    v = ref[...]
    return v.reshape(v.shape[0] * v.shape[1], v.shape[2])


def attn_forward(R, ring, i, x, gain, shift, w=None):
    nbuf, q, k, v, o, st = R.n[2 * i], R.q[i], R.k[i], R.v[i], R.o[i], R.st[i]
    wqkv, wout, qvb, part, vm = R.wqkv, R.wout, R.qvb, R.part, R.vm
    nbuf[ring.y] = ln_forward(x, gain, shift).astype(BF16)

    def project(j):
        nj = nbuf[j]
        q[j] = ((mm(nj, wqkv[i, 0]) + qvb[i : i + 1]).astype(BF16).astype(F32) * 0.125).astype(BF16)
        k[j] = mm(nj, wqkv[i, 1]).astype(BF16)
        v[j] = (mm(nj, wqkv[i, 2]) + qvb[2 + i : 3 + i]).astype(BF16)

    def early():
        w.a_along_z(0)
        w.b_along_x(2)
        w.a_along_x(1)
        w.b_along_z(3)
        w.a_along_core(0)
        w.lay(0)

    gather_blocks(ring, nbuf, LO, HI, R.ssem.at[2 * i], R.rsem.at[2 * i], project, nothing if w is None else early)
    if w is not None:
        w.b_along_core(2)
        w.a_along_z(1)
    v_all = flat(v)
    for h in range(HEADS_DEV):
        vm[h] = v_all * head_mask(h, BF16)
    k_all = flat(k)

    def rows(b):
        qb = q[b]
        acc = jnp.zeros((ROWS, HW), F32)
        stats = jnp.zeros((ROWS, 128), F32)
        lane = lax.broadcasted_iota(jnp.int32, (ROWS, 128), 1)
        for h in range(HEADS_DEV):
            s = mm(qb * head_mask(h, BF16), k_all, NT)
            top = jnp.max(s, axis=-1, keepdims=True)
            e = jnp.exp(s - top)
            tot = jnp.sum(e, axis=-1, keepdims=True)
            acc = acc + mm(e.astype(BF16), vm[h]) * (1.0 / tot)
            stats = jnp.where(lane == h, top + jnp.log(tot), stats)
        o[b] = acc
        st[b] = stats
        part[b] = mm(acc.astype(BF16), wout[i])

    if w is not None:
        w.lay(2)
        w.b_along_x(3)
    sc = Scatter(ring, part, LO, HI, R.sb, R.rb, R.ssem.at[2 * i + 1], R.rsem.at[2 * i + 1])
    rows(ring.opp)
    sc.opposite()

    def near(t, carry):
        rows(lax.rem(ring.y + 1 + 2 * t, NY))
        return carry

    lax.fori_loop(0, 2, near, 0)
    sc.near(True)
    sc.near(False)
    sc.onward()
    rows(ring.y)
    if w is not None:
        w.a_along_core(1)
        w.b_along_core(3)
    total = sc.end()
    if w is not None:
        w.lay(1)
        w.lay(3)
    return x + total + R.out_bias[i : i + 1]


EARLY, LATE, BEFORE, MIDDLE, AFTER, WEIGHTS, BESIDE, END = range(8)


def attn_backward(R, ring, i, x, gain, grad, slot, hooks):
    nbuf, q, k, v, o, st = R.n[2 * i], R.q[i], R.k[i], R.v[i], R.o[i], R.st[i]
    wqkv, wout, part = R.wqkv, R.wout, R.part
    gb, go, gm, qm, gq, gk, gv, dq = R.gb[slot // 2 % 2], R.go, R.vm, R.qm, R.gq, R.gk, R.gv, R.dq
    low = grad.astype(BF16)
    gb[ring.y] = low
    R.small[pl.ds(8 + i, 1)] = jnp.sum(low.astype(F32), axis=0, keepdims=True)

    def project(j):
        g = mm(gb[j], wout[i], NT).astype(BF16)
        go[j] = g
        prod = g.astype(F32) * o[j]
        stats = st[j]
        lane = lax.broadcasted_iota(jnp.int32, (ROWS, 128), 1)
        for h in range(HEADS_DEV):
            inner = jnp.sum(prod * head_mask(h, F32), axis=-1, keepdims=True)
            stats = jnp.where(lane == 4 + h, inner, stats)
        st[j] = stats

    at = hooks.get
    gather_blocks(
        ring, gb, LO, HI, R.ssem.at[slot], R.rsem.at[slot], project, at(EARLY, nothing), at(LATE, nothing)
    )
    at(BEFORE, nothing)()
    go_all, q_all = flat(go), flat(q)
    for h in range(HEADS_DEV):
        gm[h] = go_all * head_mask(h, BF16)
        qm[h] = q_all * head_mask(h, BF16)
    stats_t = jnp.transpose(flat(st))
    R.stt[...] = stats_t[0:8]
    dq[...] = jnp.zeros((NY * ROWS, HW), F32)

    def keys(b, carry):
        kb, vb = k[b], v[b]
        dk = jnp.zeros((ROWS, HW), F32)
        dv = jnp.zeros((ROWS, HW), F32)
        for h in range(HEADS_DEV):
            kh = kb * head_mask(h, BF16)
            p = jnp.exp(mm(kh, qm[h], NT) - R.stt[h : h + 1])
            dp = mm(vb, gm[h], NT)
            ds = (p * (dp - R.stt[4 + h : 5 + h])).astype(BF16)
            dv = dv + mm(p.astype(BF16), gm[h])
            dk = dk + mm(ds, qm[h])
            dq[...] += mm(ds, kh, TN)
        gk[b] = dk.astype(BF16)
        gv[b] = dv.astype(BF16)
        return carry

    lax.fori_loop(0, 2, keys, 0)
    at(MIDDLE, nothing)()
    lax.fori_loop(2, NY, keys, 0)
    at(AFTER, nothing)()
    gq[...] = (dq[...] * 0.125).astype(BF16).reshape(NY, ROWS, HW)

    def back(b):
        part[b] = mm(gq[b], wqkv[i, 0], NT) + mm(gk[b], wqkv[i, 1], NT) + mm(gv[b], wqkv[i, 2], NT)

    def weights():
        n_all, grads = flat(nbuf), R.g13[i]
        for t, g in enumerate((gq, gk, gv)):
            g_all = flat(g)
            keep_grad(grads, t, mm(g_all, n_all, TN))
            if t != 1:
                row = 12 + 2 * i + t // 2
                R.small[row : row + 1, 0:HW] = jnp.sum(g_all.astype(F32), axis=0, keepdims=True)
        keep_grad(grads, 3, mm(flat(o).astype(BF16), flat(gb), TN))

    if WEIGHTS in hooks:
        weights()
        hooks[WEIGHTS]()
    sc = Scatter(ring, part, LO, HI, R.sb, R.rb, R.ssem.at[slot + 1], R.rsem.at[slot + 1])
    back(ring.opp)
    sc.opposite()

    def near(t, carry):
        back(lax.rem(ring.y + 1 + 2 * t, NY))
        return carry

    lax.fori_loop(0, 2, near, 0)
    sc.near(True)
    sc.near(False)
    sc.onward()
    back(ring.y)
    if WEIGHTS not in hooks:
        weights()
    at(BESIDE, nothing)()
    total = sc.end()
    at(END, nothing)()
    dx, d_gain, d_shift = ln_backward(x, gain, total)
    R.small[pl.ds(2 * i, 1)] = d_gain
    R.small[pl.ds(4 + 2 * i, 1)] = d_shift
    return grad + dx


def across_rows(ref, n):
    return jnp.concatenate([ref[6 * n + j : 6 * n + j + 1] for j in range(6)], axis=1)


def feed_forward(R, ring, x, gain, shift):
    nbuf, u, a, part = R.n[1], R.u, R.a, R.part
    nbuf[ring.y] = ln_forward(x, gain, shift).astype(BF16)
    bias = across_rows(R.up_bias, 0)
    for y in range(1, NY):
        bias = jnp.where(ring.y == y, across_rows(R.up_bias, y), bias)

    def use(j):
        uj = mm(nbuf[j], R.up[...]) + bias
        act, slope = gelu_both(uj)
        u[j] = slope
        aj = act.astype(BF16)
        a[j] = aj
        part[j] = mm(aj, R.down[...])

    sc = Scatter(ring, part, LO, HI, R.sb, R.rb, R.ssem.at[5], R.rsem.at[5])
    total = pass_through(ring, nbuf, sc, LO, HI, R.ssem.at[4], R.rsem.at[4], use)
    return x + total + across_rows(R.down_bias, 0)


def feed_backward(R, ring, x, gain, grad, slot, hooks):
    nbuf, u, a, part, gb, gu = R.n[1], R.u, R.a, R.part, R.gb[slot // 2 % 2], R.gu
    low = grad.astype(BF16)
    gb[ring.y] = low
    R.small[10:11] = jnp.sum(low.astype(F32), axis=0, keepdims=True)

    def use(j):
        g = (mm(gb[j], R.down[...], NT) * u[j]).astype(BF16)
        gu[j] = g
        part[j] = mm(g, R.up[...], NT)

    at = hooks.get

    def beside():
        at(BEFORE, nothing)()
        n_all, g_all, a_all, gb_all = flat(nbuf), flat(gu), flat(a), flat(gb)
        keep_grad(R.g2, 0, mm(n_all, g_all, TN))
        keep_grad(R.g2, 2, mm(a_all, gb_all, TN))
        R.small[11:12] = jnp.sum(g_all.astype(F32), axis=0, keepdims=True)
        at(BESIDE, nothing)()

    sc = Scatter(ring, part, LO, HI, R.sb, R.rb, R.ssem.at[slot + 1], R.rsem.at[slot + 1])
    total = pass_through(
        ring,
        gb,
        sc,
        LO,
        HI,
        R.ssem.at[slot],
        R.rsem.at[slot],
        use,
        at(EARLY, nothing),
        at(LATE, nothing),
        beside,
    )
    at(END, nothing)()
    dx, d_gain, d_shift = ln_backward(x, gain, total)
    R.small[1:2] = d_gain
    R.small[5:6] = d_shift
    return grad + dx


def iota(shape, dim):
    return lax.broadcasted_iota(jnp.int32, shape, dim)


def slot_ids(shape, dim):
    r = iota(shape, dim)
    e, t = r >> 3, r & 7
    z = jnp.where(t < 4, e * 4 + t, -1)
    g = jnp.where(t >= 4, e * 4 + t - 4, -1)
    return z.astype(F32), g.astype(F32)


def one_hot(cond):
    return jnp.where(cond, 1.0, 0.0).astype(BF16)


def mixture(R, ring, d, x, gain, shift):
    low = ln_forward(x, gain, shift).astype(BF16)
    cot = R.cot[...].astype(F32)
    logits = mm(low, R.router[...], NT)

    idr, prr = R.ids[...], R.pri[...]
    digits = jnp.concatenate([idr, prr >> 8, prr & 255], axis=0).astype(F32).astype(BF16)
    turned = mm(one_hot(iota((ROWS, ROWS), 0) == iota((ROWS, ROWS), 1)), digits, NT)
    idc = turned[:, 0:2].astype(jnp.int32)
    prc = (turned[:, 2:4] * 256.0 + turned[:, 4:6]).astype(jnp.int32)
    key_c, key_r = [], []
    for k in range(2):
        key_c.append(prc[:, k : k + 1] * (2 * ROWS) + 2 * iota((ROWS, 1), 0) + k)
        key_r.append(prr[k : k + 1, :] * (2 * ROWS) + 2 * iota((1, ROWS), 1) + k)
    rank_c = [jnp.zeros((ROWS, 1), F32) for _ in range(2)]
    rank_r = [jnp.zeros((1, ROWS), F32) for _ in range(2)]
    for k in range(2):
        for j in range(2):
            same = idc[:, k : k + 1] == idr[j : j + 1, :]
            before = key_r[j] < key_c[k]
            after = key_c[k] < key_r[j]
            rank_c[k] = rank_c[k] + jnp.sum(jnp.where(same & before, 1.0, 0.0), axis=1, keepdims=True)
            rank_r[j] = rank_r[j] + jnp.sum(jnp.where(same & after, 1.0, 0.0), axis=0, keepdims=True)
    kept = [jnp.where(r < CAP, 1.0, 0.0) for r in rank_c]
    slot_c = [jnp.where(rank_c[k] < CAP, idc[:, k : k + 1].astype(F32) * CAP + rank_c[k], 1000.0) for k in range(2)]
    slot_r = [jnp.where(rank_r[k] < CAP, idr[k : k + 1, :].astype(F32) * CAP + rank_r[k], 1000.0) for k in range(2)]

    picks = [jnp.where(iota((ROWS, EXPERTS), 1) == idc[:, k : k + 1], 1.0, 0.0) for k in range(2)]
    chosen = [jnp.sum(logits * p, axis=-1, keepdims=True) for p in picks]
    top = jnp.maximum(chosen[0], chosen[1])
    ex = [jnp.exp(c - top) for c in chosen]
    gates = [e / (ex[0] + ex[1]) for e in ex]

    zid, gid = slot_ids((8 * EXPERTS, ROWS), 0)
    rows = mm(one_hot((zid == slot_r[0]) | (zid == slot_r[1])), low)
    for k in range(2):
        rows = rows + mm(one_hot(gid == slot_r[k]), (gates[k] * cot).astype(BF16))
    R.ds[...] = rows.reshape(EXPERTS, 8, D).astype(BF16)
    swap_all(d, R.ds, R.dr.at[0], R.dssem.at[0], R.drsem.at[0])

    n_slots = CAP * NDP
    back = iota((2 * n_slots, 2 * n_slots), 0)
    col = iota((2 * n_slots, 2 * n_slots), 1)
    s = back & (n_slots - 1)
    src = (s >> 2) * 8 + (s & 3) + jnp.where(back >= n_slots, 4, 0)
    sort = one_hot(src == col)
    arrived = R.dr[0].astype(F32).reshape(2 * n_slots, D).astype(BF16)
    moe = R.moe
    moe[ring.y] = mm(sort, arrived).astype(BF16)
    part = R.mpart

    def use(j):
        z, gy = moe[j, 0:n_slots], moe[j, n_slots : 2 * n_slots]
        c = mm(z, R.e_up[...]) + R.e_up_bias[...].astype(F32)
        act, slope = gelu_both(c)
        b = act.astype(BF16)
        R.eb[j] = b
        gc = (slope * mm(gy, R.e_down[...], NT)).astype(BF16)
        R.egc[j] = gc
        part[j, 0:n_slots] = mm(b, R.e_down[...])
        part[j, n_slots : 2 * n_slots] = mm(gc, R.e_up[...], NT)

    def beside():
        z_all = moe[:, 0:n_slots].reshape(NY * n_slots, D)
        gy_all = moe[:, n_slots : 2 * n_slots].reshape(NY * n_slots, D)
        b_all, gc_all = flat(R.eb), flat(R.egc)
        R.g_eup[...] = mm(z_all, gc_all, TN)
        R.g_edown[...] = mm(b_all, gy_all, TN)
        R.g_eub[...] = jnp.sum(gc_all.astype(F32), axis=0, keepdims=True)
        R.g_edb[...] = jnp.sum(gy_all.astype(F32), axis=0, keepdims=True)

    sc = Scatter(ring, part, n_slots, n_slots, R.msb, R.mrb, R.ssem.at[13], R.rsem.at[13])
    total = pass_through(ring, moe, sc, n_slots, n_slots, R.ssem.at[12], R.rsem.at[12], use, beside=beside)
    is_y = jnp.where(iota((2 * n_slots, 1), 0) < n_slots, 1.0, 0.0)
    total = (total + is_y * R.e_down_bias[...]).astype(BF16)
    unsort = one_hot((col & (n_slots - 1)) * 2 - (col & 3) + jnp.where(col >= n_slots, 4, 0) == back)
    R.ds[...] = mm(unsort, total).reshape(NDP, 8, D).astype(BF16)
    swap_all(d, R.ds, R.dr.at[1], R.dssem.at[1], R.drsem.at[1])
    came = R.dr[1].astype(F32).reshape(8 * EXPERTS, D).astype(BF16)

    zid, gid = slot_ids((ROWS, 8 * EXPERTS), 1)
    result = x
    grad_gate = []
    for k in range(2):
        taken = mm(one_hot(zid == slot_c[k]), came)
        result = result + (gates[k] * kept[k]) * taken
        grad_gate.append(kept[k] * jnp.sum(taken * cot, axis=-1, keepdims=True))
    R.result[...] = result
    inner = gates[0] * grad_gate[0] + gates[1] * grad_gate[1]
    gl = sum(gates[k] * (grad_gate[k] - inner) * picks[k] for k in range(2))
    gl_hi = gl.astype(BF16)
    rest = gl - gl_hi.astype(F32)
    gl_mid = rest.astype(BF16)
    gl_lo = (rest - gl_mid.astype(F32)).astype(BF16)
    grad_low = mm(one_hot((gid == slot_c[0]) | (gid == slot_c[1])), came)
    g_router = jnp.zeros((EXPERTS, D), F32)
    for piece in (gl_hi, gl_mid, gl_lo):
        grad_low = grad_low + mm(piece, R.router[...])
        g_router = g_router + mm(piece, low, TN)
    R.small[16 : 16 + EXPERTS] = g_router
    dx, d_gain, d_shift = ln_backward(x, gain, grad_low)
    R.small[3:4] = d_gain
    R.small[7:8] = d_shift
    return cot + dx


ORDERS = ("zxy", "xyz", "yzx")


def sum_scratch(r):
    low, sems = (lambda *sh: pltpu.VMEM(sh, BF16)), pltpu.SemaphoreType.DMA
    a, b = r * 2 // 3, r // 3
    return dict(
        r=low(4, 4, r, HALF),
        xa=low(3, 4, a, HALF),
        zb=low(3, 4, b, HALF),
        ba=low(4, a, HALF),
        bb=low(4, b, HALF),
        za=low(3, a, HALF),
        xb=low(3, b, HALF),
        o=low(r, HALF),
        ss=sems((70,)),
        rs=sems((70,)),
        local=sems,
    )


def wait_all(copies):
    for c in copies:
        c.wait_recv()


def add_up(first, *rest):
    total = first.astype(F32)
    for r in rest:
        total = total + r.astype(F32)
    return total.astype(BF16)


class Pushes:
    def __init__(self, place, ring, ss, rs):
        self.p, self.ring = place, ring
        self.ss, self.rs = ss, rs
        self.all = []
        self.other = place.at(c=1 - place.c)
        self.me = dict(x=place.x, y=ring.y, z=place.z)

    def push(self, src, dst, to):
        i = len(self.all)
        c = push(src, dst, self.ss.at[i], self.rs.at[i], to)
        self.all.append(c)
        return c

    def pos(self, axis, k=0):
        return lax.rem(self.me[axis] + k, 4)

    def peer(self, axis, k):
        at = self.pos(axis, k)
        return {"seq": at} if axis == "y" else self.p.at(**{axis: at})

    def end(self):
        for c in self.all:
            c.wait_send()


class Sum(Pushes):
    def __init__(self, R, place, ring, grad, full, scr):
        s = types.SimpleNamespace(**scr)
        super().__init__(place, ring, s.ss, s.rs)
        self.s, self.grad, self.full = s, grad, full
        self.rows = grad.shape[3]
        self.a = self.rows * 2 // 3
        self.third = self.rows // 3

    def halves(self):
        self.core = [self.push(self.grad.at[1 - self.p.c], self.s.r, self.other)]

    def first_axis(self):
        s, p, a = self.s, self.p, self.a
        wait_all(self.core)

        def add(z, carry):
            s.r[z] = add_up(self.grad[p.c, z], s.r[z])
            return carry

        lax.fori_loop(0, 4, add, 0)
        top, rest = pl.ds(0, a), pl.ds(a, self.rows - a)
        self.na = [self.push(s.r.at[:, self.pos("x", k), top], s.xa.at[k - 1], self.peer("x", k)) for k in RING4]
        self.nb = [self.push(s.r.at[self.pos("z", k), :, rest], s.zb.at[k - 1], self.peer("z", k)) for k in RING4]

    def second_axis(self):
        s, p, a = self.s, self.p, self.a
        wait_all(self.na)
        s.ba[...] = add_up(s.r[:, p.x, 0:a], *(s.xa[k] for k in range(3)))
        self.na = [self.push(s.ba.at[self.pos("z", k)], s.za.at[k - 1], self.peer("z", k)) for k in RING4]
        wait_all(self.nb)
        s.bb[...] = add_up(s.r[p.z, :, a : self.rows], *(s.zb[k] for k in range(3)))
        self.nb = [self.push(s.bb.at[self.pos("x", k)], s.xb.at[k - 1], self.peer("x", k)) for k in RING4]

    def view(self, t, index):
        every = pl.ds(0, 4)
        y, z, x = (index.get(n, every) for n in "yzx")
        return self.full.at[self.p.c, y, z, x, pl.ds(self.third * t, self.third)]

    def own(self):
        s, p, a, me = self.s, self.p, self.a, self.me
        wait_all(self.na)
        s.o[0:a] = add_up(s.ba[p.z], *(s.za[k] for k in range(3)))
        wait_all(self.nb)
        s.o[a : self.rows] = add_up(s.bb[p.x], *(s.xb[k] for k in range(3)))
        self.mine = pltpu.make_async_copy(s.o, self.full.at[p.c, me["y"], p.z, p.x], s.local)
        self.mine.start()
        self.one = [
            [
                self.push(s.o.at[pl.ds(self.third * t, self.third)], self.view(t, me), self.peer(order[0], k))
                for k in RING4
            ]
            for t, order in enumerate(ORDERS)
        ]

    def without(self, *axes):
        return {n: v for n, v in self.me.items() if n not in axes}

    def start(self, t, index, a, axis):
        low, high = (self.view(t, {**index, a: pl.ds(2 * h, 2)}) for h in range(2))
        right, left = self.peer(axis, 1), self.peer(axis, 3)
        a0 = self.push(low, low, right)
        b0 = self.push(high, high, left)
        return a0, b0, self.push(high, high, right), self.push(low, low, left)

    def forward(self, t, index, a, axis, copies):
        a0, b0, a1, b1 = copies
        a0.wait_recv()
        low = self.view(t, {**index, axis: self.pos(axis, 3), a: pl.ds(0, 2)})
        a2 = self.push(low, low, self.peer(axis, 1))
        b0.wait_recv()
        high = self.view(t, {**index, axis: self.pos(axis, 1), a: pl.ds(2, 2)})
        b2 = self.push(high, high, self.peer(axis, 3))
        wait_all((a1, b1))
        return a2, b2

    def to_core(self, t, index):
        v = self.view(t, index)
        self.core.append(self.push(v, v, self.other))

    def two(self):
        self.mine.wait()
        self.hop = []
        for t, (a, b, _) in enumerate(ORDERS):
            wait_all(self.one[t])
            self.hop.append(self.start(t, self.without(a), a, b))

    def two_forward(self):
        self.last = [self.forward(t, self.without(a), a, b, self.hop[t]) for t, (a, b, _) in enumerate(ORDERS)]

    def three(self):
        self.hop, self.core = [], []
        for t, (a, b, c) in enumerate(ORDERS):
            wait_all(self.last[t])
            self.hop.append(self.start(t, self.without(a, b), a, c))
        for t, (a, b, c) in enumerate(ORDERS):
            self.to_core(t, self.without(a, b))

    def three_forward(self):
        self.last = []
        for t, (a, b, c) in enumerate(ORDERS):
            self.last.append(self.forward(t, self.without(a, b), a, c, self.hop[t]))
        for t, (a, b, c) in enumerate(ORDERS):
            self.to_core(t, {c: self.pos(c, 1)})
            self.to_core(t, {c: self.pos(c, 3)})

    def three_end(self):
        for t, (a, b, c) in enumerate(ORDERS):
            wait_all(self.last[t])
            self.to_core(t, {c: self.pos(c, 2)})

    def end(self):
        wait_all(self.core)
        super().end()


class Small(Pushes):
    def __init__(self, R, place, ring):
        super().__init__(place, ring, R.tss, R.trs)
        self.R = R

    def halves(self):
        R = self.R
        for c in range(2):
            R.s0[c] = R.small[:, c * HALF : (c + 1) * HALF].astype(BF16)
        self.now = [self.push(R.s0.at[1 - self.p.c], R.sr, self.other)]

    def along_x(self):
        R = self.R
        wait_all(self.now)
        R.s1[...] = add_up(R.s0[self.p.c], R.sr[...])
        self.now = [self.push(R.s1, R.sx.at[k - 1], self.peer("x", k)) for k in RING4]

    def along_z(self):
        R = self.R
        wait_all(self.now)
        R.s2[...] = add_up(R.s1[...], *(R.sx[k] for k in range(3)))
        self.now = [self.push(R.s2, R.sz.at[k - 1], self.peer("z", k)) for k in RING4]

    def along_y(self):
        R = self.R
        wait_all(self.now)
        own = R.fs.at[self.p.c, self.ring.y]
        own[...] = add_up(R.s2[...], *(R.sz[k] for k in range(3)))
        self.now = [self.push(own, own, self.peer("y", k)) for k in RING4]

    def to_core(self):
        half = self.R.fs.at[self.p.c]
        wait_all(self.now)
        self.now = [self.push(half, half, self.other)]

    def end(self):
        wait_all(self.now)
        super().end()


IN = ("tok", "cot", "gain", "shift", "w_qkv", "qv_bias", "w_out", "out_bias", "w_up", "up_bias", "w_down", "down_bias")
IN = IN + ("router", "e_up", "e_up_bias", "e_down", "e_down_bias", "ids", "pri")


def outputs():
    return dict(
        result=((ROWS, D), F32),
        d_tok=((ROWS, D), F32),
        g_eup=((D, D), F32),
        g_edown=((D, D), F32),
        g_eub=((1, D), F32),
        g_edb=((1, D), F32),
        fs=((2, 4, 48, HALF), BF16),
        f13=((2, 2, 4, 4, 4, 48, HALF), BF16),
        f2=((2, 4, 4, 4, 96, HALF), BF16),
    )


def scratch():
    blk, att = (NY, ROWS, D), (NY, ROWS, HW)
    low, wide, sems = (lambda *sh: pltpu.VMEM(sh, BF16)), (lambda *sh: pltpu.VMEM(sh, F32)), pltpu.SemaphoreType.DMA
    n_slots = CAP * NDP
    return dict(
        n=[low(*blk) for _ in range(3)],
        q=[low(*att) for _ in range(2)],
        k=[low(*att) for _ in range(2)],
        v=[low(*att) for _ in range(2)],
        o=[wide(*att) for _ in range(2)],
        st=[wide(NY, ROWS, 128) for _ in range(2)],
        gb=[low(*blk) for _ in range(2)],
        go=low(*att),
        gq=low(*att),
        gk=low(*att),
        gv=low(*att),
        vm=low(HEADS_DEV, NY * ROWS, HW),
        qm=low(HEADS_DEV, NY * ROWS, HW),
        dq=wide(NY * ROWS, HW),
        stt=wide(8, NY * ROWS),
        u=wide(*blk),
        a=low(*blk),
        gu=low(*blk),
        moe=low(NY, 2 * n_slots, D),
        mpart=wide(NY, 2 * n_slots, D),
        msb=low(3, 2 * n_slots, D),
        mrb=low(3, 2 * n_slots, D),
        eb=low(NY, n_slots, D),
        egc=low(NY, n_slots, D),
        ds=low(EXPERTS, 8, D),
        dr=low(2, EXPERTS, 8, D),
        wa0g=low(4, 4, 2, 24, 3 * HW),
        wa1g=low(4, 4, 2, 24, D + 3 * HW),
        wa0=low(24, 3 * HW),
        wa1=low(24, D + 3 * HW),
        woutg=low(4, 2, 2, 24, D),
        wdowng=low(4, 2, 96, D),
        qvb=wide(4, HW),
        wqkv=low(2, 3, D, HW),
        wout=low(2, HW, D),
        up=low(D, D),
        down=low(D, D),
        xs=wide(4, ROWS, D),
        gs=wide(ROWS, D),
        small=wide(48, D),
        g13=[low(2, 4, 4, 48, HALF) for _ in range(2)],
        g2=low(2, 4, 4, 96, HALF),
        sums=[sum_scratch(r) for r in (48, 96, 48)],
        s0=low(2, 48, HALF),
        sr=low(48, HALF),
        s1=low(48, HALF),
        sx=low(3, 48, HALF),
        s2=low(48, HALF),
        sz=low(3, 48, HALF),
        ssem=sems((14, 6)),
        rsem=sems((14, 6)),
        dssem=sems((2, NDP)),
        drsem=sems((2, NDP)),
        wss=sems((22,)),
        wrs=sems((22,)),
        bss=sems((2, 4)),
        tss=sems((11,)),
        trs=sems((11,)),
    )


def kernel(*refs):
    n_in, n_out = len(IN), len(outputs())
    R = types.SimpleNamespace(**dict(zip(IN + tuple(outputs()), refs)), **refs[n_in + n_out])
    R.sb = R.msb.at[:, pl.ds(0, ROWS)]
    R.rb = R.mrb.at[:, pl.ds(0, ROWS)]
    R.part = R.mpart.at[:, pl.ds(0, ROWS)]
    ring, place = Ring(), Place()
    d = place.d
    barrier = pltpu.get_barrier_semaphore()
    for k in RING4:
        pl.semaphore_signal(barrier, inc=1, device_id={"seq": lax.rem(ring.y + k, NY)}, device_id_type=MESH)

    def greet(k, carry):
        pl.semaphore_signal(barrier, inc=1, device_id={"dp": lax.rem(d + k, NDP)}, device_id_type=MESH)
        return carry

    lax.fori_loop(1, NDP, greet, 0)
    R.small[...] = jnp.zeros((48, D), F32)
    w = Weights(R, place, ring)
    w.cut()
    pl.semaphore_wait(barrier, NDP + 2)

    gain = lambda j: R.gain[j : j + 1]
    shift = lambda j: R.shift[j : j + 1]
    xs, gs = R.xs, R.gs
    xs[0] = R.tok[...].astype(F32)
    w.b_along_z(2)
    w.a_along_x(0)
    xs[1] = attn_forward(R, ring, 0, xs[0], gain(0), shift(0), w)
    w.sent()
    xs[2] = feed_forward(R, ring, xs[1], gain(1), shift(1))
    xs[3] = attn_forward(R, ring, 1, xs[2], gain(2), shift(2))
    gs[...] = mixture(R, ring, d, xs[3], gain(3), shift(3))

    a1 = Sum(R, place, ring, R.g13[1], R.f13.at[1], R.sums[0])
    ff = Sum(R, place, ring, R.g2, R.f2, R.sums[1])
    a0 = Sum(R, place, ring, R.g13[0], R.f13.at[0], R.sums[2])
    small = Small(R, place, ring)

    def steps(*fs):
        def run():
            for f in fs:
                f()

        return run

    gs[...] = attn_backward(R, ring, 1, xs[2], gain(2), gs[...], 6, {BESIDE: a1.halves, END: a1.first_axis})
    gs[...] = feed_backward(
        R,
        ring,
        xs[1],
        gain(1),
        gs[...],
        8,
        {
            LATE: a1.second_axis,
            BEFORE: a1.own,
            BESIDE: steps(ff.halves, a1.two),
            END: steps(ff.first_axis, a1.two_forward),
        },
    )
    R.d_tok[...] = attn_backward(
        R,
        ring,
        0,
        xs[0],
        gain(0),
        gs[...],
        10,
        {
            LATE: a1.three,
            BEFORE: ff.second_axis,
            MIDDLE: ff.own,
            AFTER: steps(ff.two, a1.three_forward),
            WEIGHTS: a0.halves,
            BESIDE: steps(ff.two_forward, a0.first_axis, a1.three_end),
            END: steps(a0.second_axis, ff.three),
        },
    )
    small.halves()
    a0.own()
    small.along_x()
    a0.two()
    small.along_z()
    a0.two_forward()
    ff.three_forward()
    small.along_y()
    a0.three()
    small.to_core()
    ff.three_end()
    a0.three_forward()
    a0.three_end()
    for s in (a1, ff, a0, small):
        s.end()


def layers(ins):
    vmem, hbm = pl.BlockSpec(memory_space=pltpu.VMEM), pl.BlockSpec(memory_space=pl.ANY)
    out = outputs()
    return dict(
        zip(
            out,
            pl.pallas_call(
                kernel,
                out_shape=[jax.ShapeDtypeStruct(*sh) for sh in out.values()],
                in_specs=[vmem] * len(IN),
                out_specs=[vmem] * (len(out) - 2) + [hbm, hbm],
                scratch_shapes=[scratch()],
                compiler_params=pltpu.CompilerParams(
                    collective_id=0, has_side_effects=True, vmem_limit_bytes=62 * 2**20
                ),
                name="layers",
            )(*ins),
        )
    )


def spread_attention(f13):
    def body(f_ref, qkv_ref, out_ref):
        t = pl.program_id(1)
        v = f_ref[0, 0, :, 0].reshape(D, HALF).astype(F32)

        @pl.when(t < 3)
        def _():
            qkv_ref[0] = jnp.transpose(v)

        @pl.when(t == 3)
        def _():
            out_ref[0] = v

    return pl.pallas_call(
        body,
        grid=(2, 4, 2),
        in_specs=[pl.BlockSpec((1, 1, 4, 1, 4, 48, HALF), lambda i, t, c: (i, c, 0, t, 0, 0, 0))],
        out_specs=[
            pl.BlockSpec((1, HALF, D), lambda i, t, c: (i, jnp.where(t == 3, 1, c), jnp.minimum(t, 2))),
            pl.BlockSpec((1, D, HALF), lambda i, t, c: (i, 0, jnp.where(t == 3, c, 0))),
        ],
        out_shape=[jax.ShapeDtypeStruct((2, D, 3 * D), F32), jax.ShapeDtypeStruct((2, D, D), F32)],
        compiler_params=pltpu.CompilerParams(vmem_limit_bytes=40 * 2**20),
        name="spread_attention",
    )(f13)


def spread_feed(f2, fs, g_edb):
    def body(f_ref, fs_ref, edb_ref, up_ref, down_ref, gain, shift, outb, downb, upb, qvb, router, edb):
        z = pl.program_id(1)
        v = f_ref[:, 0, 0].reshape(2, HALF, HALF).astype(F32)

        @pl.when(z < 2)
        def _():
            up_ref[:, 0:HALF] = v[0]
            up_ref[:, HALF:D] = v[1]

        @pl.when(z >= 2)
        def _():
            down_ref[:, 0:HALF] = v[0]
            down_ref[:, HALF:D] = v[1]

        @pl.when((z == 0) & (pl.program_id(0) == 0))
        def _():
            by_y = [jnp.concatenate([fs_ref[0, y], fs_ref[1, y]], axis=1).astype(F32) for y in range(NY)]
            total = by_y[0] + by_y[1] + by_y[2] + by_y[3]
            gain[...] = total[0:4]
            shift[...] = total[4:8]
            outb[...] = total[8:10]
            downb[...] = total[10:11]
            router[...] = total[16:48]
            for y in range(NY):
                upb[:, y * D : (y + 1) * D] = by_y[y][11:12]
                for i in range(2):
                    for t in range(2):
                        row = by_y[y][12 + 2 * i + t : 13 + 2 * i + t, 0:HW]
                        qvb[i : i + 1, t * D + y * HW : t * D + (y + 1) * HW] = row
            own = edb_ref[:, 0:HW]
            for y in range(1, NY):
                own = jnp.where(lax.axis_index("seq") == y, edb_ref[:, y * HW : (y + 1) * HW], own)
            edb[...] = own

    small = [(4, D), (4, D), (2, D), (1, D), (1, NY * D), (2, 2 * D), (EXPERTS, D), (1, HW)]
    whole = lambda sh: pl.BlockSpec(sh, lambda y, z: (0,) * len(sh))
    return pl.pallas_call(
        body,
        grid=(4, 4),
        in_specs=[
            pl.BlockSpec((2, 1, 1, 4, 96, HALF), lambda y, z: (0, y, z, 0, 0, 0)),
            whole((2, 4, 48, HALF)),
            whole((1, D)),
        ],
        out_specs=[
            pl.BlockSpec((HALF, D), lambda y, z: (jnp.minimum(z, 1), y)),
            pl.BlockSpec((HALF, D), lambda y, z: (2 * y + jnp.maximum(z - 2, 0), 0)),
        ]
        + [whole(sh) for sh in small],
        out_shape=[jax.ShapeDtypeStruct((D, NY * D), F32), jax.ShapeDtypeStruct((NY * D, D), F32)]
        + [jax.ShapeDtypeStruct(sh, F32) for sh in small],
        compiler_params=pltpu.CompilerParams(vmem_limit_bytes=40 * 2**20),
        name="spread_feed",
    )(f2, fs, g_edb)


def local(
    tokens,
    cotangent,
    ln_gain,
    ln_shift,
    qkv_weight,
    qv_bias,
    out_weight,
    out_bias,
    up_weight,
    up_bias,
    down_weight,
    down_bias,
    router,
    expert_up,
    expert_up_bias,
    expert_down,
    expert_down_bias,
    expert_ids,
    priority,
):
    o = types.SimpleNamespace(
        **layers(
            (
                tokens[0],
                cotangent[0],
                ln_gain,
                ln_shift,
                qkv_weight,
                qv_bias,
                out_weight,
                out_bias,
                up_weight,
                up_bias.reshape(24, 128),
                down_weight,
                down_bias.reshape(6, 128),
                router.T,
                expert_up[0],
                expert_up_bias,
                expert_down[0],
                expert_down_bias,
                expert_ids[0].T,
                priority[0].T,
            )
        )
    )
    g_qkv, g_out = spread_attention(o.f13)
    g_up, g_down, gain, shift, outb, downb, upb, qvb, g_router, edb = spread_feed(o.f2, o.fs, o.g_edb)
    return (
        o.result[None],
        o.d_tok[None],
        gain,
        shift,
        g_qkv,
        qvb,
        g_out,
        outb,
        g_up,
        upb.reshape(NY * D),
        g_down,
        downb.reshape(D),
        g_router.T,
        o.g_eup[None],
        o.g_eub,
        o.g_edown[None],
        edb,
    )


def solution(mesh):
    in_specs = (
        P("dp", "seq", None),
        P("dp", "seq", None),
        P(),
        P(),
        P(None, "dp", None),
        P(),
        P(None, "dp", None),
        P(),
        P("dp", None),
        P(),
        P("dp", None),
        P(),
        P(),
        P("dp", None, "seq"),
        P("dp", "seq"),
        P("dp", "seq", None),
        P("dp", None),
        P("dp", "seq", None),
        P("dp", "seq", None),
    )
    out_specs = (
        P("dp", "seq", None),
        P("dp", "seq", None),
        P(),
        P(),
        P(),
        P(),
        P(),
        P(),
        P(),
        P(),
        P(),
        P(),
        P(),
        P("dp", None, "seq"),
        P("dp", "seq"),
        P("dp", "seq", None),
        P("dp", "seq"),
    )
    return jax.shard_map(local, mesh=mesh, in_specs=in_specs, out_specs=out_specs, check_vma=False)
```

```python
import functools
import types

import jax
import jax.numpy as jnp
from jax import lax
from jax.experimental import pallas as pl
from jax.experimental.pallas import tpu as pltpu
from jax.sharding import PartitionSpec as P

MESH = pl.DeviceIdType.MESH
F32, BF16 = jnp.float32, jnp.bfloat16

D = 768
HEADS_DEV = 3
HW = 192
ROWS = 144
NY = 4
NDP = 32
EXPERTS = 32
CAP = 4
EPS = 1e-06
LO, HI = 80, 64
HALF = D // 2

NN = (((1,), (0,)), ((), ()))
RING4 = (1, 2, 3)
NT = (((1,), (1,)), ((), ()))
TN = (((0,), (0,)), ((), ()))


def mm(a, b, dims=NN):
    return lax.dot_general(a, b, dims, preferred_element_type=F32)


def ln_stats(x):
    mean = jnp.mean(x, axis=-1, keepdims=True)
    cen = x - mean
    rstd = lax.rsqrt(jnp.mean(cen * cen, axis=-1, keepdims=True) + EPS)
    return cen * rstd, rstd


def ln_forward(x, gain, shift):
    nhat, _ = ln_stats(x)
    return nhat * gain + shift


def ln_backward(x, gain, grad):
    nhat, rstd = ln_stats(x)
    d_gain = jnp.sum(grad * nhat, axis=0, keepdims=True)
    d_shift = jnp.sum(grad, axis=0, keepdims=True)
    gg = grad * gain
    dx = rstd * (
        gg
        - jnp.mean(gg, axis=-1, keepdims=True)
        - nhat * jnp.mean(gg * nhat, axis=-1, keepdims=True)
    )
    return dx, d_gain, d_shift


GC = 0.7978845608028654
GA = 0.044715


def gelu_both(u):
    sq = u * u
    t = jnp.tanh(GC * u * (1.0 + GA * sq))
    half = 0.5 * (1.0 + t)
    slope = half + 0.5 * u * (1.0 - t * t) * (GC * (1.0 + 3.0 * GA * sq))
    return u * half, slope


class Ring:
    def __init__(self):
        self.y = lax.axis_index("seq")
        self.right = lax.rem(self.y + 1, NY)
        self.left = lax.rem(self.y + 3, NY)
        self.opp = lax.rem(self.y + 2, NY)


def send(src, dst, ss, rs, i, to):
    c = pltpu.make_async_remote_copy(
        src_ref=src,
        dst_ref=dst,
        send_sem=ss.at[i],
        recv_sem=rs.at[i],
        device_id={"seq": to},
        device_id_type=MESH,
    )
    c.start()
    return c


def gather_start(ring, buf, lo, hi, ss, rs):
    y, low, high = ring.y, pl.ds(0, lo), pl.ds(lo, hi)
    a0 = send(buf.at[y, low], buf.at[y, low], ss, rs, 0, ring.right)
    b0 = send(buf.at[y, high], buf.at[y, high], ss, rs, 1, ring.left)
    a1 = send(buf.at[y, high], buf.at[y, high], ss, rs, 2, ring.right)
    b1 = send(buf.at[y, low], buf.at[y, low], ss, rs, 3, ring.left)
    return a0, b0, a1, b1


def gather_forward(ring, buf, lo, hi, ss, rs, copies):
    a0, b0, a1, b1 = copies
    low, high = pl.ds(0, lo), pl.ds(lo, hi)
    a0.wait_recv()
    a2 = send(buf.at[ring.left, low], buf.at[ring.left, low], ss, rs, 4, ring.right)
    b0.wait_recv()
    b2 = send(buf.at[ring.right, high], buf.at[ring.right, high], ss, rs, 5, ring.left)
    a1.wait_recv()
    b1.wait_recv()
    return a2, b2


def nothing():
    pass


def gather_blocks(ring, buf, lo, hi, ss, rs, use, early=nothing, late=nothing):
    first = gather_start(ring, buf, lo, hi, ss, rs)
    early()
    use(ring.y)
    last = gather_forward(ring, buf, lo, hi, ss, rs, first)

    def near(i, carry):
        use(lax.rem(ring.y + 1 + 2 * i, NY))
        return carry

    lax.fori_loop(0, 2, near, 0)
    late()
    for c in last:
        c.wait_recv()
    use(ring.opp)
    for c in first + last:
        c.wait_send()


class Scatter:
    def __init__(self, ring, part, lo, hi, sbuf, rbuf, ss, rs):
        self.ring, self.part, self.sbuf, self.rbuf, self.ss, self.rs = ring, part, sbuf, rbuf, ss, rs
        self.low, self.high = pl.ds(0, lo), pl.ds(lo, hi)
        self.all = []

    def send(self, slot, rows, right):
        i = len(self.all)
        to = self.ring.right if right else self.ring.left
        c = send(self.sbuf.at[slot, rows], self.rbuf.at[slot, rows], self.ss, self.rs, i, to)
        self.all.append(c)
        return c

    def near(self, right):
        slot, rows, j = (1, self.high, self.ring.right) if right else (2, self.low, self.ring.left)
        self.sbuf[slot, rows] = self.part[j, rows].astype(BF16)
        self.send(slot, rows, right)

    def opposite(self):
        self.sbuf[0] = self.part[self.ring.opp].astype(BF16)
        self.over = self.send(0, self.low, True), self.send(0, self.high, False)

    def onward(self):
        for c, slot, rows, j, right in (
            (self.over[0], 1, self.low, self.ring.right, True),
            (self.over[1], 2, self.high, self.ring.left, False),
        ):
            c.wait_recv()
            self.sbuf[slot, rows] = (self.part[j, rows] + self.rbuf[0, rows].astype(F32)).astype(BF16)
            self.send(slot, rows, right)

    def end(self):
        for c in self.all:
            if all(c is not o for o in self.over):
                c.wait_recv()
        total = self.part[self.ring.y] + self.rbuf[1].astype(F32) + self.rbuf[2].astype(F32)
        for c in self.all:
            c.wait_send()
        return total


def pass_through(ring, buf, sc, lo, hi, ss, rs, use, early=nothing, late=nothing, beside=nothing):
    first = gather_start(ring, buf, lo, hi, ss, rs)
    early()
    use(ring.y)
    last = gather_forward(ring, buf, lo, hi, ss, rs, first)

    def near(i, carry):
        use(lax.rem(ring.y + 1 + 2 * i, NY))
        return carry

    lax.fori_loop(0, 2, near, 0)
    sc.near(True)
    sc.near(False)
    late()
    for c in last:
        c.wait_recv()
    use(ring.opp)
    sc.opposite()
    for c in first + last:
        c.wait_send()
    sc.onward()
    beside()
    return sc.end()


def swap_all(d, sbuf, rbuf, ss, rs):
    def copy(k):
        to = lax.rem(d + k, NDP)
        return pltpu.make_async_remote_copy(
            src_ref=sbuf.at[to],
            dst_ref=rbuf.at[d],
            send_sem=ss.at[k],
            recv_sem=rs.at[k],
            device_id={"dp": to},
            device_id_type=MESH,
        )

    def start(k, carry):
        copy(k).start()
        return carry

    lax.fori_loop(1, NDP, start, 0)
    rbuf[d] = sbuf[d]

    def finish(k, carry):
        copy(k).wait()
        return carry

    lax.fori_loop(1, NDP, finish, 0)


class Place:
    def __init__(self):
        d = lax.axis_index("dp")
        self.d = d
        self.z, self.x, self.c = lax.div(d, 8), lax.rem(lax.div(d, 2), 4), lax.rem(d, 2)

    def at(self, z=None, x=None, c=None):
        z, x, c = (m if v is None else v for v, m in ((z, self.z), (x, self.x), (c, self.c)))
        return {"dp": (z * 4 + x) * 2 + c}


def push(src, dst, ssem, rsem, to):
    c = pltpu.make_async_remote_copy(
        src_ref=src, dst_ref=dst, send_sem=ssem, recv_sem=rsem, device_id=to, device_id_type=MESH
    )
    c.start()
    return c


def across(v, sel):
    hi = v.astype(BF16)
    rest = v.astype(F32) - hi.astype(F32)
    mid = rest.astype(BF16)
    return mm(hi, sel) + mm(mid, sel) + mm((rest - mid.astype(F32)).astype(BF16), sel)


class Weights:
    def __init__(self, R, place, ring):
        self.R, self.p, self.ring = R, place, ring
        self.own = (R.wqkv0, R.wup, R.w_out, R.w_down, R.wqkv1)
        self.got = (R.wqkv0g, R.wupg, R.woutg, R.wdowng, R.wqkv1g)
        self.done, self.now = [], {}
        self.next = 0

    def push(self, src, dst, to):
        i = self.next
        self.next += 1
        return push(src, dst, self.R.wss.at[i], self.R.wrs.at[i], to)

    def cut(self):
        R, y = self.R, self.ring.y
        sel = one_hot(iota((D, HW), 0) == iota((D, HW), 1) + HW * y)
        for t in range(3):
            at = pl.ds(t * HW, HW)
            R.wqkv0[:, at] = mm(R.w_qkv[0, :, t * D : (t + 1) * D], sel).astype(BF16)
            R.wqkv1[:, at] = mm(R.w_qkv[1, :, t * D : (t + 1) * D], sel).astype(BF16)
        R.wup[...] = R.w_up[:, pl.ds(pl.multiple_of(D * y, D), D)]
        for t in range(2):
            R.qvb[2 * t : 2 * t + 2] = across(R.qv_bias[:, t * D : (t + 1) * D], sel)

    def a_along_x(self, n):
        p, buf = self.p, self.got[n]
        self.now[n] = [
            self.push(self.own[n], buf.at[p.z, p.x, p.c], p.at(x=lax.rem(p.x + k, 4))) for k in RING4
        ]
        buf[p.z, p.x, p.c] = self.own[n][...]

    def wait(self, n):
        for c in self.now[n]:
            c.wait_recv()
        self.done += self.now[n]

    def a_along_z(self, n):
        p, buf = self.p, self.got[n]
        self.wait(n)
        row = buf.at[p.z, :, p.c]
        self.now[n] = [self.push(row, row, p.at(z=lax.rem(p.z + k, 4))) for k in RING4]

    def a_along_core(self, n):
        p = self.p
        self.wait(n)
        half = self.got[n].at[:, :, p.c]
        self.now[n] = [self.push(half, half, p.at(c=1 - p.c))]

    def b_copy(self, n, k):
        p, R = self.p, self.R
        return pltpu.make_async_remote_copy(
            src_ref=self.own[n],
            dst_ref=self.got[n].at[p.x, p.c],
            send_sem=R.bss.at[n - 2, k],
            recv_sem=R.bss.at[n - 2, 0],
            device_id=p.at(z=lax.rem(p.z + k, 4)),
            device_id_type=MESH,
        )

    def b_along_z(self, n):
        @pl.when(self.p.z == self.ring.y)
        def _():
            for k in RING4:
                self.b_copy(n, k).start()
            self.got[n][self.p.x, self.p.c] = self.own[n][...]

    def b_along_x(self, n):
        p = self.p

        @pl.when(p.z != self.ring.y)
        def _():
            self.b_copy(n, 1).wait_recv()

        own = self.got[n].at[p.x, p.c]
        self.now[n] = [self.push(own, own, p.at(x=lax.rem(p.x + k, 4))) for k in RING4]

    def b_along_core(self, n):
        p = self.p
        self.wait(n)
        half = self.got[n].at[:, p.c]
        self.now[n] = [self.push(half, half, p.at(c=1 - p.c))]

    def sent(self):
        for c in self.done:
            c.wait_send()

        @pl.when(self.p.z == self.ring.y)
        def _():
            for n in (2, 3):
                for k in RING4:
                    self.b_copy(n, k).wait_send()

    def lay(self, n):
        R = self.R
        self.wait(n)

        def one(j, carry):
            rows = pl.ds(pl.multiple_of(192 * j, 192), 192)
            v = self.got[n][j].astype(F32)
            if n in (0, 4):
                v = v.reshape(192, 3 * HW).astype(BF16)
                for t in range(3):
                    R.wqkv[n // 4, t, rows] = v[:, t * HW : (t + 1) * HW]
            elif n == 1:
                R.up[rows] = v.reshape(192, D).astype(BF16)
            elif n == 2:
                for i in range(2):
                    R.wout[i, pl.ds(pl.multiple_of(48 * j, 48), 48)] = v[:, i].reshape(48, D).astype(BF16)
            else:
                R.down[rows] = v.reshape(192, D).astype(BF16)
            return carry

        lax.fori_loop(0, 4, one, 0)


def head_mask(h, dtype):
    lane = lax.broadcasted_iota(jnp.int32, (1, HW), 1)
    return ((lane >= 64 * h) & (lane < 64 * (h + 1))).astype(dtype)


def keep_grad(ref, first, grad):
    depth = ref.shape[3]
    count = grad.shape[0] // (4 * depth)
    low = grad.astype(BF16)
    for c in range(2):
        half = low[:, c * HALF : (c + 1) * HALF].reshape(count, 4, depth, HALF)
        ref[c, first : first + count] = half


def flat(ref):
    v = ref[...]
    return v.reshape(v.shape[0] * v.shape[1], v.shape[2])


def attn_forward(R, ring, i, x, gain, shift, w=None):
    nbuf, q, k, v, o, st = R.n[2 * i], R.q[i], R.k[i], R.v[i], R.o[i], R.st[i]
    wqkv, wout, qvb, part, vm = R.wqkv, R.wout, R.qvb, R.part, R.vm
    nbuf[ring.y] = ln_forward(x, gain, shift).astype(BF16)

    def project(j):
        nj = nbuf[j]
        q[j] = ((mm(nj, wqkv[i, 0]) + qvb[i : i + 1]).astype(BF16).astype(F32) * 0.125).astype(BF16)
        k[j] = mm(nj, wqkv[i, 1]).astype(BF16)
        v[j] = (mm(nj, wqkv[i, 2]) + qvb[2 + i : 3 + i]).astype(BF16)

    def early():
        w.a_along_z(0)
        w.b_along_x(2)
        w.a_along_x(1)
        w.a_along_core(0)
        w.a_along_z(1)
        w.b_along_z(3)
        w.lay(0)

    gather_blocks(ring, nbuf, LO, HI, R.ssem.at[2 * i], R.rsem.at[2 * i], project, nothing if w is None else early)
    if w is not None:
        w.b_along_core(2)
    v_all = flat(v)
    for h in range(HEADS_DEV):
        vm[h] = v_all * head_mask(h, BF16)
    k_all = flat(k)

    def rows(b):
        qb = q[b]
        acc = jnp.zeros((ROWS, HW), F32)
        stats = jnp.zeros((ROWS, 128), F32)
        lane = lax.broadcasted_iota(jnp.int32, (ROWS, 128), 1)
        for h in range(HEADS_DEV):
            s = mm(qb * head_mask(h, BF16), k_all, NT)
            top = jnp.max(s, axis=-1, keepdims=True)
            e = jnp.exp(s - top)
            tot = jnp.sum(e, axis=-1, keepdims=True)
            acc = acc + mm(e.astype(BF16), vm[h]) * (1.0 / tot)
            stats = jnp.where(lane == h, top + jnp.log(tot), stats)
        o[b] = acc
        st[b] = stats
        part[b] = mm(acc.astype(BF16), wout[i])

    if w is not None:
        w.lay(2)
    sc = Scatter(ring, part, LO, HI, R.sb, R.rb, R.ssem.at[2 * i + 1], R.rsem.at[2 * i + 1])
    rows(ring.opp)
    sc.opposite()

    def near(t, carry):
        rows(lax.rem(ring.y + 1 + 2 * t, NY))
        return carry

    lax.fori_loop(0, 2, near, 0)
    sc.near(True)
    sc.near(False)
    if w is not None:
        w.b_along_x(3)
        w.a_along_core(1)
        w.a_along_x(4)
    sc.onward()
    rows(ring.y)
    if w is not None:
        w.b_along_core(3)
        w.a_along_z(4)
    total = sc.end()
    if w is not None:
        w.lay(1)
        w.lay(3)
    return x + total + R.out_bias[i : i + 1]


EARLY, LATE, BEFORE, MIDDLE, AFTER, WEIGHTS, BESIDE, END = range(8)


def attn_backward(R, ring, i, x, gain, grad, slot, hooks):
    nbuf, q, k, v, o, st = R.n[2 * i], R.q[i], R.k[i], R.v[i], R.o[i], R.st[i]
    wqkv, wout, part = R.wqkv, R.wout, R.part
    gb, go, gm, qm, gq, gk, gv, dq = R.gb[slot // 2 % 2], R.go, R.vm, R.qm, R.gq, R.gk, R.gv, R.dq
    low = grad.astype(BF16)
    gb[ring.y] = low
    R.small[pl.ds(8 + i, 1)] = jnp.sum(low.astype(F32), axis=0, keepdims=True)

    def project(j):
        g = mm(gb[j], wout[i], NT).astype(BF16)
        go[j] = g
        prod = g.astype(F32) * o[j]
        stats = st[j]
        lane = lax.broadcasted_iota(jnp.int32, (ROWS, 128), 1)
        for h in range(HEADS_DEV):
            inner = jnp.sum(prod * head_mask(h, F32), axis=-1, keepdims=True)
            stats = jnp.where(lane == 4 + h, inner, stats)
        st[j] = stats

    at = hooks.get
    gather_blocks(
        ring, gb, LO, HI, R.ssem.at[slot], R.rsem.at[slot], project, at(EARLY, nothing), at(LATE, nothing)
    )
    at(BEFORE, nothing)()
    go_all, q_all = flat(go), flat(q)
    for h in range(HEADS_DEV):
        gm[h] = go_all * head_mask(h, BF16)
        qm[h] = q_all * head_mask(h, BF16)
    stats_t = jnp.transpose(flat(st))
    R.stt[...] = stats_t[0:8]
    dq[...] = jnp.zeros((NY * ROWS, HW), F32)

    def keys(b, carry):
        kb, vb = k[b], v[b]
        dk = jnp.zeros((ROWS, HW), F32)
        dv = jnp.zeros((ROWS, HW), F32)
        for h in range(HEADS_DEV):
            kh = kb * head_mask(h, BF16)
            p = jnp.exp(mm(kh, qm[h], NT) - R.stt[h : h + 1])
            dp = mm(vb, gm[h], NT)
            ds = (p * (dp - R.stt[4 + h : 5 + h])).astype(BF16)
            dv = dv + mm(p.astype(BF16), gm[h])
            dk = dk + mm(ds, qm[h])
            dq[...] += mm(ds, kh, TN)
        gk[b] = dk.astype(BF16)
        gv[b] = dv.astype(BF16)
        return carry

    lax.fori_loop(0, 2, keys, 0)
    at(MIDDLE, nothing)()
    lax.fori_loop(2, NY, keys, 0)
    at(AFTER, nothing)()
    gq[...] = (dq[...] * 0.125).astype(BF16).reshape(NY, ROWS, HW)

    def back(b):
        part[b] = mm(gq[b], wqkv[i, 0], NT) + mm(gk[b], wqkv[i, 1], NT) + mm(gv[b], wqkv[i, 2], NT)

    def weights():
        n_all, grads = flat(nbuf), R.g13[i]
        for t, g in enumerate((gq, gk, gv)):
            g_all = flat(g)
            keep_grad(grads, t, mm(g_all, n_all, TN))
            if t != 1:
                row = 12 + 2 * i + t // 2
                R.small[row : row + 1, 0:HW] = jnp.sum(g_all.astype(F32), axis=0, keepdims=True)
        keep_grad(grads, 3, mm(flat(o).astype(BF16), flat(gb), TN))

    if WEIGHTS in hooks:
        weights()
        hooks[WEIGHTS]()
    sc = Scatter(ring, part, LO, HI, R.sb, R.rb, R.ssem.at[slot + 1], R.rsem.at[slot + 1])
    back(ring.opp)
    sc.opposite()

    def near(t, carry):
        back(lax.rem(ring.y + 1 + 2 * t, NY))
        return carry

    lax.fori_loop(0, 2, near, 0)
    sc.near(True)
    sc.near(False)
    sc.onward()
    back(ring.y)
    if WEIGHTS not in hooks:
        weights()
    at(BESIDE, nothing)()
    total = sc.end()
    at(END, nothing)()
    dx, d_gain, d_shift = ln_backward(x, gain, total)
    R.small[pl.ds(2 * i, 1)] = d_gain
    R.small[pl.ds(4 + 2 * i, 1)] = d_shift
    return grad + dx


def across_rows(ref, n):
    return jnp.concatenate([ref[6 * n + j : 6 * n + j + 1] for j in range(6)], axis=1)


def feed_forward(R, ring, x, gain, shift, w):
    nbuf, u, a, part = R.n[1], R.u, R.a, R.part
    nbuf[ring.y] = ln_forward(x, gain, shift).astype(BF16)
    bias = across_rows(R.up_bias, 0)
    for y in range(1, NY):
        bias = jnp.where(ring.y == y, across_rows(R.up_bias, y), bias)

    def use(j):
        uj = mm(nbuf[j], R.up[...]) + bias
        act, slope = gelu_both(uj)
        u[j] = slope
        aj = act.astype(BF16)
        a[j] = aj
        part[j] = mm(aj, R.down[...])

    sc = Scatter(ring, part, LO, HI, R.sb, R.rb, R.ssem.at[5], R.rsem.at[5])
    core, lay = functools.partial(w.a_along_core, 4), functools.partial(w.lay, 4)
    total = pass_through(ring, nbuf, sc, LO, HI, R.ssem.at[4], R.rsem.at[4], use, late=core, beside=lay)
    return x + total + across_rows(R.down_bias, 0)


def feed_backward(R, ring, x, gain, grad, slot, hooks):
    nbuf, u, a, part, gb, gu = R.n[1], R.u, R.a, R.part, R.gb[slot // 2 % 2], R.gu
    low = grad.astype(BF16)
    gb[ring.y] = low
    R.small[10:11] = jnp.sum(low.astype(F32), axis=0, keepdims=True)

    def use(j):
        g = (mm(gb[j], R.down[...], NT) * u[j]).astype(BF16)
        gu[j] = g
        part[j] = mm(g, R.up[...], NT)

    at = hooks.get

    def beside():
        at(BEFORE, nothing)()
        n_all, g_all, a_all, gb_all = flat(nbuf), flat(gu), flat(a), flat(gb)
        keep_grad(R.g2, 0, mm(n_all, g_all, TN))
        keep_grad(R.g2, 2, mm(a_all, gb_all, TN))
        R.small[11:12] = jnp.sum(g_all.astype(F32), axis=0, keepdims=True)
        at(BESIDE, nothing)()

    sc = Scatter(ring, part, LO, HI, R.sb, R.rb, R.ssem.at[slot + 1], R.rsem.at[slot + 1])
    total = pass_through(
        ring,
        gb,
        sc,
        LO,
        HI,
        R.ssem.at[slot],
        R.rsem.at[slot],
        use,
        at(EARLY, nothing),
        at(LATE, nothing),
        beside,
    )
    at(END, nothing)()
    dx, d_gain, d_shift = ln_backward(x, gain, total)
    R.small[1:2] = d_gain
    R.small[5:6] = d_shift
    return grad + dx


def iota(shape, dim):
    return lax.broadcasted_iota(jnp.int32, shape, dim)


def slot_ids(shape, dim):
    r = iota(shape, dim)
    e, t = r >> 3, r & 7
    z = jnp.where(t < 4, e * 4 + t, -1)
    g = jnp.where(t >= 4, e * 4 + t - 4, -1)
    return z.astype(F32), g.astype(F32)


def one_hot(cond):
    return jnp.where(cond, 1.0, 0.0).astype(BF16)


def mixture(R, ring, d, x, gain, shift):
    low = ln_forward(x, gain, shift).astype(BF16)
    cot = R.cot[...].astype(F32)
    logits = mm(low, R.router[...], NT)

    idr, prr = R.ids[...], R.pri[...]
    digits = jnp.concatenate([idr, prr >> 8, prr & 255], axis=0).astype(F32).astype(BF16)
    turned = mm(one_hot(iota((ROWS, ROWS), 0) == iota((ROWS, ROWS), 1)), digits, NT)
    idc = turned[:, 0:2].astype(jnp.int32)
    prc = (turned[:, 2:4] * 256.0 + turned[:, 4:6]).astype(jnp.int32)
    key_c, key_r = [], []
    for k in range(2):
        key_c.append(prc[:, k : k + 1] * (2 * ROWS) + 2 * iota((ROWS, 1), 0) + k)
        key_r.append(prr[k : k + 1, :] * (2 * ROWS) + 2 * iota((1, ROWS), 1) + k)
    rank_c = [jnp.zeros((ROWS, 1), F32) for _ in range(2)]
    rank_r = [jnp.zeros((1, ROWS), F32) for _ in range(2)]
    for k in range(2):
        for j in range(2):
            same = idc[:, k : k + 1] == idr[j : j + 1, :]
            before = key_r[j] < key_c[k]
            after = key_c[k] < key_r[j]
            rank_c[k] = rank_c[k] + jnp.sum(jnp.where(same & before, 1.0, 0.0), axis=1, keepdims=True)
            rank_r[j] = rank_r[j] + jnp.sum(jnp.where(same & after, 1.0, 0.0), axis=0, keepdims=True)
    kept = [jnp.where(r < CAP, 1.0, 0.0) for r in rank_c]
    slot_c = [jnp.where(rank_c[k] < CAP, idc[:, k : k + 1].astype(F32) * CAP + rank_c[k], 1000.0) for k in range(2)]
    slot_r = [jnp.where(rank_r[k] < CAP, idr[k : k + 1, :].astype(F32) * CAP + rank_r[k], 1000.0) for k in range(2)]

    picks = [jnp.where(iota((ROWS, EXPERTS), 1) == idc[:, k : k + 1], 1.0, 0.0) for k in range(2)]
    chosen = [jnp.sum(logits * p, axis=-1, keepdims=True) for p in picks]
    top = jnp.maximum(chosen[0], chosen[1])
    ex = [jnp.exp(c - top) for c in chosen]
    gates = [e / (ex[0] + ex[1]) for e in ex]

    zid, gid = slot_ids((8 * EXPERTS, ROWS), 0)
    rows = mm(one_hot((zid == slot_r[0]) | (zid == slot_r[1])), low)
    for k in range(2):
        rows = rows + mm(one_hot(gid == slot_r[k]), (gates[k] * cot).astype(BF16))
    R.ds[...] = rows.reshape(EXPERTS, 8, D).astype(BF16)
    swap_all(d, R.ds, R.dr.at[0], R.dssem.at[0], R.drsem.at[0])

    n_slots = CAP * NDP
    back = iota((2 * n_slots, 2 * n_slots), 0)
    col = iota((2 * n_slots, 2 * n_slots), 1)
    s = back & (n_slots - 1)
    src = (s >> 2) * 8 + (s & 3) + jnp.where(back >= n_slots, 4, 0)
    sort = one_hot(src == col)
    arrived = R.dr[0].astype(F32).reshape(2 * n_slots, D).astype(BF16)
    moe = R.moe
    moe[ring.y] = mm(sort, arrived).astype(BF16)
    part = R.mpart

    def use(j):
        z, gy = moe[j, 0:n_slots], moe[j, n_slots : 2 * n_slots]
        c = mm(z, R.eu[...]) + R.e_up_bias[...].astype(F32)
        act, slope = gelu_both(c)
        b = act.astype(BF16)
        R.eb[j] = b
        gc = (slope * mm(gy, R.ed[...], NT)).astype(BF16)
        R.egc[j] = gc
        part[j, 0:n_slots] = mm(b, R.ed[...])
        part[j, n_slots : 2 * n_slots] = mm(gc, R.eu[...], NT)

    def beside():
        z_all = moe[:, 0:n_slots].reshape(NY * n_slots, D)
        gy_all = moe[:, n_slots : 2 * n_slots].reshape(NY * n_slots, D)
        b_all, gc_all = flat(R.eb), flat(R.egc)
        R.geu[...] = mm(z_all, gc_all, TN).astype(BF16)
        R.ged[...] = mm(b_all, gy_all, TN).astype(BF16)
        R.g_eub[...] = jnp.sum(gc_all.astype(F32), axis=0, keepdims=True)
        R.g_edb[...] = jnp.sum(gy_all.astype(F32), axis=0, keepdims=True)

    sc = Scatter(ring, part, n_slots, n_slots, R.msb, R.mrb, R.ssem.at[13], R.rsem.at[13])
    total = pass_through(ring, moe, sc, n_slots, n_slots, R.ssem.at[12], R.rsem.at[12], use, beside=beside)
    is_y = jnp.where(iota((2 * n_slots, 1), 0) < n_slots, 1.0, 0.0)
    total = (total + is_y * R.e_down_bias[...]).astype(BF16)
    unsort = one_hot((col & (n_slots - 1)) * 2 - (col & 3) + jnp.where(col >= n_slots, 4, 0) == back)
    R.ds[...] = mm(unsort, total).reshape(NDP, 8, D).astype(BF16)
    swap_all(d, R.ds, R.dr.at[1], R.dssem.at[1], R.drsem.at[1])
    came = R.dr[1].astype(F32).reshape(8 * EXPERTS, D).astype(BF16)

    zid, gid = slot_ids((ROWS, 8 * EXPERTS), 1)
    result = x
    grad_gate = []
    for k in range(2):
        taken = mm(one_hot(zid == slot_c[k]), came)
        result = result + (gates[k] * kept[k]) * taken
        grad_gate.append(kept[k] * jnp.sum(taken * cot, axis=-1, keepdims=True))
    R.result[...] = result
    inner = gates[0] * grad_gate[0] + gates[1] * grad_gate[1]
    gl = sum(gates[k] * (grad_gate[k] - inner) * picks[k] for k in range(2))
    gl_hi = gl.astype(BF16)
    rest = gl - gl_hi.astype(F32)
    gl_mid = rest.astype(BF16)
    gl_lo = (rest - gl_mid.astype(F32)).astype(BF16)
    grad_low = mm(one_hot((gid == slot_c[0]) | (gid == slot_c[1])), came)
    g_router = jnp.zeros((EXPERTS, D), F32)
    for piece in (gl_hi, gl_mid, gl_lo):
        grad_low = grad_low + mm(piece, R.router[...])
        g_router = g_router + mm(piece, low, TN)
    R.small[16 : 16 + EXPERTS] = g_router
    dx, d_gain, d_shift = ln_backward(x, gain, grad_low)
    R.small[3:4] = d_gain
    R.small[7:8] = d_shift
    return cot + dx


ORDERS = ("zxy", "xyz", "yzx")


def sum_scratch(r, a):
    low, sems = (lambda *sh: pltpu.VMEM(sh, BF16)), pltpu.SemaphoreType.DMA
    b = r - a
    return dict(
        r=low(4, 4, r, HALF),
        xa=low(3, 4, a, HALF),
        zb=low(3, 4, b, HALF),
        ba=low(4, a, HALF),
        bb=low(4, b, HALF),
        za=low(3, a, HALF),
        xb=low(3, b, HALF),
        o=low(r, HALF),
        ss=sems((70,)),
        rs=sems((70,)),
        local=sems,
    )


def wait_all(copies):
    for c in copies:
        c.wait_recv()


def add_up(first, *rest):
    total = first.astype(F32)
    for r in rest:
        total = total + r.astype(F32)
    return total.astype(BF16)


class Pushes:
    def __init__(self, place, ring, ss, rs):
        self.p, self.ring = place, ring
        self.ss, self.rs = ss, rs
        self.all = []
        self.other = place.at(c=1 - place.c)
        self.me = dict(x=place.x, y=ring.y, z=place.z)

    def push(self, src, dst, to):
        i = len(self.all)
        c = push(src, dst, self.ss.at[i], self.rs.at[i], to)
        self.all.append(c)
        return c

    def pos(self, axis, k=0):
        return lax.rem(self.me[axis] + k, 4)

    def peer(self, axis, k):
        at = self.pos(axis, k)
        return {"seq": at} if axis == "y" else self.p.at(**{axis: at})

    def end(self):
        for c in self.all:
            c.wait_send()


class Sum(Pushes):
    def __init__(self, R, place, ring, grad, full, scr):
        s = types.SimpleNamespace(**scr)
        super().__init__(place, ring, s.ss, s.rs)
        self.s, self.grad, self.full = s, grad, full
        self.rows = grad.shape[3]
        self.a = s.ba.shape[1]
        self.third = self.rows // 3

    def halves(self):
        self.halved = self.push(self.grad.at[1 - self.p.c], self.s.r, self.other)
        self.core = []

    def first_axis(self):
        s, p, a = self.s, self.p, self.a
        self.halved.wait_recv()

        def add(z, carry):
            s.r[z] = add_up(self.grad[p.c, z], s.r[z])
            return carry

        lax.fori_loop(0, 4, add, 0)
        top, rest = pl.ds(0, a), pl.ds(a, self.rows - a)
        self.na = [self.push(s.r.at[:, self.pos("x", k), top], s.xa.at[k - 1], self.peer("x", k)) for k in RING4]
        self.nb = [self.push(s.r.at[self.pos("z", k), :, rest], s.zb.at[k - 1], self.peer("z", k)) for k in RING4]

    def second_axis(self):
        s, p, a = self.s, self.p, self.a
        wait_all(self.na)
        s.ba[...] = add_up(s.r[:, p.x, 0:a], *(s.xa[k] for k in range(3)))
        self.na = [self.push(s.ba.at[self.pos("z", k)], s.za.at[k - 1], self.peer("z", k)) for k in RING4]
        wait_all(self.nb)
        s.bb[...] = add_up(s.r[p.z, :, a : self.rows], *(s.zb[k] for k in range(3)))
        self.nb = [self.push(s.bb.at[self.pos("x", k)], s.xb.at[k - 1], self.peer("x", k)) for k in RING4]

    def view(self, t, index):
        every = pl.ds(0, 4)
        y, z, x = (index.get(n, every) for n in "yzx")
        return self.full.at[self.p.c, y, z, x, pl.ds(self.third * t, self.third)]

    def own(self):
        s, p, a, me = self.s, self.p, self.a, self.me
        wait_all(self.na)
        s.o[0:a] = add_up(s.ba[p.z], *(s.za[k] for k in range(3)))
        wait_all(self.nb)
        s.o[a : self.rows] = add_up(s.bb[p.x], *(s.xb[k] for k in range(3)))
        self.mine = pltpu.make_async_copy(s.o, self.full.at[p.c, me["y"], p.z, p.x], s.local)
        self.mine.start()
        self.one = [
            [
                self.push(s.o.at[pl.ds(self.third * t, self.third)], self.view(t, me), self.peer(order[0], k))
                for k in RING4
            ]
            for t, order in enumerate(ORDERS)
        ]

    def without(self, *axes):
        return {n: v for n, v in self.me.items() if n not in axes}

    def start(self, t, index, a, axis):
        low, high = (self.view(t, {**index, a: pl.ds(2 * h, 2)}) for h in range(2))
        right, left = self.peer(axis, 1), self.peer(axis, 3)
        a0 = self.push(low, low, right)
        b0 = self.push(high, high, left)
        return a0, b0, self.push(high, high, right), self.push(low, low, left)

    def forward(self, t, index, a, axis, copies):
        a0, b0, a1, b1 = copies
        a0.wait_recv()
        low = self.view(t, {**index, axis: self.pos(axis, 3), a: pl.ds(0, 2)})
        a2 = self.push(low, low, self.peer(axis, 1))
        b0.wait_recv()
        high = self.view(t, {**index, axis: self.pos(axis, 1), a: pl.ds(2, 2)})
        b2 = self.push(high, high, self.peer(axis, 3))
        wait_all((a1, b1))
        return a2, b2

    def to_core(self, t, index):
        v = self.view(t, index)
        self.core.append(self.push(v, v, self.other))

    def two(self):
        self.mine.wait()
        self.hop = []
        for t, (a, b, _) in enumerate(ORDERS):
            wait_all(self.one[t])
            self.hop.append(self.start(t, self.without(a), a, b))

    def two_forward(self):
        self.last = [self.forward(t, self.without(a), a, b, self.hop[t]) for t, (a, b, _) in enumerate(ORDERS)]

    def three(self, *thirds):
        for t in thirds:
            a, b, c = ORDERS[t]
            wait_all(self.last[t])
            self.hop[t] = self.start(t, self.without(a, b), a, c)
        for t in thirds:
            a, b, c = ORDERS[t]
            self.to_core(t, self.without(a, b))

    def three_forward(self, *thirds):
        for t in thirds:
            a, b, c = ORDERS[t]
            self.last[t] = self.forward(t, self.without(a, b), a, c, self.hop[t])
        for t in thirds:
            c = ORDERS[t][2]
            self.to_core(t, {c: self.pos(c, 1)})
            self.to_core(t, {c: self.pos(c, 3)})

    def three_end(self, *thirds):
        for t in thirds:
            c = ORDERS[t][2]
            wait_all(self.last[t])
            self.to_core(t, {c: self.pos(c, 2)})

    def end(self):
        wait_all(self.core)
        super().end()


class Small(Pushes):
    def __init__(self, R, place, ring):
        super().__init__(place, ring, R.tss, R.trs)
        self.R = R

    def halves(self):
        R = self.R
        for c in range(2):
            R.s0[c] = R.small[:, c * HALF : (c + 1) * HALF].astype(BF16)
        self.now = [self.push(R.s0.at[1 - self.p.c], R.sr, self.other)]

    def along_x(self):
        R = self.R
        wait_all(self.now)
        R.s1[...] = add_up(R.s0[self.p.c], R.sr[...])
        self.now = [self.push(R.s1, R.sx.at[k - 1], self.peer("x", k)) for k in RING4]

    def along_z(self):
        R = self.R
        wait_all(self.now)
        R.s2[...] = add_up(R.s1[...], *(R.sx[k] for k in range(3)))
        self.now = [self.push(R.s2, R.sz.at[k - 1], self.peer("z", k)) for k in RING4]

    def along_y(self):
        R = self.R
        wait_all(self.now)
        own = R.fs.at[self.p.c, self.ring.y]
        own[...] = add_up(R.s2[...], *(R.sz[k] for k in range(3)))
        self.now = [self.push(own, own, self.peer("y", k)) for k in RING4]

    def to_core(self):
        half = self.R.fs.at[self.p.c]
        wait_all(self.now)
        self.now = [self.push(half, half, self.other)]

    def end(self):
        wait_all(self.now)
        super().end()


IN = ("tok", "cot", "gain", "shift", "w_qkv", "qv_bias", "w_out", "out_bias", "w_up", "up_bias", "w_down", "down_bias")
IN = IN + ("router", "e_up", "e_up_bias", "e_down", "e_down_bias", "ids", "pri")


def outputs():
    return dict(
        result=((ROWS, D), F32),
        d_tok=((ROWS, D), F32),
        g_eub=((1, D), F32),
        g_edb=((1, D), F32),
        fs=((2, 4, 48, HALF), BF16),
        g_eup=((D, D), BF16),
        g_edown=((D, D), BF16),
        f13=((2, 2, 4, 4, 4, 48, HALF), BF16),
        f2=((2, 4, 4, 4, 96, HALF), BF16),
    )


def scratch():
    blk, att = (NY, ROWS, D), (NY, ROWS, HW)
    low, wide, sems = (lambda *sh: pltpu.VMEM(sh, BF16)), (lambda *sh: pltpu.VMEM(sh, F32)), pltpu.SemaphoreType.DMA
    n_slots = CAP * NDP
    return dict(
        n=[low(*blk) for _ in range(3)],
        q=[low(*att) for _ in range(2)],
        k=[low(*att) for _ in range(2)],
        v=[low(*att) for _ in range(2)],
        o=[wide(*att) for _ in range(2)],
        st=[wide(NY, ROWS, 128) for _ in range(2)],
        gb=[low(*blk) for _ in range(2)],
        go=low(*att),
        gq=low(*att),
        gk=low(*att),
        gv=low(*att),
        vm=low(HEADS_DEV, NY * ROWS, HW),
        qm=low(HEADS_DEV, NY * ROWS, HW),
        dq=wide(NY * ROWS, HW),
        stt=wide(8, NY * ROWS),
        u=wide(*blk),
        a=low(*blk),
        gu=low(*blk),
        moe=low(NY, 2 * n_slots, D),
        mpart=wide(NY, 2 * n_slots, D),
        msb=low(3, 2 * n_slots, D),
        mrb=low(3, 2 * n_slots, D),
        eb=low(NY, n_slots, D),
        egc=low(NY, n_slots, D),
        ds=low(EXPERTS, 8, D),
        dr=low(2, EXPERTS, 8, D),
        wqkv0g=low(4, 4, 2, 24, 3 * HW),
        wqkv1g=low(4, 4, 2, 24, 3 * HW),
        wupg=low(4, 4, 2, 24, D),
        wqkv0=low(24, 3 * HW),
        wqkv1=low(24, 3 * HW),
        wup=low(24, D),
        woutg=low(4, 2, 2, 24, D),
        wdowng=low(4, 2, 96, D),
        qvb=wide(4, HW),
        wqkv=low(2, 3, D, HW),
        wout=low(2, HW, D),
        up=low(D, D),
        down=low(D, D),
        eu=low(D, D),
        ed=low(D, D),
        geu=low(D, D),
        ged=low(D, D),
        own=sems((4,)),
        xs=wide(4, ROWS, D),
        gs=wide(ROWS, D),
        small=wide(48, D),
        g13=[low(2, 4, 4, 48, HALF) for _ in range(2)],
        g2=low(2, 4, 4, 96, HALF),
        sums=[sum_scratch(r, a) for r, a in ((48, 32), (96, 48), (48, 16))],
        s0=low(2, 48, HALF),
        sr=low(48, HALF),
        s1=low(48, HALF),
        sx=low(3, 48, HALF),
        s2=low(48, HALF),
        sz=low(3, 48, HALF),
        ssem=sems((14, 6)),
        rsem=sems((14, 6)),
        dssem=sems((2, NDP)),
        drsem=sems((2, NDP)),
        wss=sems((29,)),
        wrs=sems((29,)),
        bss=sems((2, 4)),
        tss=sems((11,)),
        trs=sems((11,)),
    )


def kernel(*refs):
    n_in, n_out = len(IN), len(outputs())
    R = types.SimpleNamespace(**dict(zip(IN + tuple(outputs()), refs)), **refs[n_in + n_out])
    R.sb = R.msb.at[:, pl.ds(0, ROWS)]
    R.rb = R.mrb.at[:, pl.ds(0, ROWS)]
    R.part = R.mpart.at[:, pl.ds(0, ROWS)]
    ring, place = Ring(), Place()
    d = place.d
    barrier = pltpu.get_barrier_semaphore()
    for k in RING4:
        pl.semaphore_signal(barrier, inc=1, device_id={"seq": lax.rem(ring.y + k, NY)}, device_id_type=MESH)

    def greet(k, carry):
        pl.semaphore_signal(barrier, inc=1, device_id={"dp": lax.rem(d + k, NDP)}, device_id_type=MESH)
        return carry

    lax.fori_loop(1, NDP, greet, 0)
    R.small[...] = jnp.zeros((48, D), F32)
    fetched = [
        pltpu.make_async_copy(src, dst, R.own.at[i]) for i, (src, dst) in enumerate(((R.e_up, R.eu), (R.e_down, R.ed)))
    ]
    stored = [
        pltpu.make_async_copy(src, dst, R.own.at[2 + i])
        for i, (src, dst) in enumerate(((R.geu, R.g_eup), (R.ged, R.g_edown)))
    ]
    for c in fetched:
        c.start()
    w = Weights(R, place, ring)
    w.cut()
    pl.semaphore_wait(barrier, NDP + 2)

    gain = lambda j: R.gain[j : j + 1]
    shift = lambda j: R.shift[j : j + 1]
    xs, gs = R.xs, R.gs
    xs[0] = R.tok[...].astype(F32)
    w.b_along_z(2)
    w.a_along_x(0)
    xs[1] = attn_forward(R, ring, 0, xs[0], gain(0), shift(0), w)
    xs[2] = feed_forward(R, ring, xs[1], gain(1), shift(1), w)
    w.sent()
    xs[3] = attn_forward(R, ring, 1, xs[2], gain(2), shift(2))
    for c in fetched:
        c.wait()
    gs[...] = mixture(R, ring, d, xs[3], gain(3), shift(3))
    for c in stored:
        c.start()

    a1 = Sum(R, place, ring, R.g13[1], R.f13.at[1], R.sums[0])
    ff = Sum(R, place, ring, R.g2, R.f2, R.sums[1])
    a0 = Sum(R, place, ring, R.g13[0], R.f13.at[0], R.sums[2])
    small = Small(R, place, ring)

    def steps(*fs):
        def run():
            for f in fs:
                f()

        return run

    part = functools.partial
    gs[...] = attn_backward(R, ring, 1, xs[2], gain(2), gs[...], 6, {BESIDE: a1.halves, END: a1.first_axis})
    gs[...] = feed_backward(
        R,
        ring,
        xs[1],
        gain(1),
        gs[...],
        8,
        {
            LATE: a1.second_axis,
            BEFORE: a1.own,
            BESIDE: steps(ff.halves, a1.two),
            END: steps(ff.first_axis, a1.two_forward),
        },
    )
    R.d_tok[...] = attn_backward(
        R,
        ring,
        0,
        xs[0],
        gain(0),
        gs[...],
        10,
        {
            BEFORE: steps(ff.second_axis, part(a1.three, 0, 1, 2)),
            MIDDLE: ff.own,
            AFTER: steps(ff.two, part(a1.three_forward, 0, 1, 2)),
            WEIGHTS: a0.halves,
            BESIDE: steps(ff.two_forward, a0.first_axis, part(a1.three_end, 0, 1, 2)),
            END: steps(a0.second_axis, part(ff.three, 0, 1, 2)),
        },
    )
    small.halves()
    a0.own()
    small.along_x()
    a0.two()
    small.along_z()
    a0.two_forward()
    small.along_y()
    a0.three(0, 1, 2)
    ff.three_forward(0, 1, 2)
    small.to_core()
    a0.three_forward(0, 1, 2)
    ff.three_end(0, 1, 2)
    a0.three_end(0, 1, 2)
    for c in stored:
        c.wait()
    for s in (a1, ff, a0, small):
        s.end()


def layers(ins):
    vmem, hbm = pl.BlockSpec(memory_space=pltpu.VMEM), pl.BlockSpec(memory_space=pl.ANY)
    out = outputs()
    return dict(
        zip(
            out,
            pl.pallas_call(
                kernel,
                out_shape=[jax.ShapeDtypeStruct(*sh) for sh in out.values()],
                in_specs=[hbm if n in ("e_up", "e_down") else vmem for n in IN],
                out_specs=[vmem] * (len(out) - 4) + [hbm] * 4,
                scratch_shapes=[scratch()],
                compiler_params=pltpu.CompilerParams(
                    collective_id=0, has_side_effects=True, vmem_limit_bytes=62 * 2**20
                ),
                name="layers",
            )(*ins),
        )
    )


def spread(o):
    def body(*refs):
        f_qkv, f_out, f_up, f_down, geu, ged, res, tok, fs, edb, eub = refs[:11]
        qkv, out, up, down, geu_o, ged_o, res_o, tok_o = refs[11:19]
        gain, shift, outb, downb, upb, qvb, router, edb_o, eub_o = refs[19:]
        s = pl.program_id(0)

        @pl.when(s < 12)
        def _():
            qkv[0] = jnp.transpose(f_qkv[0, 0, :, 0].reshape(D, HALF).astype(F32))

        out[0] = f_out[0, 0, 0, 0].reshape(HW, HALF).astype(F32)
        for c in range(2):
            at = pl.ds(c * HALF, HALF)
            up[:, at] = f_up[c, 0, 0].reshape(HW, HALF).astype(F32)
            down[:, at] = f_down[c, 0, 0].reshape(HW, HALF).astype(F32)
        geu_o[...] = geu[...].astype(F32)
        ged_o[...] = ged[...].astype(F32)
        res_o[...] = res[...]
        tok_o[...] = tok[...]

        @pl.when(s == 0)
        def _():
            by_y = [jnp.concatenate([fs[0, y], fs[1, y]], axis=1).astype(F32) for y in range(NY)]
            total = by_y[0] + by_y[1] + by_y[2] + by_y[3]
            gain[...] = total[0:4]
            shift[...] = total[4:8]
            outb[...] = total[8:10]
            downb[...] = total[10:11]
            router[...] = total[16:48]
            for y in range(NY):
                upb[:, y * D : (y + 1) * D] = by_y[y][11:12]
                for i in range(2):
                    for t in range(2):
                        row = by_y[y][12 + 2 * i + t : 13 + 2 * i + t, 0:HW]
                        qvb[i : i + 1, t * D + y * HW : t * D + (y + 1) * HW] = row
            own = edb[:, 0:HW]
            for y in range(1, NY):
                own = jnp.where(lax.axis_index("seq") == y, edb[:, y * HW : (y + 1) * HW], own)
            edb_o[...] = own
            eub_o[...] = eub[...]

    def qkv_at(s):
        j = jnp.minimum(s, 11)
        return lax.div(j, 6), lax.rem(j, 2), lax.div(lax.rem(j, 6), 2)

    def out_at(s):
        return lax.div(s, 8), lax.rem(lax.div(s, 4), 2), lax.rem(s, 4)

    def feed_at(s, z):
        y, j = lax.div(s, 4), lax.rem(s, 4)
        return 0, y, z + lax.div(j, 2), lax.rem(j, 2), 0, 0

    def qkv_in(s):
        i, c, t = qkv_at(s)
        return i, c, 0, t, 0, 0, 0

    def qkv_out(s):
        i, c, t = qkv_at(s)
        return i, c, t

    def out_in(s):
        i, c, y = out_at(s)
        return i, c, y, 3, 0, 0, 0

    def out_out(s):
        i, c, y = out_at(s)
        return i, y, c

    small = [(4, D), (4, D), (2, D), (1, D), (1, NY * D), (2, 2 * D), (EXPERTS, D), (1, HW), (1, D)]
    whole = lambda sh: pl.BlockSpec(sh, lambda s: (0,) * len(sh))
    rows = lambda n, last: pl.BlockSpec((n, D), lambda s: (jnp.minimum(s, last), 0))
    passed = [rows(48, 15), rows(48, 15), rows(16, 8), rows(16, 8)]
    big = [(2, D, 3 * D), (2, D, D), (D, NY * D), (NY * D, D), (D, D), (D, D), (ROWS, D), (ROWS, D)]
    return pl.pallas_call(
        body,
        grid=(16,),
        in_specs=[
            pl.BlockSpec((1, 1, 4, 1, 4, 48, HALF), qkv_in),
            pl.BlockSpec((1, 1, 1, 1, 4, 48, HALF), out_in),
            pl.BlockSpec((2, 1, 1, 2, 96, HALF), lambda s: feed_at(s, 0)),
            pl.BlockSpec((2, 1, 1, 2, 96, HALF), lambda s: feed_at(s, 2)),
        ]
        + passed
        + [whole((2, 4, 48, HALF)), whole((1, D)), whole((1, D))],
        out_specs=[
            pl.BlockSpec((1, HALF, D), qkv_out),
            pl.BlockSpec((1, HW, HALF), out_out),
            pl.BlockSpec((HW, D), lambda s: (lax.rem(s, 4), lax.div(s, 4))),
            pl.BlockSpec((HW, D), lambda s: (s, 0)),
        ]
        + passed
        + [whole(sh) for sh in small],
        out_shape=[jax.ShapeDtypeStruct(sh, F32) for sh in big + small],
        compiler_params=pltpu.CompilerParams(vmem_limit_bytes=62 * 2**20),
        name="spread",
    )(o.f13, o.f13, o.f2, o.f2, o.g_eup, o.g_edown, o.result, o.d_tok, o.fs, o.g_edb, o.g_eub)


def local(
    tokens,
    cotangent,
    ln_gain,
    ln_shift,
    qkv_weight,
    qv_bias,
    out_weight,
    out_bias,
    up_weight,
    up_bias,
    down_weight,
    down_bias,
    router,
    expert_up,
    expert_up_bias,
    expert_down,
    expert_down_bias,
    expert_ids,
    priority,
):
    o = types.SimpleNamespace(
        **layers(
            (
                tokens[0],
                cotangent[0],
                ln_gain,
                ln_shift,
                qkv_weight,
                qv_bias,
                out_weight,
                out_bias,
                up_weight,
                up_bias.reshape(24, 128),
                down_weight,
                down_bias.reshape(6, 128),
                router.T,
                expert_up[0],
                expert_up_bias,
                expert_down[0],
                expert_down_bias,
                expert_ids[0].T,
                priority[0].T,
            )
        )
    )
    g_qkv, g_out, g_up, g_down, geu, ged, res, tok, *small = spread(o)
    gain, shift, outb, downb, upb, qvb, g_router, edb, eub = small
    return (
        res[None],
        tok[None],
        gain,
        shift,
        g_qkv,
        qvb,
        g_out,
        outb,
        g_up,
        upb.reshape(NY * D),
        g_down,
        downb.reshape(D),
        g_router.T,
        geu[None],
        eub,
        ged[None],
        edb,
    )


def solution(mesh):
    in_specs = (
        P("dp", "seq", None),
        P("dp", "seq", None),
        P(),
        P(),
        P(None, "dp", None),
        P(),
        P(None, "dp", None),
        P(),
        P("dp", None),
        P(),
        P("dp", None),
        P(),
        P(),
        P("dp", None, "seq"),
        P("dp", "seq"),
        P("dp", "seq", None),
        P("dp", None),
        P("dp", "seq", None),
        P("dp", "seq", None),
    )
    out_specs = (
        P("dp", "seq", None),
        P("dp", "seq", None),
        P(),
        P(),
        P(),
        P(),
        P(),
        P(),
        P(),
        P(),
        P(),
        P(),
        P(),
        P("dp", None, "seq"),
        P("dp", "seq"),
        P("dp", "seq", None),
        P("dp", "seq"),
    )
    return jax.shard_map(local, mesh=mesh, in_specs=in_specs, out_specs=out_specs, check_vma=False)
```

```python
import functools
import types

import jax
import jax.numpy as jnp
from jax import lax
from jax.experimental import pallas as pl
from jax.experimental.pallas import tpu as pltpu
from jax.sharding import PartitionSpec as P

MESH = pl.DeviceIdType.MESH
F32, BF16 = jnp.float32, jnp.bfloat16

D = 768
HEADS_DEV = 3
HW = 192
ROWS = 144
NY = 4
NDP = 32
EXPERTS = 32
CAP = 4
EPS = 1e-06
LO, HI = 80, 64
HALF = D // 2

NN = (((1,), (0,)), ((), ()))
RING4 = (1, 2, 3)
NT = (((1,), (1,)), ((), ()))
TN = (((0,), (0,)), ((), ()))


def mm(a, b, dims=NN):
    return lax.dot_general(a, b, dims, preferred_element_type=F32)


def ln_stats(x):
    mean = jnp.mean(x, axis=-1, keepdims=True)
    cen = x - mean
    rstd = lax.rsqrt(jnp.mean(cen * cen, axis=-1, keepdims=True) + EPS)
    return cen * rstd, rstd


def ln_forward(x, gain, shift):
    nhat, _ = ln_stats(x)
    return nhat * gain + shift


def ln_backward(x, gain, grad):
    nhat, rstd = ln_stats(x)
    d_gain = jnp.sum(grad * nhat, axis=0, keepdims=True)
    d_shift = jnp.sum(grad, axis=0, keepdims=True)
    gg = grad * gain
    dx = rstd * (
        gg
        - jnp.mean(gg, axis=-1, keepdims=True)
        - nhat * jnp.mean(gg * nhat, axis=-1, keepdims=True)
    )
    return dx, d_gain, d_shift


GC = 0.7978845608028654
GA = 0.044715


def gelu_both(u):
    sq = u * u
    t = jnp.tanh(GC * u * (1.0 + GA * sq))
    half = 0.5 * (1.0 + t)
    slope = half + 0.5 * u * (1.0 - t * t) * (GC * (1.0 + 3.0 * GA * sq))
    return u * half, slope


class Ring:
    def __init__(self):
        self.y = lax.axis_index("seq")
        self.right = lax.rem(self.y + 1, NY)
        self.left = lax.rem(self.y + 3, NY)
        self.opp = lax.rem(self.y + 2, NY)


def send(src, dst, ss, rs, i, to):
    c = pltpu.make_async_remote_copy(
        src_ref=src,
        dst_ref=dst,
        send_sem=ss.at[i],
        recv_sem=rs.at[i],
        device_id={"seq": to},
        device_id_type=MESH,
    )
    c.start()
    return c


def gather_start(ring, buf, lo, hi, ss, rs):
    y, low, high = ring.y, pl.ds(0, lo), pl.ds(lo, hi)
    a0 = send(buf.at[y, low], buf.at[y, low], ss, rs, 0, ring.right)
    b0 = send(buf.at[y, high], buf.at[y, high], ss, rs, 1, ring.left)
    a1 = send(buf.at[y, high], buf.at[y, high], ss, rs, 2, ring.right)
    b1 = send(buf.at[y, low], buf.at[y, low], ss, rs, 3, ring.left)
    return a0, b0, a1, b1


def gather_forward(ring, buf, lo, hi, ss, rs, copies):
    a0, b0, a1, b1 = copies
    low, high = pl.ds(0, lo), pl.ds(lo, hi)
    a0.wait_recv()
    a2 = send(buf.at[ring.left, low], buf.at[ring.left, low], ss, rs, 4, ring.right)
    b0.wait_recv()
    b2 = send(buf.at[ring.right, high], buf.at[ring.right, high], ss, rs, 5, ring.left)
    a1.wait_recv()
    b1.wait_recv()
    return a2, b2


def nothing():
    pass


def gather_blocks(ring, buf, lo, hi, ss, rs, use, early=nothing, late=nothing):
    first = gather_start(ring, buf, lo, hi, ss, rs)
    early()
    use(ring.y)
    last = gather_forward(ring, buf, lo, hi, ss, rs, first)

    def near(i, carry):
        use(lax.rem(ring.y + 1 + 2 * i, NY))
        return carry

    lax.fori_loop(0, 2, near, 0)
    late()
    for c in last:
        c.wait_recv()
    use(ring.opp)
    for c in first + last:
        c.wait_send()


class Scatter:
    def __init__(self, ring, part, lo, hi, sbuf, rbuf, ss, rs):
        self.ring, self.part, self.sbuf, self.rbuf, self.ss, self.rs = ring, part, sbuf, rbuf, ss, rs
        self.low, self.high = pl.ds(0, lo), pl.ds(lo, hi)
        self.all = []

    def send(self, slot, rows, right):
        i = len(self.all)
        to = self.ring.right if right else self.ring.left
        c = send(self.sbuf.at[slot, rows], self.rbuf.at[slot, rows], self.ss, self.rs, i, to)
        self.all.append(c)
        return c

    def near(self, right):
        slot, rows, j = (1, self.high, self.ring.right) if right else (2, self.low, self.ring.left)
        self.sbuf[slot, rows] = self.part[j, rows].astype(BF16)
        self.send(slot, rows, right)

    def opposite(self):
        self.sbuf[0] = self.part[self.ring.opp].astype(BF16)
        self.over = self.send(0, self.low, True), self.send(0, self.high, False)

    def onward(self):
        for c, slot, rows, j, right in (
            (self.over[0], 1, self.low, self.ring.right, True),
            (self.over[1], 2, self.high, self.ring.left, False),
        ):
            c.wait_recv()
            self.sbuf[slot, rows] = (self.part[j, rows] + self.rbuf[0, rows].astype(F32)).astype(BF16)
            self.send(slot, rows, right)

    def end(self):
        for c in self.all:
            if all(c is not o for o in self.over):
                c.wait_recv()
        total = self.part[self.ring.y] + self.rbuf[1].astype(F32) + self.rbuf[2].astype(F32)
        for c in self.all:
            c.wait_send()
        return total


def pass_through(ring, buf, sc, lo, hi, ss, rs, use, early=nothing, late=nothing, beside=nothing):
    first = gather_start(ring, buf, lo, hi, ss, rs)
    early()
    use(ring.y)
    last = gather_forward(ring, buf, lo, hi, ss, rs, first)

    def near(i, carry):
        use(lax.rem(ring.y + 1 + 2 * i, NY))
        return carry

    lax.fori_loop(0, 2, near, 0)
    sc.near(True)
    sc.near(False)
    late()
    for c in last:
        c.wait_recv()
    use(ring.opp)
    sc.opposite()
    for c in first + last:
        c.wait_send()
    sc.onward()
    beside()
    return sc.end()


def swap_all(d, sbuf, rbuf, ssem, rsem):
    def start(k, carry):
        to = lax.rem(d + k, NDP)
        push(sbuf.at[to], rbuf.at[d], ssem, rsem, {"dp": to})
        return carry

    lax.fori_loop(1, NDP, start, 0)
    rbuf[d] = sbuf[d]
    for buf, sem in ((sbuf, ssem), (rbuf, rsem)):
        others = buf.at[pl.ds(0, NDP - 1)]
        pltpu.make_async_copy(others, others, sem).wait()


class Place:
    def __init__(self):
        d = lax.axis_index("dp")
        self.d = d
        self.z, self.x, self.c = lax.div(d, 8), lax.rem(lax.div(d, 2), 4), lax.rem(d, 2)

    def at(self, z=None, x=None, c=None):
        z, x, c = (m if v is None else v for v, m in ((z, self.z), (x, self.x), (c, self.c)))
        return {"dp": (z * 4 + x) * 2 + c}


class Pool:
    def __init__(self, sems, size):
        self.sems, self.size, self.copies = sems, size, []

    def push(self, src, dst, rsem, to):
        n = len(self.copies)
        if n >= self.size:
            self.copies[n - self.size].wait_send()
        c = push(src, dst, self.sems.at[n % self.size], rsem, to)
        self.copies.append(c)
        return c

    def end(self):
        for c in self.copies[-self.size :]:
            c.wait_send()


def push(src, dst, ssem, rsem, to):
    c = pltpu.make_async_remote_copy(
        src_ref=src, dst_ref=dst, send_sem=ssem, recv_sem=rsem, device_id=to, device_id_type=MESH
    )
    c.start()
    return c


def across(v, sel):
    hi = v.astype(BF16)
    rest = v.astype(F32) - hi.astype(F32)
    mid = rest.astype(BF16)
    return mm(hi, sel) + mm(mid, sel) + mm((rest - mid.astype(F32)).astype(BF16), sel)


class Weights:
    def __init__(self, R, place, ring):
        self.R, self.p, self.ring = R, place, ring
        self.own = (R.wqkv0, R.wup, R.w_out, R.w_down, R.wqkv1)
        self.got = (R.wqkv0g, R.wupg, R.woutg, R.wdowng, R.wqkv1g)
        self.now = {}
        self.next = 0

    def push(self, src, dst, to):
        i = self.next
        self.next += 1
        return self.R.pool.push(src, dst, self.R.wrs.at[i], to)

    def cut(self):
        R, y = self.R, self.ring.y
        sel = one_hot(iota((D, HW), 0) == iota((D, HW), 1) + HW * y)
        for t in range(3):
            at = pl.ds(t * HW, HW)
            R.wqkv0[:, at] = mm(R.w_qkv[0, :, t * D : (t + 1) * D], sel).astype(BF16)
            R.wqkv1[:, at] = mm(R.w_qkv[1, :, t * D : (t + 1) * D], sel).astype(BF16)
        R.wup[...] = R.w_up[:, pl.ds(pl.multiple_of(D * y, D), D)]
        for t in range(2):
            R.qvb[2 * t : 2 * t + 2] = across(R.qv_bias[:, t * D : (t + 1) * D], sel)

    def a_along_x(self, n):
        p, buf = self.p, self.got[n]
        self.now[n] = [
            self.push(self.own[n], buf.at[p.z, p.x, p.c], p.at(x=lax.rem(p.x + k, 4))) for k in RING4
        ]
        buf[p.z, p.x, p.c] = self.own[n][...]

    def wait(self, n):
        for c in self.now[n]:
            c.wait_recv()

    def a_along_z(self, n):
        p, buf = self.p, self.got[n]
        self.wait(n)
        row = buf.at[p.z, :, p.c]
        self.now[n] = [self.push(row, row, p.at(z=lax.rem(p.z + k, 4))) for k in RING4]

    def a_along_core(self, n):
        p = self.p
        self.wait(n)
        half = self.got[n].at[:, :, p.c]
        self.now[n] = [self.push(half, half, p.at(c=1 - p.c))]

    def b_copy(self, n, k):
        p, R = self.p, self.R
        return pltpu.make_async_remote_copy(
            src_ref=self.own[n],
            dst_ref=self.got[n].at[p.x, p.c],
            send_sem=R.bss.at[n - 2, k],
            recv_sem=R.bss.at[n - 2, 0],
            device_id=p.at(z=lax.rem(p.z + k, 4)),
            device_id_type=MESH,
        )

    def b_along_z(self, n):
        @pl.when(self.p.z == self.ring.y)
        def _():
            for k in RING4:
                self.b_copy(n, k).start()
            self.got[n][self.p.x, self.p.c] = self.own[n][...]

    def b_along_x(self, n):
        p = self.p

        @pl.when(p.z != self.ring.y)
        def _():
            self.b_copy(n, 1).wait_recv()

        own = self.got[n].at[p.x, p.c]
        self.now[n] = [self.push(own, own, p.at(x=lax.rem(p.x + k, 4))) for k in RING4]

    def b_along_core(self, n):
        p = self.p
        self.wait(n)
        half = self.got[n].at[:, p.c]
        self.now[n] = [self.push(half, half, p.at(c=1 - p.c))]

    def sent(self):
        @pl.when(self.p.z == self.ring.y)
        def _():
            for n in (2, 3):
                for k in RING4:
                    self.b_copy(n, k).wait_send()

    def lay(self, n):
        R = self.R
        self.wait(n)

        def one(j, carry):
            rows = pl.ds(pl.multiple_of(192 * j, 192), 192)
            v = self.got[n][j].astype(F32)
            if n in (0, 4):
                v = v.reshape(192, 3 * HW).astype(BF16)
                for t in range(3):
                    R.wqkv[n // 4, t, rows] = v[:, t * HW : (t + 1) * HW]
            elif n == 1:
                R.up[rows] = v.reshape(192, D).astype(BF16)
            elif n == 2:
                for i in range(2):
                    R.wout[i, pl.ds(pl.multiple_of(48 * j, 48), 48)] = v[:, i].reshape(48, D).astype(BF16)
            else:
                R.down[rows] = v.reshape(192, D).astype(BF16)
            return carry

        lax.fori_loop(0, 4, one, 0)


def head_mask(h, dtype):
    lane = lax.broadcasted_iota(jnp.int32, (1, HW), 1)
    return ((lane >= 64 * h) & (lane < 64 * (h + 1))).astype(dtype)


def keep_grad(ref, first, grad):
    depth = ref.shape[3]
    count = grad.shape[0] // (4 * depth)
    low = grad.astype(BF16)
    for c in range(2):
        half = low[:, c * HALF : (c + 1) * HALF].reshape(count, 4, depth, HALF)
        ref[c, first : first + count] = half


def flat(ref):
    v = ref[...]
    return v.reshape(v.shape[0] * v.shape[1], v.shape[2])


def attn_forward(R, ring, i, x, gain, shift, w=None):
    nbuf, q, k, v, o, st = R.n[2 * i], R.q[i], R.k[i], R.v[i], R.o[i], R.st[i]
    wqkv, wout, qvb, part, vm = R.wqkv, R.wout, R.qvb, R.part, R.vm
    nbuf[ring.y] = ln_forward(x, gain, shift).astype(BF16)

    def project(j):
        nj = nbuf[j]
        q[j] = ((mm(nj, wqkv[i, 0]) + qvb[i : i + 1]).astype(BF16).astype(F32) * 0.125).astype(BF16)
        k[j] = mm(nj, wqkv[i, 1]).astype(BF16)
        v[j] = (mm(nj, wqkv[i, 2]) + qvb[2 + i : 3 + i]).astype(BF16)

    def early():
        w.a_along_z(0)
        w.b_along_x(2)
        w.a_along_x(1)
        w.a_along_core(0)
        w.a_along_z(1)
        w.b_along_z(3)
        w.lay(0)

    gather_blocks(ring, nbuf, LO, HI, R.ssem.at[0], R.rsem.at[0], project, nothing if w is None else early)
    if w is not None:
        w.b_along_core(2)
    v_all = flat(v)
    for h in range(HEADS_DEV):
        vm[h] = v_all * head_mask(h, BF16)
    k_all = flat(k)

    def rows(b):
        qb = q[b]
        acc = jnp.zeros((ROWS, HW), F32)
        stats = jnp.zeros((ROWS, 128), F32)
        lane = lax.broadcasted_iota(jnp.int32, (ROWS, 128), 1)
        for h in range(HEADS_DEV):
            s = mm(qb * head_mask(h, BF16), k_all, NT)
            top = jnp.max(s, axis=-1, keepdims=True)
            e = jnp.exp(s - top)
            tot = jnp.sum(e, axis=-1, keepdims=True)
            acc = acc + mm(e.astype(BF16), vm[h]) * (1.0 / tot)
            stats = jnp.where(lane == h, top + jnp.log(tot), stats)
        o[b] = acc
        st[b] = stats
        part[b] = mm(acc.astype(BF16), wout[i])

    if w is not None:
        w.lay(2)
    sc = Scatter(ring, part, LO, HI, R.sb, R.rb, R.ssem.at[1], R.rsem.at[1])
    rows(ring.opp)
    sc.opposite()

    def near(t, carry):
        rows(lax.rem(ring.y + 1 + 2 * t, NY))
        return carry

    lax.fori_loop(0, 2, near, 0)
    sc.near(True)
    sc.near(False)
    if w is not None:
        w.b_along_x(3)
        w.a_along_core(1)
        w.a_along_x(4)
    sc.onward()
    rows(ring.y)
    if w is not None:
        w.b_along_core(3)
        w.a_along_z(4)
    total = sc.end()
    if w is not None:
        w.lay(1)
        w.lay(3)
    return x + total + R.out_bias[i : i + 1]


EARLY, LATE, BEFORE, MIDDLE, AFTER, WEIGHTS, BESIDE, END = range(8)


def attn_backward(R, ring, i, x, gain, grad, slot, hooks):
    nbuf, q, k, v, o, st = R.n[2 * i], R.q[i], R.k[i], R.v[i], R.o[i], R.st[i]
    wqkv, wout, part = R.wqkv, R.wout, R.part
    gb, go, gm, qm, gq, gk, gv, dq = R.gb[slot // 2 % 2], R.go, R.vm, R.qm, R.gq, R.gk, R.gv, R.dq
    low = grad.astype(BF16)
    gb[ring.y] = low
    R.small[pl.ds(8 + i, 1)] = jnp.sum(low.astype(F32), axis=0, keepdims=True)

    def project(j):
        g = mm(gb[j], wout[i], NT).astype(BF16)
        go[j] = g
        prod = g.astype(F32) * o[j]
        stats = st[j]
        lane = lax.broadcasted_iota(jnp.int32, (ROWS, 128), 1)
        for h in range(HEADS_DEV):
            inner = jnp.sum(prod * head_mask(h, F32), axis=-1, keepdims=True)
            stats = jnp.where(lane == 4 + h, inner, stats)
        st[j] = stats

    at = hooks.get
    gather_blocks(
        ring, gb, LO, HI, R.ssem.at[0], R.rsem.at[0], project, at(EARLY, nothing), at(LATE, nothing)
    )
    at(BEFORE, nothing)()
    go_all, q_all = flat(go), flat(q)
    for h in range(HEADS_DEV):
        gm[h] = go_all * head_mask(h, BF16)
        qm[h] = q_all * head_mask(h, BF16)
    stats_t = jnp.transpose(flat(st))
    R.stt[...] = stats_t[0:8]
    dq[...] = jnp.zeros((NY * ROWS, HW), F32)

    def keys(b, carry):
        kb, vb = k[b], v[b]
        dk = jnp.zeros((ROWS, HW), F32)
        dv = jnp.zeros((ROWS, HW), F32)
        for h in range(HEADS_DEV):
            kh = kb * head_mask(h, BF16)
            p = jnp.exp(mm(kh, qm[h], NT) - R.stt[h : h + 1])
            dp = mm(vb, gm[h], NT)
            ds = (p * (dp - R.stt[4 + h : 5 + h])).astype(BF16)
            dv = dv + mm(p.astype(BF16), gm[h])
            dk = dk + mm(ds, qm[h])
            dq[...] += mm(ds, kh, TN)
        gk[b] = dk.astype(BF16)
        gv[b] = dv.astype(BF16)
        return carry

    lax.fori_loop(0, 2, keys, 0)
    at(MIDDLE, nothing)()
    lax.fori_loop(2, NY, keys, 0)
    at(AFTER, nothing)()
    gq[...] = (dq[...] * 0.125).astype(BF16).reshape(NY, ROWS, HW)

    def back(b):
        part[b] = mm(gq[b], wqkv[i, 0], NT) + mm(gk[b], wqkv[i, 1], NT) + mm(gv[b], wqkv[i, 2], NT)

    def weights():
        n_all, grads = flat(nbuf), R.g13[i]
        for t, g in enumerate((gq, gk, gv)):
            g_all = flat(g)
            keep_grad(grads, t, mm(g_all, n_all, TN))
            if t != 1:
                row = 12 + 2 * i + t // 2
                R.small[row : row + 1, 0:HW] = jnp.sum(g_all.astype(F32), axis=0, keepdims=True)
        keep_grad(grads, 3, mm(flat(o).astype(BF16), flat(gb), TN))

    if WEIGHTS in hooks:
        weights()
        hooks[WEIGHTS]()
    sc = Scatter(ring, part, LO, HI, R.sb, R.rb, R.ssem.at[1], R.rsem.at[1])
    back(ring.opp)
    sc.opposite()

    def near(t, carry):
        back(lax.rem(ring.y + 1 + 2 * t, NY))
        return carry

    lax.fori_loop(0, 2, near, 0)
    sc.near(True)
    sc.near(False)
    sc.onward()
    back(ring.y)
    if WEIGHTS not in hooks:
        weights()
    at(BESIDE, nothing)()
    total = sc.end()
    at(END, nothing)()
    dx, d_gain, d_shift = ln_backward(x, gain, total)
    R.small[pl.ds(2 * i, 1)] = d_gain
    R.small[pl.ds(4 + 2 * i, 1)] = d_shift
    return grad + dx


def across_rows(ref, n):
    return jnp.concatenate([ref[6 * n + j : 6 * n + j + 1] for j in range(6)], axis=1)


def feed_forward(R, ring, x, gain, shift, w):
    nbuf, u, a, part = R.n[1], R.u, R.a, R.part
    nbuf[ring.y] = ln_forward(x, gain, shift).astype(BF16)
    bias = across_rows(R.up_bias, 0)
    for y in range(1, NY):
        bias = jnp.where(ring.y == y, across_rows(R.up_bias, y), bias)

    def use(j):
        uj = mm(nbuf[j], R.up[...]) + bias
        act, slope = gelu_both(uj)
        u[j] = slope
        aj = act.astype(BF16)
        a[j] = aj
        part[j] = mm(aj, R.down[...])

    sc = Scatter(ring, part, LO, HI, R.sb, R.rb, R.ssem.at[1], R.rsem.at[1])
    core, lay = functools.partial(w.a_along_core, 4), functools.partial(w.lay, 4)
    total = pass_through(ring, nbuf, sc, LO, HI, R.ssem.at[0], R.rsem.at[0], use, late=core, beside=lay)
    return x + total + across_rows(R.down_bias, 0)


def feed_backward(R, ring, x, gain, grad, slot, hooks):
    nbuf, u, a, part, gb, gu = R.n[1], R.u, R.a, R.part, R.gb[slot // 2 % 2], R.gu
    low = grad.astype(BF16)
    gb[ring.y] = low
    R.small[10:11] = jnp.sum(low.astype(F32), axis=0, keepdims=True)

    def use(j):
        g = (mm(gb[j], R.down[...], NT) * u[j]).astype(BF16)
        gu[j] = g
        part[j] = mm(g, R.up[...], NT)

    at = hooks.get

    def beside():
        at(BEFORE, nothing)()
        n_all, g_all, a_all, gb_all = flat(nbuf), flat(gu), flat(a), flat(gb)
        keep_grad(R.g2, 0, mm(n_all, g_all, TN))
        keep_grad(R.g2, 2, mm(a_all, gb_all, TN))
        R.small[11:12] = jnp.sum(g_all.astype(F32), axis=0, keepdims=True)
        at(BESIDE, nothing)()

    sc = Scatter(ring, part, LO, HI, R.sb, R.rb, R.ssem.at[1], R.rsem.at[1])
    total = pass_through(
        ring,
        gb,
        sc,
        LO,
        HI,
        R.ssem.at[0],
        R.rsem.at[0],
        use,
        at(EARLY, nothing),
        at(LATE, nothing),
        beside,
    )
    at(END, nothing)()
    dx, d_gain, d_shift = ln_backward(x, gain, total)
    R.small[1:2] = d_gain
    R.small[5:6] = d_shift
    return grad + dx


def iota(shape, dim):
    return lax.broadcasted_iota(jnp.int32, shape, dim)


def slot_ids(shape, dim):
    r = iota(shape, dim)
    e, t = r >> 3, r & 7
    z = jnp.where(t < 4, e * 4 + t, -1)
    g = jnp.where(t >= 4, e * 4 + t - 4, -1)
    return z.astype(F32), g.astype(F32)


def one_hot(cond):
    return jnp.where(cond, 1.0, 0.0).astype(BF16)


def mixture(R, ring, d, x, gain, shift):
    low = ln_forward(x, gain, shift).astype(BF16)
    cot = R.cot[...].astype(F32)
    logits = mm(low, R.router[...], NT)

    idr, prr = R.ids[...], R.pri[...]
    digits = jnp.concatenate([idr, prr >> 8, prr & 255], axis=0).astype(F32).astype(BF16)
    turned = mm(one_hot(iota((ROWS, ROWS), 0) == iota((ROWS, ROWS), 1)), digits, NT)
    idc = turned[:, 0:2].astype(jnp.int32)
    prc = (turned[:, 2:4] * 256.0 + turned[:, 4:6]).astype(jnp.int32)
    key_c, key_r = [], []
    for k in range(2):
        key_c.append(prc[:, k : k + 1] * (2 * ROWS) + 2 * iota((ROWS, 1), 0) + k)
        key_r.append(prr[k : k + 1, :] * (2 * ROWS) + 2 * iota((1, ROWS), 1) + k)
    rank_c = [jnp.zeros((ROWS, 1), F32) for _ in range(2)]
    rank_r = [jnp.zeros((1, ROWS), F32) for _ in range(2)]
    for k in range(2):
        for j in range(2):
            same = idc[:, k : k + 1] == idr[j : j + 1, :]
            before = key_r[j] < key_c[k]
            after = key_c[k] < key_r[j]
            rank_c[k] = rank_c[k] + jnp.sum(jnp.where(same & before, 1.0, 0.0), axis=1, keepdims=True)
            rank_r[j] = rank_r[j] + jnp.sum(jnp.where(same & after, 1.0, 0.0), axis=0, keepdims=True)
    kept = [jnp.where(r < CAP, 1.0, 0.0) for r in rank_c]
    slot_c = [jnp.where(rank_c[k] < CAP, idc[:, k : k + 1].astype(F32) * CAP + rank_c[k], 1000.0) for k in range(2)]
    slot_r = [jnp.where(rank_r[k] < CAP, idr[k : k + 1, :].astype(F32) * CAP + rank_r[k], 1000.0) for k in range(2)]

    picks = [jnp.where(iota((ROWS, EXPERTS), 1) == idc[:, k : k + 1], 1.0, 0.0) for k in range(2)]
    chosen = [jnp.sum(logits * p, axis=-1, keepdims=True) for p in picks]
    top = jnp.maximum(chosen[0], chosen[1])
    ex = [jnp.exp(c - top) for c in chosen]
    gates = [e / (ex[0] + ex[1]) for e in ex]

    zid, gid = slot_ids((8 * EXPERTS, ROWS), 0)
    rows = mm(one_hot((zid == slot_r[0]) | (zid == slot_r[1])), low)
    for k in range(2):
        rows = rows + mm(one_hot(gid == slot_r[k]), (gates[k] * cot).astype(BF16))
    R.ds[...] = rows.reshape(EXPERTS, 8, D).astype(BF16)
    swap_all(d, R.ds, R.dr.at[0], R.dssem.at[0], R.drsem.at[0])

    n_slots = CAP * NDP
    back = iota((2 * n_slots, 2 * n_slots), 0)
    col = iota((2 * n_slots, 2 * n_slots), 1)
    s = back & (n_slots - 1)
    src = (s >> 2) * 8 + (s & 3) + jnp.where(back >= n_slots, 4, 0)
    sort = one_hot(src == col)
    arrived = R.dr[0].astype(F32).reshape(2 * n_slots, D).astype(BF16)
    moe = R.moe
    moe[ring.y] = mm(sort, arrived).astype(BF16)
    part = R.mpart

    def use(j):
        z, gy = moe[j, 0:n_slots], moe[j, n_slots : 2 * n_slots]
        c = mm(z, R.eu[...]) + R.e_up_bias[...].astype(F32)
        act, slope = gelu_both(c)
        b = act.astype(BF16)
        R.eb[j] = b
        gc = (slope * mm(gy, R.ed[...], NT)).astype(BF16)
        R.egc[j] = gc
        part[j, 0:n_slots] = mm(b, R.ed[...])
        part[j, n_slots : 2 * n_slots] = mm(gc, R.eu[...], NT)

    def beside():
        z_all = moe[:, 0:n_slots].reshape(NY * n_slots, D)
        gy_all = moe[:, n_slots : 2 * n_slots].reshape(NY * n_slots, D)
        b_all, gc_all = flat(R.eb), flat(R.egc)
        R.geu[...] = mm(z_all, gc_all, TN).astype(BF16)
        R.ged[...] = mm(b_all, gy_all, TN).astype(BF16)
        R.g_eub[...] = jnp.sum(gc_all.astype(F32), axis=0, keepdims=True)
        R.g_edb[...] = jnp.sum(gy_all.astype(F32), axis=0, keepdims=True)

    sc = Scatter(ring, part, n_slots, n_slots, R.msb, R.mrb, R.ssem.at[1], R.rsem.at[1])
    total = pass_through(ring, moe, sc, n_slots, n_slots, R.ssem.at[0], R.rsem.at[0], use, beside=beside)
    is_y = jnp.where(iota((2 * n_slots, 1), 0) < n_slots, 1.0, 0.0)
    total = (total + is_y * R.e_down_bias[...]).astype(BF16)
    unsort = one_hot((col & (n_slots - 1)) * 2 - (col & 3) + jnp.where(col >= n_slots, 4, 0) == back)
    R.ds[...] = mm(unsort, total).reshape(NDP, 8, D).astype(BF16)
    swap_all(d, R.ds, R.dr.at[1], R.dssem.at[1], R.drsem.at[1])
    came = R.dr[1].astype(F32).reshape(8 * EXPERTS, D).astype(BF16)

    zid, gid = slot_ids((ROWS, 8 * EXPERTS), 1)
    result = x
    grad_gate = []
    for k in range(2):
        taken = mm(one_hot(zid == slot_c[k]), came)
        result = result + (gates[k] * kept[k]) * taken
        grad_gate.append(kept[k] * jnp.sum(taken * cot, axis=-1, keepdims=True))
    R.result[...] = result
    inner = gates[0] * grad_gate[0] + gates[1] * grad_gate[1]
    gl = sum(gates[k] * (grad_gate[k] - inner) * picks[k] for k in range(2))
    gl_hi = gl.astype(BF16)
    rest = gl - gl_hi.astype(F32)
    gl_mid = rest.astype(BF16)
    gl_lo = (rest - gl_mid.astype(F32)).astype(BF16)
    grad_low = mm(one_hot((gid == slot_c[0]) | (gid == slot_c[1])), came)
    g_router = jnp.zeros((EXPERTS, D), F32)
    for piece in (gl_hi, gl_mid, gl_lo):
        grad_low = grad_low + mm(piece, R.router[...])
        g_router = g_router + mm(piece, low, TN)
    R.small[16 : 16 + EXPERTS] = g_router
    dx, d_gain, d_shift = ln_backward(x, gain, grad_low)
    R.small[3:4] = d_gain
    R.small[7:8] = d_shift
    return cot + dx


ORDERS = ("zxy", "xyz", "yzx")


def sum_scratch(r, a):
    low, sems = (lambda *sh: pltpu.VMEM(sh, BF16)), pltpu.SemaphoreType.DMA
    b = r - a
    return dict(
        r=low(4, 4, r, HALF),
        xa=low(3, 4, a, HALF),
        zb=low(3, 4, b, HALF),
        ba=low(4, a, HALF),
        bb=low(4, b, HALF),
        za=low(3, a, HALF),
        xb=low(3, b, HALF),
        o=low(r, HALF),
        rs=sems((70,)),
        local=sems,
    )


def wait_all(copies):
    for c in copies:
        c.wait_recv()


def add_up(first, *rest):
    total = first.astype(F32)
    for r in rest:
        total = total + r.astype(F32)
    return total.astype(BF16)


class Pushes:
    def __init__(self, pool, place, ring, rs):
        self.pool, self.p, self.ring, self.rs = pool, place, ring, rs
        self.next = 0
        self.other = place.at(c=1 - place.c)
        self.me = dict(x=place.x, y=ring.y, z=place.z)

    def push(self, src, dst, to):
        i = self.next
        self.next += 1
        return self.pool.push(src, dst, self.rs.at[i], to)

    def pos(self, axis, k=0):
        return lax.rem(self.me[axis] + k, 4)

    def peer(self, axis, k):
        at = self.pos(axis, k)
        return {"seq": at} if axis == "y" else self.p.at(**{axis: at})


class Sum(Pushes):
    def __init__(self, R, place, ring, grad, full, scr):
        s = types.SimpleNamespace(**scr)
        super().__init__(R.pool, place, ring, s.rs)
        self.s, self.grad, self.full = s, grad, full
        self.rows = grad.shape[3]
        self.a = s.ba.shape[1]
        self.third = self.rows // 3

    def halves(self):
        self.halved = self.push(self.grad.at[1 - self.p.c], self.s.r, self.other)
        self.core = []

    def first_axis(self):
        s, p, a = self.s, self.p, self.a
        self.halved.wait_recv()

        def add(z, carry):
            s.r[z] = add_up(self.grad[p.c, z], s.r[z])
            return carry

        lax.fori_loop(0, 4, add, 0)
        top, rest = pl.ds(0, a), pl.ds(a, self.rows - a)
        self.na = [self.push(s.r.at[:, self.pos("x", k), top], s.xa.at[k - 1], self.peer("x", k)) for k in RING4]
        self.nb = [self.push(s.r.at[self.pos("z", k), :, rest], s.zb.at[k - 1], self.peer("z", k)) for k in RING4]

    def second_axis(self):
        s, p, a = self.s, self.p, self.a
        wait_all(self.na)
        s.ba[...] = add_up(s.r[:, p.x, 0:a], *(s.xa[k] for k in range(3)))
        self.na = [self.push(s.ba.at[self.pos("z", k)], s.za.at[k - 1], self.peer("z", k)) for k in RING4]
        wait_all(self.nb)
        s.bb[...] = add_up(s.r[p.z, :, a : self.rows], *(s.zb[k] for k in range(3)))
        self.nb = [self.push(s.bb.at[self.pos("x", k)], s.xb.at[k - 1], self.peer("x", k)) for k in RING4]

    def view(self, t, index):
        every = pl.ds(0, 4)
        y, z, x = (index.get(n, every) for n in "yzx")
        return self.full.at[self.p.c, y, z, x, pl.ds(self.third * t, self.third)]

    def own(self):
        s, p, a, me = self.s, self.p, self.a, self.me
        wait_all(self.na)
        s.o[0:a] = add_up(s.ba[p.z], *(s.za[k] for k in range(3)))
        wait_all(self.nb)
        s.o[a : self.rows] = add_up(s.bb[p.x], *(s.xb[k] for k in range(3)))
        self.mine = pltpu.make_async_copy(s.o, self.full.at[p.c, me["y"], p.z, p.x], s.local)
        self.mine.start()
        self.one = [
            [
                self.push(s.o.at[pl.ds(self.third * t, self.third)], self.view(t, me), self.peer(order[0], k))
                for k in RING4
            ]
            for t, order in enumerate(ORDERS)
        ]

    def without(self, *axes):
        return {n: v for n, v in self.me.items() if n not in axes}

    def start(self, t, index, a, axis):
        low, high = (self.view(t, {**index, a: pl.ds(2 * h, 2)}) for h in range(2))
        right, left = self.peer(axis, 1), self.peer(axis, 3)
        a0 = self.push(low, low, right)
        b0 = self.push(high, high, left)
        return a0, b0, self.push(high, high, right), self.push(low, low, left)

    def forward(self, t, index, a, axis, copies):
        a0, b0, a1, b1 = copies
        a0.wait_recv()
        low = self.view(t, {**index, axis: self.pos(axis, 3), a: pl.ds(0, 2)})
        a2 = self.push(low, low, self.peer(axis, 1))
        b0.wait_recv()
        high = self.view(t, {**index, axis: self.pos(axis, 1), a: pl.ds(2, 2)})
        b2 = self.push(high, high, self.peer(axis, 3))
        wait_all((a1, b1))
        return a2, b2

    def to_core(self, t, index):
        v = self.view(t, index)
        self.core.append(self.push(v, v, self.other))

    def two(self):
        self.mine.wait()
        self.hop = []
        for t, (a, b, _) in enumerate(ORDERS):
            wait_all(self.one[t])
            self.hop.append(self.start(t, self.without(a), a, b))

    def two_forward(self):
        self.last = [self.forward(t, self.without(a), a, b, self.hop[t]) for t, (a, b, _) in enumerate(ORDERS)]

    def three(self, *thirds):
        for t in thirds:
            a, b, c = ORDERS[t]
            wait_all(self.last[t])
            self.hop[t] = self.start(t, self.without(a, b), a, c)
        for t in thirds:
            a, b, c = ORDERS[t]
            self.to_core(t, self.without(a, b))

    def three_forward(self, *thirds):
        for t in thirds:
            a, b, c = ORDERS[t]
            self.last[t] = self.forward(t, self.without(a, b), a, c, self.hop[t])
        for t in thirds:
            c = ORDERS[t][2]
            self.to_core(t, {c: self.pos(c, 1)})
            self.to_core(t, {c: self.pos(c, 3)})

    def three_end(self, *thirds):
        for t in thirds:
            c = ORDERS[t][2]
            wait_all(self.last[t])
            self.to_core(t, {c: self.pos(c, 2)})

    def end(self):
        wait_all(self.core)


class Small(Pushes):
    def __init__(self, R, place, ring):
        super().__init__(R.pool, place, ring, R.trs)
        self.R = R

    def halves(self):
        R = self.R
        for c in range(2):
            R.s0[c] = R.small[:, c * HALF : (c + 1) * HALF].astype(BF16)
        self.now = [self.push(R.s0.at[1 - self.p.c], R.sr, self.other)]

    def along_x(self):
        R = self.R
        wait_all(self.now)
        R.s1[...] = add_up(R.s0[self.p.c], R.sr[...])
        self.now = [self.push(R.s1, R.sx.at[k - 1], self.peer("x", k)) for k in RING4]

    def along_z(self):
        R = self.R
        wait_all(self.now)
        R.s2[...] = add_up(R.s1[...], *(R.sx[k] for k in range(3)))
        self.now = [self.push(R.s2, R.sz.at[k - 1], self.peer("z", k)) for k in RING4]

    def along_y(self):
        R = self.R
        wait_all(self.now)
        own = R.fs.at[self.p.c, self.ring.y]
        own[...] = add_up(R.s2[...], *(R.sz[k] for k in range(3)))
        self.now = [self.push(own, own, self.peer("y", k)) for k in RING4]

    def to_core(self):
        half = self.R.fs.at[self.p.c]
        wait_all(self.now)
        self.now = [self.push(half, half, self.other)]

    def end(self):
        wait_all(self.now)


IN = ("tok", "cot", "gain", "shift", "w_qkv", "qv_bias", "w_out", "out_bias", "w_up", "up_bias", "w_down", "down_bias")
IN = IN + ("router", "e_up", "e_up_bias", "e_down", "e_down_bias", "ids", "pri")


def outputs():
    return dict(
        result=((ROWS, D), F32),
        d_tok=((ROWS, D), F32),
        g_eub=((1, D), F32),
        g_edb=((1, D), F32),
        fs=((2, 4, 48, HALF), BF16),
        g_eup=((D, D), BF16),
        g_edown=((D, D), BF16),
        f13=((2, 2, 4, 4, 4, 48, HALF), BF16),
        f2=((2, 4, 4, 4, 96, HALF), BF16),
    )


def scratch():
    blk, att = (NY, ROWS, D), (NY, ROWS, HW)
    low, wide, sems = (lambda *sh: pltpu.VMEM(sh, BF16)), (lambda *sh: pltpu.VMEM(sh, F32)), pltpu.SemaphoreType.DMA
    n_slots = CAP * NDP
    return dict(
        n=[low(*blk) for _ in range(3)],
        q=[low(*att) for _ in range(2)],
        k=[low(*att) for _ in range(2)],
        v=[low(*att) for _ in range(2)],
        o=[wide(*att) for _ in range(2)],
        st=[wide(NY, ROWS, 128) for _ in range(2)],
        gb=[low(*blk) for _ in range(2)],
        go=low(*att),
        gq=low(*att),
        gk=low(*att),
        gv=low(*att),
        vm=low(HEADS_DEV, NY * ROWS, HW),
        qm=low(HEADS_DEV, NY * ROWS, HW),
        dq=wide(NY * ROWS, HW),
        stt=wide(8, NY * ROWS),
        u=wide(*blk),
        a=low(*blk),
        gu=low(*blk),
        moe=low(NY, 2 * n_slots, D),
        mpart=wide(NY, 2 * n_slots, D),
        msb=low(3, 2 * n_slots, D),
        mrb=low(3, 2 * n_slots, D),
        eb=low(NY, n_slots, D),
        egc=low(NY, n_slots, D),
        ds=low(EXPERTS, 8, D),
        dr=low(2, EXPERTS, 8, D),
        wqkv0g=low(4, 4, 2, 24, 3 * HW),
        wqkv1g=low(4, 4, 2, 24, 3 * HW),
        wupg=low(4, 4, 2, 24, D),
        wqkv0=low(24, 3 * HW),
        wqkv1=low(24, 3 * HW),
        wup=low(24, D),
        woutg=low(4, 2, 2, 24, D),
        wdowng=low(4, 2, 96, D),
        qvb=wide(4, HW),
        wqkv=low(2, 3, D, HW),
        wout=low(2, HW, D),
        up=low(D, D),
        down=low(D, D),
        eu=low(D, D),
        ed=low(D, D),
        geu=low(D, D),
        ged=low(D, D),
        own=sems((4,)),
        xs=wide(4, ROWS, D),
        gs=wide(ROWS, D),
        small=wide(48, D),
        g13=[low(2, 4, 4, 48, HALF) for _ in range(2)],
        g2=low(2, 4, 4, 96, HALF),
        sums=[sum_scratch(r, a) for r, a in ((48, 32), (96, 48), (48, 16))],
        s0=low(2, 48, HALF),
        sr=low(48, HALF),
        s1=low(48, HALF),
        sx=low(3, 48, HALF),
        s2=low(48, HALF),
        sz=low(3, 48, HALF),
        ssem=sems((2, 6)),
        rsem=sems((2, 6)),
        dssem=sems((2,)),
        drsem=sems((2,)),
        pss=sems((64,)),
        wrs=sems((29,)),
        bss=sems((2, 4)),
        trs=sems((11,)),
    )


def kernel(*refs):
    n_in, n_out = len(IN), len(outputs())
    R = types.SimpleNamespace(**dict(zip(IN + tuple(outputs()), refs)), **refs[n_in + n_out])
    R.pool = Pool(R.pss, 64)
    R.sb = R.msb.at[:, pl.ds(0, ROWS)]
    R.rb = R.mrb.at[:, pl.ds(0, ROWS)]
    R.part = R.mpart.at[:, pl.ds(0, ROWS)]
    ring, place = Ring(), Place()
    d = place.d
    barrier = pltpu.get_barrier_semaphore()
    near = [place.at(c=1 - place.c)] + [{"seq": lax.rem(ring.y + k, NY)} for k in RING4]
    near += [place.at(x=lax.rem(place.x + k, 4)) for k in RING4] + [place.at(z=lax.rem(place.z + k, 4)) for k in RING4]
    for to in near:
        pl.semaphore_signal(barrier, inc=1, device_id=to, device_id_type=MESH)
    R.small[...] = jnp.zeros((48, D), F32)
    fetched = [
        pltpu.make_async_copy(src, dst, R.own.at[i]) for i, (src, dst) in enumerate(((R.e_up, R.eu), (R.e_down, R.ed)))
    ]
    stored = [
        pltpu.make_async_copy(src, dst, R.own.at[2 + i])
        for i, (src, dst) in enumerate(((R.geu, R.g_eup), (R.ged, R.g_edown)))
    ]
    for c in fetched:
        c.start()
    w = Weights(R, place, ring)
    w.cut()
    pl.semaphore_wait(barrier, len(near))

    gain = lambda j: R.gain[j : j + 1]
    shift = lambda j: R.shift[j : j + 1]
    xs, gs = R.xs, R.gs
    xs[0] = R.tok[...].astype(F32)
    w.b_along_z(2)
    w.a_along_x(0)
    xs[1] = attn_forward(R, ring, 0, xs[0], gain(0), shift(0), w)
    xs[2] = feed_forward(R, ring, xs[1], gain(1), shift(1), w)
    w.sent()
    xs[3] = attn_forward(R, ring, 1, xs[2], gain(2), shift(2))
    for c in fetched:
        c.wait()
    gs[...] = mixture(R, ring, d, xs[3], gain(3), shift(3))
    for c in stored:
        c.start()

    a1 = Sum(R, place, ring, R.g13[1], R.f13.at[1], R.sums[0])
    ff = Sum(R, place, ring, R.g2, R.f2, R.sums[1])
    a0 = Sum(R, place, ring, R.g13[0], R.f13.at[0], R.sums[2])
    small = Small(R, place, ring)

    def steps(*fs):
        def run():
            for f in fs:
                f()

        return run

    part = functools.partial
    gs[...] = attn_backward(R, ring, 1, xs[2], gain(2), gs[...], 6, {BESIDE: a1.halves, END: a1.first_axis})
    gs[...] = feed_backward(
        R,
        ring,
        xs[1],
        gain(1),
        gs[...],
        8,
        {
            LATE: a1.second_axis,
            BEFORE: a1.own,
            BESIDE: steps(ff.halves, a1.two),
            END: steps(ff.first_axis, a1.two_forward),
        },
    )
    R.d_tok[...] = attn_backward(
        R,
        ring,
        0,
        xs[0],
        gain(0),
        gs[...],
        10,
        {
            BEFORE: steps(ff.second_axis, part(a1.three, 0, 1, 2)),
            MIDDLE: ff.own,
            AFTER: steps(ff.two, part(a1.three_forward, 0, 1, 2)),
            WEIGHTS: a0.halves,
            BESIDE: steps(ff.two_forward, a0.first_axis, part(a1.three_end, 0, 1, 2)),
            END: steps(a0.second_axis, part(ff.three, 0, 1, 2)),
        },
    )
    small.halves()
    a0.own()
    small.along_x()
    a0.two()
    small.along_z()
    a0.two_forward()
    small.along_y()
    a0.three(0, 1, 2)
    ff.three_forward(0, 1, 2)
    small.to_core()
    a0.three_forward(0, 1, 2)
    ff.three_end(0, 1, 2)
    a0.three_end(0, 1, 2)
    for c in stored:
        c.wait()
    for s in (a1, ff, a0, small, R.pool):
        s.end()


def layers(ins):
    vmem, hbm = pl.BlockSpec(memory_space=pltpu.VMEM), pl.BlockSpec(memory_space=pl.ANY)
    out = outputs()
    return dict(
        zip(
            out,
            pl.pallas_call(
                kernel,
                out_shape=[jax.ShapeDtypeStruct(*sh) for sh in out.values()],
                in_specs=[hbm if n in ("e_up", "e_down") else vmem for n in IN],
                out_specs=[vmem] * (len(out) - 4) + [hbm] * 4,
                scratch_shapes=[scratch()],
                compiler_params=pltpu.CompilerParams(
                    collective_id=0, has_side_effects=True, vmem_limit_bytes=62 * 2**20
                ),
                name="layers",
            )(*ins),
        )
    )


def spread(o):
    def body(*refs):
        f_qkv, f_out, f_up, f_down, geu, ged, res, tok, fs, edb, eub = refs[:11]
        qkv, out, up, down, geu_o, ged_o, res_o, tok_o = refs[11:19]
        gain, shift, outb, downb, upb, qvb, router, edb_o, eub_o = refs[19:]
        s = pl.program_id(0)

        @pl.when(s < 12)
        def _():
            qkv[0] = jnp.transpose(f_qkv[0, 0, :, 0].reshape(D, HALF).astype(F32))

        out[0] = f_out[0, 0, 0, 0].reshape(HW, HALF).astype(F32)
        for c in range(2):
            at = pl.ds(c * HALF, HALF)
            up[:, at] = f_up[c, 0, 0].reshape(HW, HALF).astype(F32)
            down[:, at] = f_down[c, 0, 0].reshape(HW, HALF).astype(F32)
        geu_o[...] = geu[...].astype(F32)
        ged_o[...] = ged[...].astype(F32)
        res_o[...] = res[...]
        tok_o[...] = tok[...]

        @pl.when(s == 0)
        def _():
            by_y = [jnp.concatenate([fs[0, y], fs[1, y]], axis=1).astype(F32) for y in range(NY)]
            total = by_y[0] + by_y[1] + by_y[2] + by_y[3]
            gain[...] = total[0:4]
            shift[...] = total[4:8]
            outb[...] = total[8:10]
            for j in range(6):
                downb[j : j + 1] = total[10:11, 128 * j : 128 * (j + 1)]
            router[...] = total[16:48]
            for y in range(NY):
                for j in range(6):
                    upb[6 * y + j : 6 * y + j + 1] = by_y[y][11:12, 128 * j : 128 * (j + 1)]
                for i in range(2):
                    for t in range(2):
                        row = by_y[y][12 + 2 * i + t : 13 + 2 * i + t, 0:HW]
                        qvb[i : i + 1, t * D + y * HW : t * D + (y + 1) * HW] = row
            own = edb[:, 0:HW]
            for y in range(1, NY):
                own = jnp.where(lax.axis_index("seq") == y, edb[:, y * HW : (y + 1) * HW], own)
            edb_o[...] = own
            eub_o[...] = eub[...]

    def qkv_at(s):
        j = jnp.minimum(s, 11)
        return lax.div(j, 6), lax.rem(j, 2), lax.div(lax.rem(j, 6), 2)

    def out_at(s):
        return lax.div(s, 8), lax.rem(lax.div(s, 4), 2), lax.rem(s, 4)

    def feed_at(s, z):
        y, j = lax.div(s, 4), lax.rem(s, 4)
        return 0, y, z + lax.div(j, 2), lax.rem(j, 2), 0, 0

    def qkv_in(s):
        i, c, t = qkv_at(s)
        return i, c, 0, t, 0, 0, 0

    def qkv_out(s):
        i, c, t = qkv_at(s)
        return i, c, t

    def out_in(s):
        i, c, y = out_at(s)
        return i, c, y, 3, 0, 0, 0

    def out_out(s):
        i, c, y = out_at(s)
        return i, y, c

    small = [(4, D), (4, D), (2, D), (6, 128), (24, 128), (2, 2 * D), (EXPERTS, D), (1, HW), (1, D)]
    whole = lambda sh: pl.BlockSpec(sh, lambda s: (0,) * len(sh))
    rows = lambda n, last: pl.BlockSpec((n, D), lambda s: (jnp.minimum(s, last), 0))
    passed = [rows(48, 15), rows(48, 15), rows(16, 8), rows(16, 8)]
    big = [(2, D, 3 * D), (2, D, D), (D, NY * D), (NY * D, D), (D, D), (D, D), (ROWS, D), (ROWS, D)]
    return pl.pallas_call(
        body,
        grid=(16,),
        in_specs=[
            pl.BlockSpec((1, 1, 4, 1, 4, 48, HALF), qkv_in),
            pl.BlockSpec((1, 1, 1, 1, 4, 48, HALF), out_in),
            pl.BlockSpec((2, 1, 1, 2, 96, HALF), lambda s: feed_at(s, 0)),
            pl.BlockSpec((2, 1, 1, 2, 96, HALF), lambda s: feed_at(s, 2)),
        ]
        + passed
        + [whole((2, 4, 48, HALF)), whole((1, D)), whole((1, D))],
        out_specs=[
            pl.BlockSpec((1, HALF, D), qkv_out),
            pl.BlockSpec((1, HW, HALF), out_out),
            pl.BlockSpec((HW, D), lambda s: (lax.rem(s, 4), lax.div(s, 4))),
            pl.BlockSpec((HW, D), lambda s: (s, 0)),
        ]
        + passed
        + [whole(sh) for sh in small],
        out_shape=[jax.ShapeDtypeStruct(sh, F32) for sh in big + small],
        compiler_params=pltpu.CompilerParams(vmem_limit_bytes=62 * 2**20),
        name="spread",
    )(o.f13, o.f13, o.f2, o.f2, o.g_eup, o.g_edown, o.result, o.d_tok, o.fs, o.g_edb, o.g_eub)


def local(
    tokens,
    cotangent,
    ln_gain,
    ln_shift,
    qkv_weight,
    qv_bias,
    out_weight,
    out_bias,
    up_weight,
    up_bias,
    down_weight,
    down_bias,
    router,
    expert_up,
    expert_up_bias,
    expert_down,
    expert_down_bias,
    expert_ids,
    priority,
):
    o = types.SimpleNamespace(
        **layers(
            (
                tokens[0],
                cotangent[0],
                ln_gain,
                ln_shift,
                qkv_weight,
                qv_bias,
                out_weight,
                out_bias,
                up_weight,
                up_bias.reshape(24, 128),
                down_weight,
                down_bias.reshape(6, 128),
                router.T,
                expert_up[0],
                expert_up_bias,
                expert_down[0],
                expert_down_bias,
                expert_ids[0].T,
                priority[0].T,
            )
        )
    )
    g_qkv, g_out, g_up, g_down, geu, ged, res, tok, *small = spread(o)
    gain, shift, outb, downb, upb, qvb, g_router, edb, eub = small
    return (
        res[None],
        tok[None],
        gain,
        shift,
        g_qkv,
        qvb,
        g_out,
        outb,
        g_up,
        upb.reshape(NY * D),
        g_down,
        downb.reshape(D),
        g_router.T,
        geu[None],
        eub,
        ged[None],
        edb,
    )


def solution(mesh):
    in_specs = (
        P("dp", "seq", None),
        P("dp", "seq", None),
        P(),
        P(),
        P(None, "dp", None),
        P(),
        P(None, "dp", None),
        P(),
        P("dp", None),
        P(),
        P("dp", None),
        P(),
        P(),
        P("dp", None, "seq"),
        P("dp", "seq"),
        P("dp", "seq", None),
        P("dp", None),
        P("dp", "seq", None),
        P("dp", "seq", None),
    )
    out_specs = (
        P("dp", "seq", None),
        P("dp", "seq", None),
        P(),
        P(),
        P(),
        P(),
        P(),
        P(),
        P(),
        P(),
        P(),
        P(),
        P(),
        P("dp", None, "seq"),
        P("dp", "seq"),
        P("dp", "seq", None),
        P("dp", "seq"),
    )
    return jax.shard_map(local, mesh=mesh, in_specs=in_specs, out_specs=out_specs, check_vma=False)
```

```python
import functools
import types

import jax
import jax.numpy as jnp
from jax import lax
from jax.experimental import pallas as pl
from jax.experimental.pallas import tpu as pltpu
from jax.sharding import PartitionSpec as P

MESH = pl.DeviceIdType.MESH
F32, BF16 = jnp.float32, jnp.bfloat16

D = 768
HEADS_DEV = 3
HW = 192
ROWS = 144
NY = 4
NDP = 32
EXPERTS = 32
CAP = 4
EPS = 1e-06
LO, HI = 80, 64
HALF = D // 2

NN = (((1,), (0,)), ((), ()))
RING4 = (1, 2, 3)
NT = (((1,), (1,)), ((), ()))
TN = (((0,), (0,)), ((), ()))


def mm(a, b, dims=NN):
    return lax.dot_general(a, b, dims, preferred_element_type=F32)


def ln_stats(x):
    mean = jnp.mean(x, axis=-1, keepdims=True)
    cen = x - mean
    rstd = lax.rsqrt(jnp.mean(cen * cen, axis=-1, keepdims=True) + EPS)
    return cen * rstd, rstd


def ln_forward(x, gain, shift):
    nhat, _ = ln_stats(x)
    return nhat * gain + shift


def ln_backward(x, gain, grad):
    nhat, rstd = ln_stats(x)
    d_gain = jnp.sum(grad * nhat, axis=0, keepdims=True)
    d_shift = jnp.sum(grad, axis=0, keepdims=True)
    gg = grad * gain
    dx = rstd * (
        gg
        - jnp.mean(gg, axis=-1, keepdims=True)
        - nhat * jnp.mean(gg * nhat, axis=-1, keepdims=True)
    )
    return dx, d_gain, d_shift


GC = 0.7978845608028654
GA = 0.044715


def gelu_both(u):
    sq = u * u
    t = jnp.tanh(GC * u * (1.0 + GA * sq))
    half = 0.5 * (1.0 + t)
    slope = half + 0.5 * u * (1.0 - t * t) * (GC * (1.0 + 3.0 * GA * sq))
    return u * half, slope


class Ring:
    def __init__(self):
        self.y = lax.axis_index("seq")
        self.right = lax.rem(self.y + 1, NY)
        self.left = lax.rem(self.y + 3, NY)
        self.opp = lax.rem(self.y + 2, NY)


def send(src, dst, ss, rs, i, to):
    c = pltpu.make_async_remote_copy(
        src_ref=src,
        dst_ref=dst,
        send_sem=ss.at[i],
        recv_sem=rs.at[i],
        device_id={"seq": to},
        device_id_type=MESH,
    )
    c.start()
    return c


def gather_start(ring, buf, lo, hi, ss, rs):
    y, low, high = ring.y, pl.ds(0, lo), pl.ds(lo, hi)
    a0 = send(buf.at[y, low], buf.at[y, low], ss, rs, 0, ring.right)
    b0 = send(buf.at[y, high], buf.at[y, high], ss, rs, 1, ring.left)
    a1 = send(buf.at[y, high], buf.at[y, high], ss, rs, 2, ring.right)
    b1 = send(buf.at[y, low], buf.at[y, low], ss, rs, 3, ring.left)
    return a0, b0, a1, b1


def gather_forward(ring, buf, lo, hi, ss, rs, copies):
    a0, b0, a1, b1 = copies
    low, high = pl.ds(0, lo), pl.ds(lo, hi)
    a0.wait_recv()
    a2 = send(buf.at[ring.left, low], buf.at[ring.left, low], ss, rs, 4, ring.right)
    b0.wait_recv()
    b2 = send(buf.at[ring.right, high], buf.at[ring.right, high], ss, rs, 5, ring.left)
    a1.wait_recv()
    b1.wait_recv()
    return a2, b2


def nothing():
    pass


def gather_blocks(ring, buf, lo, hi, ss, rs, use, early=nothing, late=nothing):
    first = gather_start(ring, buf, lo, hi, ss, rs)
    early()
    use(ring.y)
    last = gather_forward(ring, buf, lo, hi, ss, rs, first)

    def near(i, carry):
        use(lax.rem(ring.y + 1 + 2 * i, NY))
        return carry

    lax.fori_loop(0, 2, near, 0)
    late()
    for c in last:
        c.wait_recv()
    use(ring.opp)
    for c in first + last:
        c.wait_send()


class Scatter:
    def __init__(self, ring, part, lo, hi, sbuf, rbuf, ss, rs):
        self.ring, self.part, self.sbuf, self.rbuf, self.ss, self.rs = ring, part, sbuf, rbuf, ss, rs
        self.low, self.high = pl.ds(0, lo), pl.ds(lo, hi)
        self.all = []

    def send(self, slot, rows, right):
        i = len(self.all)
        to = self.ring.right if right else self.ring.left
        c = send(self.sbuf.at[slot, rows], self.rbuf.at[slot, rows], self.ss, self.rs, i, to)
        self.all.append(c)
        return c

    def near(self, right):
        slot, rows, j = (1, self.high, self.ring.right) if right else (2, self.low, self.ring.left)
        self.sbuf[slot, rows] = self.part[j, rows].astype(BF16)
        self.send(slot, rows, right)

    def opposite(self):
        self.sbuf[0] = self.part[self.ring.opp].astype(BF16)
        self.over = self.send(0, self.low, True), self.send(0, self.high, False)

    def onward(self):
        for c, slot, rows, j, right in (
            (self.over[0], 1, self.low, self.ring.right, True),
            (self.over[1], 2, self.high, self.ring.left, False),
        ):
            c.wait_recv()
            self.sbuf[slot, rows] = (self.part[j, rows] + self.rbuf[0, rows].astype(F32)).astype(BF16)
            self.send(slot, rows, right)

    def end(self):
        for c in self.all:
            if all(c is not o for o in self.over):
                c.wait_recv()
        total = self.part[self.ring.y] + self.rbuf[1].astype(F32) + self.rbuf[2].astype(F32)
        for c in self.all:
            c.wait_send()
        return total


def pass_through(ring, buf, sc, lo, hi, ss, rs, use, early=nothing, late=nothing, beside=nothing):
    first = gather_start(ring, buf, lo, hi, ss, rs)
    early()
    use(ring.y)
    last = gather_forward(ring, buf, lo, hi, ss, rs, first)

    def near(i, carry):
        use(lax.rem(ring.y + 1 + 2 * i, NY))
        return carry

    lax.fori_loop(0, 2, near, 0)
    sc.near(True)
    sc.near(False)
    late()
    for c in last:
        c.wait_recv()
    use(ring.opp)
    sc.opposite()
    for c in first + last:
        c.wait_send()
    sc.onward()
    beside()
    return sc.end()


def swap_all(d, sbuf, rbuf, ssem, rsem):
    def start(k, carry):
        to = lax.rem(d + k, NDP)
        push(sbuf.at[to], rbuf.at[d], ssem, rsem, {"dp": to})
        return carry

    lax.fori_loop(1, NDP, start, 0)
    rbuf[d] = sbuf[d]
    for buf, sem in ((sbuf, ssem), (rbuf, rsem)):
        others = buf.at[pl.ds(0, NDP - 1)]
        pltpu.make_async_copy(others, others, sem).wait()


class Place:
    def __init__(self):
        d = lax.axis_index("dp")
        self.d = d
        self.z, self.x, self.c = lax.div(d, 8), lax.rem(lax.div(d, 2), 4), lax.rem(d, 2)

    def at(self, z=None, x=None, c=None):
        z, x, c = (m if v is None else v for v, m in ((z, self.z), (x, self.x), (c, self.c)))
        return {"dp": (z * 4 + x) * 2 + c}


class Pool:
    def __init__(self, sems, size):
        self.sems, self.size, self.copies = sems, size, []

    def push(self, src, dst, rsem, to):
        n = len(self.copies)
        if n >= self.size:
            self.copies[n - self.size].wait_send()
        c = push(src, dst, self.sems.at[n % self.size], rsem, to)
        self.copies.append(c)
        return c

    def end(self):
        for c in self.copies[-self.size :]:
            c.wait_send()


def push(src, dst, ssem, rsem, to):
    c = pltpu.make_async_remote_copy(
        src_ref=src, dst_ref=dst, send_sem=ssem, recv_sem=rsem, device_id=to, device_id_type=MESH
    )
    c.start()
    return c


def across(v, sel):
    hi = v.astype(BF16)
    rest = v.astype(F32) - hi.astype(F32)
    mid = rest.astype(BF16)
    return mm(hi, sel) + mm(mid, sel) + mm((rest - mid.astype(F32)).astype(BF16), sel)


class Weights:
    def __init__(self, R, place, ring):
        self.R, self.p, self.ring = R, place, ring
        self.own = (R.wqkv0, R.wup, R.w_out, R.w_down, R.wqkv1)
        self.got = (R.wqkv0g, R.wupg, R.woutg, R.wdowng, R.wqkv1g)
        self.now = {}
        self.next = 0

    def push(self, src, dst, to):
        i = self.next
        self.next += 1
        return self.R.pool.push(src, dst, self.R.wrs.at[i], to)

    def cut(self):
        R, y = self.R, self.ring.y
        sel = one_hot(iota((D, HW), 0) == iota((D, HW), 1) + HW * y)
        for t in range(3):
            at = pl.ds(t * HW, HW)
            R.wqkv0[:, at] = mm(R.w_qkv[0, :, t * D : (t + 1) * D], sel).astype(BF16)
            R.wqkv1[:, at] = mm(R.w_qkv[1, :, t * D : (t + 1) * D], sel).astype(BF16)
        R.wup[...] = R.w_up[:, pl.ds(pl.multiple_of(D * y, D), D)]
        for t in range(2):
            R.qvb[2 * t : 2 * t + 2] = across(R.qv_bias[:, t * D : (t + 1) * D], sel)

    def a_along_x(self, n):
        p, buf = self.p, self.got[n]
        self.now[n] = [
            self.push(self.own[n], buf.at[p.z, p.x, p.c], p.at(x=lax.rem(p.x + k, 4))) for k in RING4
        ]
        buf[p.z, p.x, p.c] = self.own[n][...]

    def wait(self, n):
        for c in self.now[n]:
            c.wait_recv()

    def a_along_z(self, n):
        p, buf = self.p, self.got[n]
        self.wait(n)
        row = buf.at[p.z, :, p.c]
        self.now[n] = [self.push(row, row, p.at(z=lax.rem(p.z + k, 4))) for k in RING4]

    def a_along_core(self, n):
        p = self.p
        self.wait(n)
        half = self.got[n].at[:, :, p.c]
        self.now[n] = [self.push(half, half, p.at(c=1 - p.c))]

    def b_copy(self, n, k):
        p, R = self.p, self.R
        return pltpu.make_async_remote_copy(
            src_ref=self.own[n],
            dst_ref=self.got[n].at[p.x, p.c],
            send_sem=R.bss.at[n - 2, k],
            recv_sem=R.bss.at[n - 2, 0],
            device_id=p.at(z=lax.rem(p.z + k, 4)),
            device_id_type=MESH,
        )

    def b_along_z(self, n):
        @pl.when(self.p.z == self.ring.y)
        def _():
            for k in RING4:
                self.b_copy(n, k).start()
            self.got[n][self.p.x, self.p.c] = self.own[n][...]

    def b_along_x(self, n):
        p = self.p

        @pl.when(p.z != self.ring.y)
        def _():
            self.b_copy(n, 1).wait_recv()

        own = self.got[n].at[p.x, p.c]
        self.now[n] = [self.push(own, own, p.at(x=lax.rem(p.x + k, 4))) for k in RING4]

    def b_along_core(self, n):
        p = self.p
        self.wait(n)
        half = self.got[n].at[:, p.c]
        self.now[n] = [self.push(half, half, p.at(c=1 - p.c))]

    def sent(self):
        @pl.when(self.p.z == self.ring.y)
        def _():
            for n in (2, 3):
                for k in RING4:
                    self.b_copy(n, k).wait_send()

    def lay(self, n):
        R = self.R
        self.wait(n)

        def one(j, carry):
            rows = pl.ds(pl.multiple_of(192 * j, 192), 192)
            v = self.got[n][j].astype(F32)
            if n in (0, 4):
                v = v.reshape(192, 3 * HW).astype(BF16)
                for t in range(3):
                    R.wqkv[n // 4, t, rows] = v[:, t * HW : (t + 1) * HW]
            elif n == 1:
                R.up[rows] = v.reshape(192, D).astype(BF16)
            elif n == 2:
                for i in range(2):
                    R.wout[i, pl.ds(pl.multiple_of(48 * j, 48), 48)] = v[:, i].reshape(48, D).astype(BF16)
            else:
                R.down[rows] = v.reshape(192, D).astype(BF16)
            return carry

        lax.fori_loop(0, 4, one, 0)


def head_mask(h, dtype):
    lane = lax.broadcasted_iota(jnp.int32, (1, HW), 1)
    return ((lane >= 64 * h) & (lane < 64 * (h + 1))).astype(dtype)


def keep_grad(ref, first, grad):
    depth = ref.shape[3]
    count = grad.shape[0] // (4 * depth)
    low = grad.astype(BF16)
    for c in range(2):
        half = low[:, c * HALF : (c + 1) * HALF].reshape(count, 4, depth, HALF)
        ref[c, first : first + count] = half


def flat(ref):
    v = ref[...]
    return v.reshape(v.shape[0] * v.shape[1], v.shape[2])


def attn_forward(R, ring, i, x, gain, shift, w=None):
    nbuf, q, k, v, o, st = R.n[2 * i], R.q[i], R.k[i], R.v[i], R.o[i], R.st[i]
    wqkv, wout, qvb, part, vm = R.wqkv, R.wout, R.qvb, R.part, R.vm
    nbuf[ring.y] = ln_forward(x, gain, shift).astype(BF16)

    def project(j):
        nj = nbuf[j]
        q[j] = ((mm(nj, wqkv[i, 0]) + qvb[i : i + 1]).astype(BF16).astype(F32) * 0.125).astype(BF16)
        k[j] = mm(nj, wqkv[i, 1]).astype(BF16)
        v[j] = (mm(nj, wqkv[i, 2]) + qvb[2 + i : 3 + i]).astype(BF16)

    def early():
        w.a_along_z(0)
        w.b_along_x(2)
        w.a_along_x(1)
        w.a_along_core(0)
        w.a_along_z(1)
        w.b_along_z(3)
        w.lay(0)

    gather_blocks(ring, nbuf, LO, HI, R.ssem.at[0], R.rsem.at[0], project, nothing if w is None else early)
    if w is not None:
        w.b_along_core(2)
    v_all = flat(v)
    for h in range(HEADS_DEV):
        vm[h] = v_all * head_mask(h, BF16)
    k_all = flat(k)

    def rows(b):
        qb = q[b]
        acc = jnp.zeros((ROWS, HW), F32)
        stats = jnp.zeros((ROWS, 128), F32)
        lane = lax.broadcasted_iota(jnp.int32, (ROWS, 128), 1)
        for h in range(HEADS_DEV):
            s = mm(qb * head_mask(h, BF16), k_all, NT)
            top = jnp.max(s, axis=-1, keepdims=True)
            e = jnp.exp(s - top)
            tot = jnp.sum(e, axis=-1, keepdims=True)
            acc = acc + mm(e.astype(BF16), vm[h]) * (1.0 / tot)
            stats = jnp.where(lane == h, top + jnp.log(tot), stats)
        o[b] = acc
        st[b] = stats
        part[b] = mm(acc.astype(BF16), wout[i])

    if w is not None:
        w.lay(2)
    sc = Scatter(ring, part, LO, HI, R.sb, R.rb, R.ssem.at[1], R.rsem.at[1])
    rows(ring.opp)
    sc.opposite()

    def near(t, carry):
        rows(lax.rem(ring.y + 1 + 2 * t, NY))
        return carry

    lax.fori_loop(0, 2, near, 0)
    sc.near(True)
    sc.near(False)
    if w is not None:
        w.b_along_x(3)
        w.a_along_core(1)
        w.a_along_x(4)
    sc.onward()
    rows(ring.y)
    if w is not None:
        w.b_along_core(3)
        w.a_along_z(4)
    total = sc.end()
    if w is not None:
        w.lay(1)
        w.lay(3)
    return x + total + R.out_bias[i : i + 1]


EARLY, LATE, BEFORE, MIDDLE, AFTER, WEIGHTS, BESIDE, END = range(8)


def attn_backward(R, ring, i, x, gain, grad, slot, hooks):
    nbuf, q, k, v, o, st = R.n[2 * i], R.q[i], R.k[i], R.v[i], R.o[i], R.st[i]
    wqkv, wout, part = R.wqkv, R.wout, R.part
    gb, go, gm, qm, gq, gk, gv, dq = R.gb[slot // 2 % 2], R.go, R.vm, R.qm, R.gq, R.gk, R.gv, R.dq
    low = grad.astype(BF16)
    gb[ring.y] = low
    R.small[pl.ds(8 + i, 1)] = jnp.sum(low.astype(F32), axis=0, keepdims=True)

    def project(j):
        g = mm(gb[j], wout[i], NT).astype(BF16)
        go[j] = g
        prod = g.astype(F32) * o[j]
        stats = st[j]
        lane = lax.broadcasted_iota(jnp.int32, (ROWS, 128), 1)
        for h in range(HEADS_DEV):
            inner = jnp.sum(prod * head_mask(h, F32), axis=-1, keepdims=True)
            stats = jnp.where(lane == 4 + h, inner, stats)
        st[j] = stats

    at = hooks.get
    gather_blocks(
        ring, gb, LO, HI, R.ssem.at[0], R.rsem.at[0], project, at(EARLY, nothing), at(LATE, nothing)
    )
    at(BEFORE, nothing)()
    go_all, q_all = flat(go), flat(q)
    for h in range(HEADS_DEV):
        gm[h] = go_all * head_mask(h, BF16)
        qm[h] = q_all * head_mask(h, BF16)
    stats_t = jnp.transpose(flat(st))
    R.stt[...] = stats_t[0:8]
    dq[...] = jnp.zeros((NY * ROWS, HW), F32)

    def keys(b, carry):
        kb, vb = k[b], v[b]
        dk = jnp.zeros((ROWS, HW), F32)
        dv = jnp.zeros((ROWS, HW), F32)
        for h in range(HEADS_DEV):
            kh = kb * head_mask(h, BF16)
            p = jnp.exp(mm(kh, qm[h], NT) - R.stt[h : h + 1])
            dp = mm(vb, gm[h], NT)
            ds = (p * (dp - R.stt[4 + h : 5 + h])).astype(BF16)
            dv = dv + mm(p.astype(BF16), gm[h])
            dk = dk + mm(ds, qm[h])
            dq[...] += mm(ds, kh, TN)
        gk[b] = dk.astype(BF16)
        gv[b] = dv.astype(BF16)
        return carry

    lax.fori_loop(0, 2, keys, 0)
    at(MIDDLE, nothing)()
    lax.fori_loop(2, NY, keys, 0)
    at(AFTER, nothing)()
    gq[...] = (dq[...] * 0.125).astype(BF16).reshape(NY, ROWS, HW)

    def back(b):
        part[b] = mm(gq[b], wqkv[i, 0], NT) + mm(gk[b], wqkv[i, 1], NT) + mm(gv[b], wqkv[i, 2], NT)

    def weights():
        n_all, grads = flat(nbuf), R.g13[i]
        for t, g in enumerate((gq, gk, gv)):
            g_all = flat(g)
            keep_grad(grads, t, mm(g_all, n_all, TN))
            if t != 1:
                row = 12 + 2 * i + t // 2
                R.small[row : row + 1, 0:HW] = jnp.sum(g_all.astype(F32), axis=0, keepdims=True)
        keep_grad(grads, 3, mm(flat(o).astype(BF16), flat(gb), TN))

    if WEIGHTS in hooks:
        weights()
        hooks[WEIGHTS]()
    sc = Scatter(ring, part, LO, HI, R.sb, R.rb, R.ssem.at[1], R.rsem.at[1])
    back(ring.opp)
    sc.opposite()

    def near(t, carry):
        back(lax.rem(ring.y + 1 + 2 * t, NY))
        return carry

    lax.fori_loop(0, 2, near, 0)
    sc.near(True)
    sc.near(False)
    sc.onward()
    back(ring.y)
    if WEIGHTS not in hooks:
        weights()
    at(BESIDE, nothing)()
    total = sc.end()
    at(END, nothing)()
    dx, d_gain, d_shift = ln_backward(x, gain, total)
    R.small[pl.ds(2 * i, 1)] = d_gain
    R.small[pl.ds(4 + 2 * i, 1)] = d_shift
    return grad + dx


def across_rows(ref, n):
    return jnp.concatenate([ref[6 * n + j : 6 * n + j + 1] for j in range(6)], axis=1)


def feed_forward(R, ring, x, gain, shift, w):
    nbuf, u, a, part = R.n[1], R.u, R.a, R.part
    nbuf[ring.y] = ln_forward(x, gain, shift).astype(BF16)
    bias = across_rows(R.up_bias, 0)
    for y in range(1, NY):
        bias = jnp.where(ring.y == y, across_rows(R.up_bias, y), bias)

    def use(j):
        uj = mm(nbuf[j], R.up[...]) + bias
        act, slope = gelu_both(uj)
        u[j] = slope
        aj = act.astype(BF16)
        a[j] = aj
        part[j] = mm(aj, R.down[...])

    sc = Scatter(ring, part, LO, HI, R.sb, R.rb, R.ssem.at[1], R.rsem.at[1])
    core, lay = functools.partial(w.a_along_core, 4), functools.partial(w.lay, 4)
    total = pass_through(ring, nbuf, sc, LO, HI, R.ssem.at[0], R.rsem.at[0], use, late=core, beside=lay)
    return x + total + across_rows(R.down_bias, 0)


def feed_backward(R, ring, x, gain, grad, slot, hooks):
    nbuf, u, a, part, gb, gu = R.n[1], R.u, R.a, R.part, R.gb[slot // 2 % 2], R.gu
    low = grad.astype(BF16)
    gb[ring.y] = low
    R.small[10:11] = jnp.sum(low.astype(F32), axis=0, keepdims=True)

    def use(j):
        g = (mm(gb[j], R.down[...], NT) * u[j]).astype(BF16)
        gu[j] = g
        part[j] = mm(g, R.up[...], NT)

    at = hooks.get

    def beside():
        at(BEFORE, nothing)()
        n_all, g_all, a_all, gb_all = flat(nbuf), flat(gu), flat(a), flat(gb)
        keep_grad(R.g2, 0, mm(n_all, g_all, TN))
        keep_grad(R.g2, 2, mm(a_all, gb_all, TN))
        R.small[11:12] = jnp.sum(g_all.astype(F32), axis=0, keepdims=True)
        at(BESIDE, nothing)()

    sc = Scatter(ring, part, LO, HI, R.sb, R.rb, R.ssem.at[1], R.rsem.at[1])
    total = pass_through(
        ring,
        gb,
        sc,
        LO,
        HI,
        R.ssem.at[0],
        R.rsem.at[0],
        use,
        at(EARLY, nothing),
        at(LATE, nothing),
        beside,
    )
    at(END, nothing)()
    dx, d_gain, d_shift = ln_backward(x, gain, total)
    R.small[1:2] = d_gain
    R.small[5:6] = d_shift
    return grad + dx


def iota(shape, dim):
    return lax.broadcasted_iota(jnp.int32, shape, dim)


def slot_ids(shape, dim):
    r = iota(shape, dim)
    e, t = r >> 3, r & 7
    z = jnp.where(t < 4, e * 4 + t, -1)
    g = jnp.where(t >= 4, e * 4 + t - 4, -1)
    return z.astype(F32), g.astype(F32)


def one_hot(cond):
    return jnp.where(cond, 1.0, 0.0).astype(BF16)


def mixture(R, ring, d, x, gain, shift):
    low = ln_forward(x, gain, shift).astype(BF16)
    cot = R.cot[...].astype(F32)
    logits = mm(low, R.router[...], NT)

    idr, prr = R.ids[...], R.pri[...]
    digits = jnp.concatenate([idr, prr >> 8, prr & 255], axis=0).astype(F32).astype(BF16)
    turned = mm(one_hot(iota((ROWS, ROWS), 0) == iota((ROWS, ROWS), 1)), digits, NT)
    idc = turned[:, 0:2].astype(jnp.int32)
    prc = (turned[:, 2:4] * 256.0 + turned[:, 4:6]).astype(jnp.int32)
    key_c, key_r = [], []
    for k in range(2):
        key_c.append(prc[:, k : k + 1] * (2 * ROWS) + 2 * iota((ROWS, 1), 0) + k)
        key_r.append(prr[k : k + 1, :] * (2 * ROWS) + 2 * iota((1, ROWS), 1) + k)
    rank_c = [jnp.zeros((ROWS, 1), F32) for _ in range(2)]
    rank_r = [jnp.zeros((1, ROWS), F32) for _ in range(2)]
    for k in range(2):
        for j in range(2):
            same = idc[:, k : k + 1] == idr[j : j + 1, :]
            before = key_r[j] < key_c[k]
            after = key_c[k] < key_r[j]
            rank_c[k] = rank_c[k] + jnp.sum(jnp.where(same & before, 1.0, 0.0), axis=1, keepdims=True)
            rank_r[j] = rank_r[j] + jnp.sum(jnp.where(same & after, 1.0, 0.0), axis=0, keepdims=True)
    kept = [jnp.where(r < CAP, 1.0, 0.0) for r in rank_c]
    slot_c = [jnp.where(rank_c[k] < CAP, idc[:, k : k + 1].astype(F32) * CAP + rank_c[k], 1000.0) for k in range(2)]
    slot_r = [jnp.where(rank_r[k] < CAP, idr[k : k + 1, :].astype(F32) * CAP + rank_r[k], 1000.0) for k in range(2)]

    picks = [jnp.where(iota((ROWS, EXPERTS), 1) == idc[:, k : k + 1], 1.0, 0.0) for k in range(2)]
    chosen = [jnp.sum(logits * p, axis=-1, keepdims=True) for p in picks]
    top = jnp.maximum(chosen[0], chosen[1])
    ex = [jnp.exp(c - top) for c in chosen]
    gates = [e / (ex[0] + ex[1]) for e in ex]

    zid, gid = slot_ids((8 * EXPERTS, ROWS), 0)
    rows = mm(one_hot((zid == slot_r[0]) | (zid == slot_r[1])), low)
    for k in range(2):
        rows = rows + mm(one_hot(gid == slot_r[k]), (gates[k] * cot).astype(BF16))
    R.ds[...] = rows.reshape(EXPERTS, 8, D).astype(BF16)
    swap_all(d, R.ds, R.dr.at[0], R.dssem.at[0], R.drsem.at[0])

    n_slots = CAP * NDP
    back = iota((2 * n_slots, 2 * n_slots), 0)
    col = iota((2 * n_slots, 2 * n_slots), 1)
    s = back & (n_slots - 1)
    src = (s >> 2) * 8 + (s & 3) + jnp.where(back >= n_slots, 4, 0)
    sort = one_hot(src == col)
    arrived = R.dr[0].astype(F32).reshape(2 * n_slots, D).astype(BF16)
    moe = R.moe
    moe[ring.y] = mm(sort, arrived).astype(BF16)
    part = R.mpart

    def use(j):
        z, gy = moe[j, 0:n_slots], moe[j, n_slots : 2 * n_slots]
        c = mm(z, R.eu[...]) + R.e_up_bias[...].astype(F32)
        act, slope = gelu_both(c)
        b = act.astype(BF16)
        R.eb[j] = b
        gc = (slope * mm(gy, R.ed[...], NT)).astype(BF16)
        R.egc[j] = gc
        part[j, 0:n_slots] = mm(b, R.ed[...])
        part[j, n_slots : 2 * n_slots] = mm(gc, R.eu[...], NT)

    def beside():
        z_all = moe[:, 0:n_slots].reshape(NY * n_slots, D)
        gy_all = moe[:, n_slots : 2 * n_slots].reshape(NY * n_slots, D)
        b_all, gc_all = flat(R.eb), flat(R.egc)
        R.geu[...] = mm(z_all, gc_all, TN).astype(BF16)
        R.ged[...] = mm(b_all, gy_all, TN).astype(BF16)
        R.g_eub[...] = jnp.sum(gc_all.astype(F32), axis=0, keepdims=True)
        R.g_edb[...] = jnp.sum(gy_all.astype(F32), axis=0, keepdims=True)

    sc = Scatter(ring, part, n_slots, n_slots, R.msb, R.mrb, R.ssem.at[1], R.rsem.at[1])
    total = pass_through(ring, moe, sc, n_slots, n_slots, R.ssem.at[0], R.rsem.at[0], use, beside=beside)
    is_y = jnp.where(iota((2 * n_slots, 1), 0) < n_slots, 1.0, 0.0)
    total = (total + is_y * R.e_down_bias[...]).astype(BF16)
    unsort = one_hot((col & (n_slots - 1)) * 2 - (col & 3) + jnp.where(col >= n_slots, 4, 0) == back)
    R.ds[...] = mm(unsort, total).reshape(NDP, 8, D).astype(BF16)
    swap_all(d, R.ds, R.dr.at[1], R.dssem.at[1], R.drsem.at[1])
    came = R.dr[1].astype(F32).reshape(8 * EXPERTS, D).astype(BF16)

    zid, gid = slot_ids((ROWS, 8 * EXPERTS), 1)
    result = x
    grad_gate = []
    for k in range(2):
        taken = mm(one_hot(zid == slot_c[k]), came)
        result = result + (gates[k] * kept[k]) * taken
        grad_gate.append(kept[k] * jnp.sum(taken * cot, axis=-1, keepdims=True))
    R.result[...] = result
    inner = gates[0] * grad_gate[0] + gates[1] * grad_gate[1]
    gl = sum(gates[k] * (grad_gate[k] - inner) * picks[k] for k in range(2))
    gl_hi = gl.astype(BF16)
    rest = gl - gl_hi.astype(F32)
    gl_mid = rest.astype(BF16)
    gl_lo = (rest - gl_mid.astype(F32)).astype(BF16)
    grad_low = mm(one_hot((gid == slot_c[0]) | (gid == slot_c[1])), came)
    g_router = jnp.zeros((EXPERTS, D), F32)
    for piece in (gl_hi, gl_mid, gl_lo):
        grad_low = grad_low + mm(piece, R.router[...])
        g_router = g_router + mm(piece, low, TN)
    R.small[16 : 16 + EXPERTS] = g_router
    dx, d_gain, d_shift = ln_backward(x, gain, grad_low)
    R.small[3:4] = d_gain
    R.small[7:8] = d_shift
    return cot + dx


ORDERS = ("zxy", "xyz", "yzx")


def sum_scratch(r, a):
    low, sems = (lambda *sh: pltpu.VMEM(sh, BF16)), pltpu.SemaphoreType.DMA
    b = r - a
    return dict(
        r=low(4, 4, r, HALF),
        xa=low(3, 4, a, HALF),
        zb=low(3, 4, b, HALF),
        ba=low(4, a, HALF),
        bb=low(4, b, HALF),
        za=low(3, a, HALF),
        xb=low(3, b, HALF),
        o=low(r, HALF),
        rs=sems((62,)),
        local=sems,
    )


def wait_all(copies):
    for c in copies:
        c.wait_recv()


def add_up(first, *rest):
    total = first.astype(F32)
    for r in rest:
        total = total + r.astype(F32)
    return total.astype(BF16)


class Pushes:
    def __init__(self, pool, place, ring, rs):
        self.pool, self.p, self.ring, self.rs = pool, place, ring, rs
        self.next = 0
        self.other = place.at(c=1 - place.c)
        self.me = dict(x=place.x, y=ring.y, z=place.z)

    def push(self, src, dst, to):
        i = self.next
        self.next += 1
        return self.pool.push(src, dst, self.rs.at[i], to)

    def push_three(self, axis, source, landing):
        sem = self.rs.at[self.next]
        self.next += 1
        for k in RING4:
            self.pool.push(source(self.pos(axis, k)), landing.at[k - 1], sem, self.peer(axis, k))
        return lambda: pltpu.make_async_copy(landing, landing, sem).wait()

    def pos(self, axis, k=0):
        return lax.rem(self.me[axis] + k, 4)

    def peer(self, axis, k):
        at = self.pos(axis, k)
        return {"seq": at} if axis == "y" else self.p.at(**{axis: at})


class Sum(Pushes):
    def __init__(self, R, place, ring, grad, full, scr):
        s = types.SimpleNamespace(**scr)
        super().__init__(R.pool, place, ring, s.rs)
        self.s, self.grad, self.full = s, grad, full
        self.rows = grad.shape[3]
        self.a = s.ba.shape[1]
        self.third = self.rows // 3

    def halves(self):
        self.halved = self.push(self.grad.at[1 - self.p.c], self.s.r, self.other)
        self.core = []

    def first_axis(self):
        s, p, a = self.s, self.p, self.a
        self.halved.wait_recv()

        def add(z, carry):
            s.r[z] = add_up(self.grad[p.c, z], s.r[z])
            return carry

        lax.fori_loop(0, 4, add, 0)
        top, rest = pl.ds(0, a), pl.ds(a, self.rows - a)
        self.na = self.push_three("x", lambda j: s.r.at[:, j, top], s.xa)
        self.nb = self.push_three("z", lambda j: s.r.at[j, :, rest], s.zb)

    def second_axis(self):
        s, p, a = self.s, self.p, self.a
        self.na()
        s.ba[...] = add_up(s.r[:, p.x, 0:a], *(s.xa[k] for k in range(3)))
        self.na = self.push_three("z", lambda j: s.ba.at[j], s.za)
        self.nb()
        s.bb[...] = add_up(s.r[p.z, :, a : self.rows], *(s.zb[k] for k in range(3)))
        self.nb = self.push_three("x", lambda j: s.bb.at[j], s.xb)

    def view(self, t, index):
        every = pl.ds(0, 4)
        y, z, x = (index.get(n, every) for n in "yzx")
        return self.full.at[self.p.c, y, z, x, pl.ds(self.third * t, self.third)]

    def own(self):
        s, p, a, me = self.s, self.p, self.a, self.me
        self.na()
        s.o[0:a] = add_up(s.ba[p.z], *(s.za[k] for k in range(3)))
        self.nb()
        s.o[a : self.rows] = add_up(s.bb[p.x], *(s.xb[k] for k in range(3)))
        self.mine = pltpu.make_async_copy(s.o, self.full.at[p.c, me["y"], p.z, p.x], s.local)
        self.mine.start()
        self.one = [
            [
                self.push(s.o.at[pl.ds(self.third * t, self.third)], self.view(t, me), self.peer(order[0], k))
                for k in RING4
            ]
            for t, order in enumerate(ORDERS)
        ]

    def without(self, *axes):
        return {n: v for n, v in self.me.items() if n not in axes}

    def start(self, t, index, a, axis):
        low, high = (self.view(t, {**index, a: pl.ds(2 * h, 2)}) for h in range(2))
        right, left = self.peer(axis, 1), self.peer(axis, 3)
        a0 = self.push(low, low, right)
        b0 = self.push(high, high, left)
        return a0, b0, self.push(high, high, right), self.push(low, low, left)

    def forward(self, t, index, a, axis, copies):
        a0, b0, a1, b1 = copies
        a0.wait_recv()
        low = self.view(t, {**index, axis: self.pos(axis, 3), a: pl.ds(0, 2)})
        a2 = self.push(low, low, self.peer(axis, 1))
        b0.wait_recv()
        high = self.view(t, {**index, axis: self.pos(axis, 1), a: pl.ds(2, 2)})
        b2 = self.push(high, high, self.peer(axis, 3))
        wait_all((a1, b1))
        return a2, b2

    def to_core(self, t, index):
        v = self.view(t, index)
        self.core.append(self.push(v, v, self.other))

    def two(self):
        self.mine.wait()
        self.hop = []
        for t, (a, b, _) in enumerate(ORDERS):
            wait_all(self.one[t])
            self.hop.append(self.start(t, self.without(a), a, b))

    def two_forward(self):
        self.last = [self.forward(t, self.without(a), a, b, self.hop[t]) for t, (a, b, _) in enumerate(ORDERS)]

    def three(self, *thirds):
        for t in thirds:
            a, b, c = ORDERS[t]
            wait_all(self.last[t])
            self.hop[t] = self.start(t, self.without(a, b), a, c)
        for t in thirds:
            a, b, c = ORDERS[t]
            self.to_core(t, self.without(a, b))

    def three_forward(self, *thirds):
        for t in thirds:
            a, b, c = ORDERS[t]
            self.last[t] = self.forward(t, self.without(a, b), a, c, self.hop[t])
        for t in thirds:
            c = ORDERS[t][2]
            self.to_core(t, {c: self.pos(c, 1)})
            self.to_core(t, {c: self.pos(c, 3)})

    def three_end(self, *thirds):
        for t in thirds:
            c = ORDERS[t][2]
            wait_all(self.last[t])
            self.to_core(t, {c: self.pos(c, 2)})

    def end(self):
        wait_all(self.core)


class Small(Pushes):
    def __init__(self, R, place, ring):
        super().__init__(R.pool, place, ring, R.trs)
        self.R = R

    def halves(self):
        R = self.R
        for c in range(2):
            R.s0[c] = R.small[:, c * HALF : (c + 1) * HALF].astype(BF16)
        self.now = [self.push(R.s0.at[1 - self.p.c], R.sr, self.other)]

    def along_x(self):
        R = self.R
        wait_all(self.now)
        R.s1[...] = add_up(R.s0[self.p.c], R.sr[...])
        self.now = [self.push(R.s1, R.sx.at[k - 1], self.peer("x", k)) for k in RING4]

    def along_z(self):
        R = self.R
        wait_all(self.now)
        R.s2[...] = add_up(R.s1[...], *(R.sx[k] for k in range(3)))
        self.now = [self.push(R.s2, R.sz.at[k - 1], self.peer("z", k)) for k in RING4]

    def along_y(self):
        R = self.R
        wait_all(self.now)
        own = R.fs.at[self.p.c, self.ring.y]
        own[...] = add_up(R.s2[...], *(R.sz[k] for k in range(3)))
        self.now = [self.push(own, own, self.peer("y", k)) for k in RING4]

    def to_core(self):
        half = self.R.fs.at[self.p.c]
        wait_all(self.now)
        self.now = [self.push(half, half, self.other)]

    def end(self):
        wait_all(self.now)


IN = ("tok", "cot", "gain", "shift", "w_qkv", "qv_bias", "w_out", "out_bias", "w_up", "up_bias", "w_down", "down_bias")
IN = IN + ("router", "e_up", "e_up_bias", "e_down", "e_down_bias", "ids", "pri")


def outputs():
    return dict(
        result=((ROWS, D), F32),
        d_tok=((ROWS, D), F32),
        g_eub=((1, D), F32),
        g_edb=((1, D), F32),
        fs=((2, 4, 48, HALF), BF16),
        g_eup=((D, D), BF16),
        g_edown=((D, D), BF16),
        f13=((2, 2, 4, 4, 4, 48, HALF), BF16),
        f2=((2, 4, 4, 4, 96, HALF), BF16),
    )


def scratch():
    blk, att = (NY, ROWS, D), (NY, ROWS, HW)
    low, wide, sems = (lambda *sh: pltpu.VMEM(sh, BF16)), (lambda *sh: pltpu.VMEM(sh, F32)), pltpu.SemaphoreType.DMA
    n_slots = CAP * NDP
    return dict(
        n=[low(*blk) for _ in range(3)],
        q=[low(*att) for _ in range(2)],
        k=[low(*att) for _ in range(2)],
        v=[low(*att) for _ in range(2)],
        o=[wide(*att) for _ in range(2)],
        st=[wide(NY, ROWS, 128) for _ in range(2)],
        gb=[low(*blk) for _ in range(2)],
        go=low(*att),
        gq=low(*att),
        gk=low(*att),
        gv=low(*att),
        vm=low(HEADS_DEV, NY * ROWS, HW),
        qm=low(HEADS_DEV, NY * ROWS, HW),
        dq=wide(NY * ROWS, HW),
        stt=wide(8, NY * ROWS),
        u=wide(*blk),
        a=low(*blk),
        gu=low(*blk),
        moe=low(NY, 2 * n_slots, D),
        mpart=wide(NY, 2 * n_slots, D),
        msb=low(3, 2 * n_slots, D),
        mrb=low(3, 2 * n_slots, D),
        eb=low(NY, n_slots, D),
        egc=low(NY, n_slots, D),
        ds=low(EXPERTS, 8, D),
        dr=low(2, EXPERTS, 8, D),
        wqkv0g=low(4, 4, 2, 24, 3 * HW),
        wqkv1g=low(4, 4, 2, 24, 3 * HW),
        wupg=low(4, 4, 2, 24, D),
        wqkv0=low(24, 3 * HW),
        wqkv1=low(24, 3 * HW),
        wup=low(24, D),
        woutg=low(4, 2, 2, 24, D),
        wdowng=low(4, 2, 96, D),
        qvb=wide(4, HW),
        wqkv=low(2, 3, D, HW),
        wout=low(2, HW, D),
        up=low(D, D),
        down=low(D, D),
        eu=low(D, D),
        ed=low(D, D),
        geu=low(D, D),
        ged=low(D, D),
        own=sems((4,)),
        xs=wide(4, ROWS, D),
        gs=wide(ROWS, D),
        small=wide(48, D),
        g13=[low(2, 4, 4, 48, HALF) for _ in range(2)],
        g2=low(2, 4, 4, 96, HALF),
        sums=[sum_scratch(r, a) for r, a in ((48, 32), (96, 48), (48, 16))],
        s0=low(2, 48, HALF),
        sr=low(48, HALF),
        s1=low(48, HALF),
        sx=low(3, 48, HALF),
        s2=low(48, HALF),
        sz=low(3, 48, HALF),
        ssem=sems((2, 6)),
        rsem=sems((2, 6)),
        dssem=sems((2,)),
        drsem=sems((2,)),
        pss=sems((48,)),
        wrs=sems((29,)),
        bss=sems((2, 4)),
        trs=sems((11,)),
    )


def kernel(*refs):
    n_in, n_out = len(IN), len(outputs())
    R = types.SimpleNamespace(**dict(zip(IN + tuple(outputs()), refs)), **refs[n_in + n_out])
    R.pool = Pool(R.pss, 48)
    R.sb = R.msb.at[:, pl.ds(0, ROWS)]
    R.rb = R.mrb.at[:, pl.ds(0, ROWS)]
    R.part = R.mpart.at[:, pl.ds(0, ROWS)]
    ring, place = Ring(), Place()
    d = place.d
    barrier = pltpu.get_barrier_semaphore()
    near = [place.at(c=1 - place.c)] + [{"seq": lax.rem(ring.y + k, NY)} for k in RING4]
    near += [place.at(x=lax.rem(place.x + k, 4)) for k in RING4] + [place.at(z=lax.rem(place.z + k, 4)) for k in RING4]
    for to in near:
        pl.semaphore_signal(barrier, inc=1, device_id=to, device_id_type=MESH)
    R.small[...] = jnp.zeros((48, D), F32)
    fetched = [
        pltpu.make_async_copy(src, dst, R.own.at[i]) for i, (src, dst) in enumerate(((R.e_up, R.eu), (R.e_down, R.ed)))
    ]
    stored = [
        pltpu.make_async_copy(src, dst, R.own.at[2 + i])
        for i, (src, dst) in enumerate(((R.geu, R.g_eup), (R.ged, R.g_edown)))
    ]
    for c in fetched:
        c.start()
    w = Weights(R, place, ring)
    w.cut()
    pl.semaphore_wait(barrier, len(near))

    gain = lambda j: R.gain[j : j + 1]
    shift = lambda j: R.shift[j : j + 1]
    xs, gs = R.xs, R.gs
    xs[0] = R.tok[...].astype(F32)
    w.b_along_z(2)
    w.a_along_x(0)
    xs[1] = attn_forward(R, ring, 0, xs[0], gain(0), shift(0), w)
    xs[2] = feed_forward(R, ring, xs[1], gain(1), shift(1), w)
    w.sent()
    xs[3] = attn_forward(R, ring, 1, xs[2], gain(2), shift(2))
    for c in fetched:
        c.wait()
    gs[...] = mixture(R, ring, d, xs[3], gain(3), shift(3))
    for c in stored:
        c.start()

    a1 = Sum(R, place, ring, R.g13[1], R.f13.at[1], R.sums[0])
    ff = Sum(R, place, ring, R.g2, R.f2, R.sums[1])
    a0 = Sum(R, place, ring, R.g13[0], R.f13.at[0], R.sums[2])
    small = Small(R, place, ring)

    def steps(*fs):
        def run():
            for f in fs:
                f()

        return run

    part = functools.partial
    gs[...] = attn_backward(R, ring, 1, xs[2], gain(2), gs[...], 6, {BESIDE: a1.halves, END: a1.first_axis})
    gs[...] = feed_backward(
        R,
        ring,
        xs[1],
        gain(1),
        gs[...],
        8,
        {
            LATE: a1.second_axis,
            BEFORE: a1.own,
            BESIDE: steps(ff.halves, a1.two),
            END: steps(ff.first_axis, a1.two_forward),
        },
    )
    R.d_tok[...] = attn_backward(
        R,
        ring,
        0,
        xs[0],
        gain(0),
        gs[...],
        10,
        {
            BEFORE: steps(ff.second_axis, part(a1.three, 0, 1, 2)),
            MIDDLE: ff.own,
            AFTER: steps(ff.two, part(a1.three_forward, 0, 1, 2)),
            WEIGHTS: a0.halves,
            BESIDE: steps(ff.two_forward, a0.first_axis, part(a1.three_end, 0, 1, 2)),
            END: steps(a0.second_axis, part(ff.three, 0, 1, 2)),
        },
    )
    small.halves()
    a0.own()
    small.along_x()
    a0.two()
    small.along_z()
    a0.two_forward()
    small.along_y()
    a0.three(0, 1, 2)
    ff.three_forward(0, 1, 2)
    small.to_core()
    a0.three_forward(0, 1, 2)
    ff.three_end(0, 1, 2)
    a0.three_end(0, 1, 2)
    for c in stored:
        c.wait()
    for s in (a1, ff, a0, small, R.pool):
        s.end()


def layers(ins):
    vmem, hbm = pl.BlockSpec(memory_space=pltpu.VMEM), pl.BlockSpec(memory_space=pl.ANY)
    out = outputs()
    return dict(
        zip(
            out,
            pl.pallas_call(
                kernel,
                out_shape=[jax.ShapeDtypeStruct(*sh) for sh in out.values()],
                in_specs=[hbm if n in ("e_up", "e_down") else vmem for n in IN],
                out_specs=[vmem] * (len(out) - 4) + [hbm] * 4,
                scratch_shapes=[scratch()],
                compiler_params=pltpu.CompilerParams(
                    collective_id=0, has_side_effects=True, vmem_limit_bytes=62 * 2**20
                ),
                name="layers",
            )(*ins),
        )
    )


def spread(o):
    def body(*refs):
        f_qkv, f_out, f_up, f_down, geu, ged, res, tok, fs, edb, eub = refs[:11]
        qkv, out, up, down, geu_o, ged_o, res_o, tok_o = refs[11:19]
        gain, shift, outb, downb, upb, qvb, router, edb_o, eub_o = refs[19:]
        s = pl.program_id(0)

        @pl.when(s < 12)
        def _():
            qkv[0] = jnp.transpose(f_qkv[0, 0, :, 0].reshape(D, HALF).astype(F32))

        out[0] = f_out[0, 0, 0, 0].reshape(HW, HALF).astype(F32)
        for c in range(2):
            at = pl.ds(c * HALF, HALF)
            up[:, at] = f_up[c, 0, 0].reshape(HW, HALF).astype(F32)
            down[:, at] = f_down[c, 0, 0].reshape(HW, HALF).astype(F32)
        geu_o[...] = geu[...].astype(F32)
        ged_o[...] = ged[...].astype(F32)
        res_o[...] = res[...]
        tok_o[...] = tok[...]

        @pl.when(s == 0)
        def _():
            by_y = [jnp.concatenate([fs[0, y], fs[1, y]], axis=1).astype(F32) for y in range(NY)]
            total = by_y[0] + by_y[1] + by_y[2] + by_y[3]
            gain[...] = total[0:4]
            shift[...] = total[4:8]
            outb[...] = total[8:10]
            for j in range(6):
                downb[j : j + 1] = total[10:11, 128 * j : 128 * (j + 1)]
            router[...] = total[16:48]
            for y in range(NY):
                for j in range(6):
                    upb[6 * y + j : 6 * y + j + 1] = by_y[y][11:12, 128 * j : 128 * (j + 1)]
                for i in range(2):
                    for t in range(2):
                        row = by_y[y][12 + 2 * i + t : 13 + 2 * i + t, 0:HW]
                        qvb[i : i + 1, t * D + y * HW : t * D + (y + 1) * HW] = row
            own = edb[:, 0:HW]
            for y in range(1, NY):
                own = jnp.where(lax.axis_index("seq") == y, edb[:, y * HW : (y + 1) * HW], own)
            edb_o[...] = own
            eub_o[...] = eub[...]

    def qkv_at(s):
        j = jnp.minimum(s, 11)
        return lax.div(j, 6), lax.rem(j, 2), lax.div(lax.rem(j, 6), 2)

    def out_at(s):
        return lax.div(s, 8), lax.rem(lax.div(s, 4), 2), lax.rem(s, 4)

    def feed_at(s, z):
        y, j = lax.div(s, 4), lax.rem(s, 4)
        return 0, y, z + lax.div(j, 2), lax.rem(j, 2), 0, 0

    def qkv_in(s):
        i, c, t = qkv_at(s)
        return i, c, 0, t, 0, 0, 0

    def qkv_out(s):
        i, c, t = qkv_at(s)
        return i, c, t

    def out_in(s):
        i, c, y = out_at(s)
        return i, c, y, 3, 0, 0, 0

    def out_out(s):
        i, c, y = out_at(s)
        return i, y, c

    small = [(4, D), (4, D), (2, D), (6, 128), (24, 128), (2, 2 * D), (EXPERTS, D), (1, HW), (1, D)]
    whole = lambda sh: pl.BlockSpec(sh, lambda s: (0,) * len(sh))
    rows = lambda n, last: pl.BlockSpec((n, D), lambda s: (jnp.minimum(s, last), 0))
    passed = [rows(48, 15), rows(48, 15), rows(16, 8), rows(16, 8)]
    big = [(2, D, 3 * D), (2, D, D), (D, NY * D), (NY * D, D), (D, D), (D, D), (ROWS, D), (ROWS, D)]
    return pl.pallas_call(
        body,
        grid=(16,),
        in_specs=[
            pl.BlockSpec((1, 1, 4, 1, 4, 48, HALF), qkv_in),
            pl.BlockSpec((1, 1, 1, 1, 4, 48, HALF), out_in),
            pl.BlockSpec((2, 1, 1, 2, 96, HALF), lambda s: feed_at(s, 0)),
            pl.BlockSpec((2, 1, 1, 2, 96, HALF), lambda s: feed_at(s, 2)),
        ]
        + passed
        + [whole((2, 4, 48, HALF)), whole((1, D)), whole((1, D))],
        out_specs=[
            pl.BlockSpec((1, HALF, D), qkv_out),
            pl.BlockSpec((1, HW, HALF), out_out),
            pl.BlockSpec((HW, D), lambda s: (lax.rem(s, 4), lax.div(s, 4))),
            pl.BlockSpec((HW, D), lambda s: (s, 0)),
        ]
        + passed
        + [whole(sh) for sh in small],
        out_shape=[jax.ShapeDtypeStruct(sh, F32) for sh in big + small],
        compiler_params=pltpu.CompilerParams(vmem_limit_bytes=62 * 2**20),
        name="spread",
    )(o.f13, o.f13, o.f2, o.f2, o.g_eup, o.g_edown, o.result, o.d_tok, o.fs, o.g_edb, o.g_eub)


def local(
    tokens,
    cotangent,
    ln_gain,
    ln_shift,
    qkv_weight,
    qv_bias,
    out_weight,
    out_bias,
    up_weight,
    up_bias,
    down_weight,
    down_bias,
    router,
    expert_up,
    expert_up_bias,
    expert_down,
    expert_down_bias,
    expert_ids,
    priority,
):
    o = types.SimpleNamespace(
        **layers(
            (
                tokens[0],
                cotangent[0],
                ln_gain,
                ln_shift,
                qkv_weight,
                qv_bias,
                out_weight,
                out_bias,
                up_weight,
                up_bias.reshape(24, 128),
                down_weight,
                down_bias.reshape(6, 128),
                router.T,
                expert_up[0],
                expert_up_bias,
                expert_down[0],
                expert_down_bias,
                expert_ids[0].T,
                priority[0].T,
            )
        )
    )
    g_qkv, g_out, g_up, g_down, geu, ged, res, tok, *small = spread(o)
    gain, shift, outb, downb, upb, qvb, g_router, edb, eub = small
    return (
        res[None],
        tok[None],
        gain,
        shift,
        g_qkv,
        qvb,
        g_out,
        outb,
        g_up,
        upb.reshape(NY * D),
        g_down,
        downb.reshape(D),
        g_router.T,
        geu[None],
        eub,
        ged[None],
        edb,
    )


def solution(mesh):
    in_specs = (
        P("dp", "seq", None),
        P("dp", "seq", None),
        P(),
        P(),
        P(None, "dp", None),
        P(),
        P(None, "dp", None),
        P(),
        P("dp", None),
        P(),
        P("dp", None),
        P(),
        P(),
        P("dp", None, "seq"),
        P("dp", "seq"),
        P("dp", "seq", None),
        P("dp", None),
        P("dp", "seq", None),
        P("dp", "seq", None),
    )
    out_specs = (
        P("dp", "seq", None),
        P("dp", "seq", None),
        P(),
        P(),
        P(),
        P(),
        P(),
        P(),
        P(),
        P(),
        P(),
        P(),
        P(),
        P("dp", None, "seq"),
        P("dp", "seq"),
        P("dp", "seq", None),
        P("dp", "seq"),
    )
    return jax.shard_map(local, mesh=mesh, in_specs=in_specs, out_specs=out_specs, check_vma=False)
```
